128 devices in a mesh: grp: 2 (over x_lo), px: 8 (over x_hi, y), py: 8 (over z, core).
Axes of the slice: x: 4 (x_hi: 2, x_lo: 2; x = x_hi * 2 + x_lo), y: 4, z: 4, core: 2. Of those that a mesh axis runs over, the one named last changes fastest.
Arguments:
- multiplier: float32 [3, 32, 16, 256, 256], P(None, 'py', None, ('grp', 'px')), may hold values from -6 to 6
- auxiliary: float32 [3, 32, 16, 256, 256], P(None, 'py', None, ('grp', 'px')), may hold values from -6 to 6
- density_start: float32 [16, 256, 256], P(None, ('grp', 'px')), may hold values from 0.5 to 2
- density_end: float32 [16, 256, 256], P(None, ('grp', 'px')), may hold values from 0.5 to 2
Outputs:
- multiplier_next: float32 [3, 32, 16, 256, 256], P(None, 'py', None, ('grp', 'px'))
- auxiliary_next: float32 [3, 32, 16, 256, 256], P(None, 'py', None, ('grp', 'px'))
The draws below stay inside these ranges and needn't reach their ends.
All inputs are finite; a program needn't handle non-finite values.
Results may differ from the reference program's by a relative error of at most 0.0003.
Values sent between devices are 32-bit elements; how exact they have to be, the bound alone decides.
No kernel may reach another device: no remote copies, remote signals or barrier semaphores. Data moves between devices by JAX's collectives and lax.ppermute only.
A program may use at most 64 MiB of HBM per device.

```python
import math
import jax
import jax.numpy as jnp
from jax import lax

NX = 256
NY = 256
LEVELS = 32
BATCH = 16
NEWTON = 4


def wave_field(key):
    keys = jax.random.split(key, 4)
    problem = jnp.arange(BATCH, dtype=jnp.int32)
    low_shift = jax.random.randint(keys[0], (), 0, 9)
    high_shift = jax.random.randint(keys[1], (), 0, 13)
    low_wave = 12 + (problem * 9 // BATCH + low_shift) % 9
    high_wave = 28 + (problem * 13 // BATCH + high_shift) % 13
    phases = jax.random.uniform(keys[2], (2, BATCH, 1, 1), jnp.float32, -math.pi, math.pi)
    row_signs = jnp.where(jax.random.bernoulli(keys[3], 0.5, (2, BATCH, NX, 1)), 1.0, -1.0).astype(jnp.float32)
    column = jnp.arange(NY, dtype=jnp.int32)
    low_phase = (low_wave[:, None] * column[None, :] % NY).astype(jnp.float32) * (2.0 * math.pi / NY)
    high_phase = (high_wave[:, None] * column[None, :] % NY).astype(jnp.float32) * (2.0 * math.pi / NY)
    low_part = jnp.cos(low_phase[:, None, :] + phases[0]) * row_signs[0]
    high_part = jnp.cos(high_phase[:, None, :] + phases[1]) * row_signs[1]
    return 1.5 * (low_part + high_part)


def field_draw(key):
    base_key = jax.random.fold_in(key, 101)
    wave_key = jax.random.fold_in(key, 202)
    shape = (3, LEVELS, BATCH, NX, NY)
    base = jax.random.normal(base_key, shape, jnp.float32)
    wave = wave_field(wave_key)
    second = base[2] + wave[None]
    whole = jnp.concatenate([base[:2], second[None]], axis=0)
    return jnp.clip(whole, -6.0, 6.0).astype(jnp.float32)


def draw_multiplier(key, part):
    return field_draw(jax.random.fold_in(key, 11))


def draw_auxiliary(key, part):
    return field_draw(jax.random.fold_in(key, 23))


def block_scale(stream_key, extent, cuts, least, high):
    def one(position, parts):
        draws = jax.random.uniform(jax.random.fold_in(jax.random.fold_in(stream_key, 6), position), (parts,), jnp.float32, least / len(cuts), high / len(cuts))
        return jnp.repeat(jnp.exp(draws), extent[position] // parts).reshape((-1,) + (1,) * (len(extent) - position - 1))

    gain = one(*cuts[0])
    for cut in cuts[1:]:
        gain = gain * one(*cut)
    return gain


def setup_inputs(seed: int = 0) -> dict:
    key_of = jax.random.split(jax.random.key(seed), 5)
    return {
        "multiplier": draw_multiplier(jax.random.fold_in(key_of[4], 71), 0),
        "auxiliary": draw_auxiliary(jax.random.fold_in(key_of[4], 71), 0),
        "density_start": jnp.clip(jnp.exp(math.log(2.0) - 1.3862944 * jax.random.uniform(key_of[2], (BATCH, NX, NY), jnp.float32) ** block_scale(key_of[2], (BATCH, NX, NY), ((1, 16),), -0.2, 0.2)), 0.5, 2.0),
        "density_end": jnp.clip(jnp.exp(math.log(2.0) - 1.3862944 * jax.random.uniform(key_of[3], (BATCH, NX, NY), jnp.float32) ** block_scale(key_of[3], (BATCH, NX, NY), ((1, 16),), -0.2, 0.2)), 0.5, 2.0),
    }


PENALTY = 1.0
PRECISE = lax.Precision.HIGHEST

def cosine_table(levels):
    mode_index = lax.broadcasted_iota(jnp.int32, (levels, levels), 0)
    time_index = lax.broadcasted_iota(jnp.int32, (levels, levels), 1)
    phase_index = mode_index * (2 * time_index + 1) % (4 * levels)
    angles = phase_index.astype(jnp.float32) * (math.pi / (2 * levels))
    weights = jnp.where(mode_index == 0, math.sqrt(1.0 / levels), math.sqrt(2.0 / levels))
    return weights * jnp.cos(angles)

def eigenvalues(levels, row_start, row_total, row_count, col_count):
    time_modes = lax.broadcasted_iota(jnp.int32, (levels, 1, 1, 1), 0).astype(jnp.float32)
    row_modes = (row_start + lax.broadcasted_iota(jnp.int32, (1, 1, row_total, 1), 2)).astype(jnp.float32)
    col_modes = lax.broadcasted_iota(jnp.int32, (1, 1, 1, col_count), 3).astype(jnp.float32)
    time_part = 4.0 * jnp.sin(time_modes * (math.pi / (2 * levels))) ** 2
    row_part = 4.0 * jnp.sin(row_modes * (math.pi / row_count)) ** 2
    col_part = 4.0 * jnp.sin(col_modes * (math.pi / col_count)) ** 2
    return time_part + row_part + col_part

def project(target):
    time_part = target[0]
    space_first = target[1]
    space_second = target[2]
    kinetic = 0.5 * (space_first * space_first + space_second * space_second)
    offset_one = 1.0 + time_part
    scaling = jnp.maximum(offset_one, 1.0) + jnp.cbrt(kinetic)
    for newton_step in range(NEWTON):
        residue = scaling * scaling * (scaling - offset_one) - kinetic
        derivative = scaling * (3.0 * scaling - 2.0 * offset_one)
        scaling = jnp.maximum(scaling - residue / derivative, 1.0)
    feasible = time_part + kinetic <= 0.0
    return jnp.stack([jnp.where(feasible, time_part, time_part - (scaling - 1.0)), jnp.where(feasible, space_first, space_first / scaling), jnp.where(feasible, space_second, space_second / scaling)])

def reference(multiplier, auxiliary, density_start, density_end):
    offset_field = auxiliary - multiplier / PENALTY
    level_index = lax.broadcasted_iota(jnp.int32, (LEVELS, 1, 1, 1), 0)
    offset_time = jnp.where(level_index == LEVELS - 1, 0.0, offset_field[0])
    earlier = jnp.concatenate([jnp.zeros_like(offset_time[:1]), offset_time[:-1]], axis=0)
    boundary = jnp.where(level_index == 0, -density_start / PENALTY, 0.0) + jnp.where(level_index == LEVELS - 1, density_end / PENALTY, 0.0)
    offset_first = offset_field[1]
    offset_second = offset_field[2]
    source = earlier - offset_time + jnp.roll(offset_first, 1, axis=2) - offset_first + jnp.roll(offset_second, 1, axis=3) - offset_second + boundary
    cosine = cosine_table(LEVELS)
    transformed = jnp.einsum('kt,tbxy->kbxy', cosine, source, precision=PRECISE)
    spectrum = jnp.fft.fft2(transformed, axes=(2, 3))
    eigen = eigenvalues(LEVELS, 0, NX, NX, NY)
    positive = eigen > 0.0
    inverse = jnp.where(positive, 1.0 / jnp.where(positive, eigen, 1.0), 0.0)
    potential_modes = jnp.real(jnp.fft.ifft2(spectrum * inverse, axes=(2, 3))).astype(source.dtype)
    potential = jnp.einsum('kt,kbxy->tbxy', cosine, potential_modes, precision=PRECISE)
    time_rate = jnp.concatenate([potential[1:] - potential[:-1], jnp.zeros_like(potential[:1])], axis=0)
    gradient = jnp.stack([time_rate, jnp.roll(potential, -1, axis=2) - potential, jnp.roll(potential, -1, axis=3) - potential])
    target = gradient + multiplier / PENALTY
    auxiliary_next = project(target)
    multiplier_next = multiplier + PENALTY * (gradient - auxiliary_next)
    return (multiplier_next, auxiliary_next)
```

```python
import functools
import math

import jax
import jax.numpy as jnp
import numpy as np
from jax import lax
from jax.experimental import pallas as pl
from jax.experimental.pallas import tpu as pltpu
from jax.sharding import PartitionSpec as P

NEWTON = 4
ROWS = ("grp", "px")
EVERY = ("grp", "px", "py")
VMEM_BYTES = 48 * 1024 * 1024


def moved(value, axis, steps, wrap):
    count = lax.axis_size(axis)
    pairs = [(i, (i + steps) % count) for i in range(count) if wrap or 0 <= i + steps < count]
    return lax.ppermute(value, axis, pairs)


def hartley_table(length):
    index = np.arange(length)
    angles = (index[:, None] * index[None, :] % length) * (2.0 * np.pi / length)
    return ((np.cos(angles) + np.sin(angles)) / np.sqrt(length)).astype(np.float32)


def halves(value):
    high = value.astype(jnp.bfloat16)
    return high, (value - high.astype(jnp.float32)).astype(jnp.bfloat16)


def table_halves(length):
    table = hartley_table(length)
    high = table.astype(jnp.bfloat16)
    return np.stack([high, (table - high.astype(np.float32)).astype(jnp.bfloat16)])


def elimination_table(levels, row_count, col_count, blocks):
    col = 4.0 * np.sin(np.pi * np.arange(col_count) / col_count) ** 2
    row = 4.0 * np.sin(np.pi * np.arange(row_count) / row_count) ** 2
    eigen = col[:, None] + row[None, :]
    factors = [1.0 / (1.0 + eigen)]
    for _ in range(levels // 2 - 1):
        factors.append(1.0 / (2.0 + eigen - factors[-1]))
    gap = 1.0 - factors[-1] ** 2
    middle = np.where(eigen > 0.0, 1.0 / np.where(eigen > 0.0, gap, 1.0), 0.0)
    table = np.stack(factors + [middle]).astype(np.float32)
    table = table.reshape(levels // 2 + 1, blocks, col_count // blocks, row_count)
    return np.ascontiguousarray(table.transpose(1, 0, 2, 3))


def dot3(left, right, dims):
    (lh, ll), (rh, rl) = left, right
    one = functools.partial(
        lax.dot_general, dimension_numbers=(dims, ((), ())), preferred_element_type=jnp.float32
    )
    return one(lh, rh) + (one(lh, rl) + one(ll, rh))


def exchange_pieces(blocks, width):
    count = len(blocks)
    lanes = count * width
    group = lax.broadcasted_iota(jnp.int32, blocks[0].shape, 1) // width
    step = 1
    while step < count:
        upper = (group // step) % 2 == 1
        fresh = list(blocks)
        for j in range(count):
            if (j // step) % 2 == 0:
                low, high = blocks[j], blocks[j + step]
                fresh[j] = jnp.where(upper, pltpu.roll(high, step * width, 1), low)
                fresh[j + step] = jnp.where(upper, high, pltpu.roll(low, lanes - step * width, 1))
        blocks = fresh
        step *= 2
    return blocks


def source_kernel(
    levels, mult_ref, aux_ref, start_ref, end_ref, before_ref, rim_ref, hart_ref, out_ref
):
    here, pair, rows, cols = mult_ref.shape[1:]
    first = lax.axis_index("py") * here
    starts = jnp.where(first == 0, 1.0, 0.0)
    ends = jnp.where(first + here == levels, 1.0, 0.0)
    last_row = lax.broadcasted_iota(jnp.int32, (rows, cols), 0) == 0
    blocks = []
    earlier = [before_ref[b] for b in range(pair)]
    for t in range(here):
        for b in range(pair):
            time = aux_ref[0, t, b] - mult_ref[0, t, b]
            if t == here - 1:
                time = time * (1.0 - ends)
            along = aux_ref[1, t, b] - mult_ref[1, t, b]
            second = aux_ref[2, t, b] - mult_ref[2, t, b]
            beside = jnp.where(last_row, rim_ref[t, b], pltpu.roll(along, 1, 0))
            total = (earlier[b] - time) + (beside - along) + (pltpu.roll(second, 1, 1) - second)
            if t == 0:
                total = total - start_ref[b] * starts
            if t == here - 1:
                total = total + end_ref[b] * ends
            earlier[b] = time
            blocks.append(total)
    field = halves(jnp.concatenate(blocks, axis=0))
    modes = dot3((hart_ref[0], hart_ref[1]), field, ((1,), (1,)))
    out_ref[...] = modes.reshape(out_ref.shape)


def solve_kernel(in_ref, hart_ref, table_ref, out_ref, field_ref, factor_ref, sem):
    row_blocks, time_blocks, width, lanes = in_ref.shape
    pieces = lanes // width
    levels, pair, _, cols = field_ref.shape
    here = levels // time_blocks
    half = levels // 2
    mine = lax.axis_index("grp") * lax.axis_size("px") + lax.axis_index("px")
    fetch = pltpu.make_async_copy(table_ref.at[mine], factor_ref, sem)
    fetch.start()
    hart = (hart_ref[0], hart_ref[1])

    def forward(i, carry):
        groups = [
            exchange_pieces([in_ref[g * pieces + j, i] for j in range(pieces)], width)
            for g in range(row_blocks // pieces)
        ]
        field = jnp.concatenate(
            [jnp.concatenate([group[j] for group in groups], axis=1) for j in range(pieces)], axis=0
        )
        modes = dot3(halves(field), hart, ((1,), (0,)))
        field_ref[pl.ds(i * here, here)] = modes.reshape(here, pair, width, cols)
        return carry

    lax.fori_loop(0, time_blocks, forward, 0)
    fetch.wait()

    corner = (8, 128)
    zero = (
        (lax.broadcasted_iota(jnp.int32, corner, 0) == 0)
        & (lax.broadcasted_iota(jnp.int32, corner, 1) == 0)
        & (mine == 0)
    )

    def remove_mean():
        for b in range(pair):
            sums = field_ref[0, b, :8, :128]
            for t in range(1, levels):
                sums = sums + field_ref[t, b, :8, :128]
            mean = jnp.where(zero, sums * (1.0 / levels), 0.0)
            for t in range(levels):
                field_ref[t, b, :8, :128] = field_ref[t, b, :8, :128] - mean

    @pl.when(mine == 0)
    def _():
        remove_mean()

    left = jnp.zeros(field_ref.shape[1:], jnp.float32)
    right = left
    for t in range(half):
        factor = factor_ref[t][None]
        left = (field_ref[t] + left) * factor
        right = (field_ref[levels - 1 - t] + right) * factor
        if t < half - 1:
            field_ref[t] = left
            field_ref[levels - 1 - t] = right
    first = (left + factor * right) * factor_ref[half][None]
    right = right + factor * first
    left = first
    field_ref[half - 1] = left
    field_ref[half] = right
    for t in range(half - 2, -1, -1):
        factor = factor_ref[t][None]
        left = field_ref[t] + factor * left
        right = field_ref[levels - 1 - t] + factor * right
        field_ref[t] = left
        field_ref[levels - 1 - t] = right

    @pl.when(mine == 0)
    def _():
        remove_mean()

    def backward(i, carry):
        field = field_ref[pl.ds(i * here, here)].reshape(here * pair * width, cols)
        modes = dot3(hart, halves(field), ((1,), (1,)))
        out_ref[:, i] = modes.reshape(row_blocks, width, lanes)
        return carry

    lax.fori_loop(0, time_blocks, backward, 0)


def potential_kernel(in_ref, hart_ref, out_ref):
    col_blocks, _, width, lanes = in_ref.shape
    pieces = lanes // width
    groups = [
        exchange_pieces([in_ref[g * pieces + j, 0] for j in range(pieces)], width)
        for g in range(col_blocks // pieces)
    ]
    field = jnp.concatenate(
        [jnp.concatenate([group[j] for group in groups], axis=1) for j in range(pieces)], axis=0
    )
    values = dot3(halves(field), (hart_ref[0], hart_ref[1]), ((1,), (0,)))
    out_ref[...] = values.reshape(out_ref.shape)


def step_kernel(levels, mult_ref, phi_ref, later_ref, below_ref, mult_out, aux_out):
    here, pair, rows, cols = phi_ref.shape
    first = lax.axis_index("py") * here
    inner = jnp.where(first + here == levels, 0.0, 1.0)
    last_row = lax.broadcasted_iota(jnp.int32, (rows, cols), 0) == rows - 1
    for t in range(here):
        for b in range(pair):
            phi = phi_ref[t, b]
            if t < here - 1:
                time_rate = phi_ref[t + 1, b] - phi
            else:
                time_rate = (later_ref[b] - phi) * inner
            below = jnp.where(last_row, below_ref[t, b], pltpu.roll(phi, rows - 1, 0))
            gradient = (time_rate, below - phi, pltpu.roll(phi, cols - 1, 1) - phi)
            mult = [mult_ref[c, t, b] for c in range(3)]
            time_part, one, two = (g + m for g, m in zip(gradient, mult))
            kinetic = 0.5 * (one * one + two * two)
            center = 1.0 + time_part
            scaling = jnp.maximum(center, 1.0) + jnp.exp(jnp.log(kinetic) * (1.0 / 3.0))
            for _ in range(NEWTON):
                residue = scaling * scaling * (scaling - center) - kinetic
                derivative = scaling * (3.0 * scaling - 2.0 * center)
                scaling = jnp.maximum(scaling - residue / derivative, 1.0)
            feasible = time_part + kinetic <= 0.0
            shrink = jnp.where(feasible, 1.0, 1.0 / scaling)
            fresh = (
                jnp.where(feasible, time_part, time_part - (scaling - 1.0)),
                one * shrink,
                two * shrink,
            )
            for c in range(3):
                aux_out[c, t, b] = fresh[c]
                mult_out[c, t, b] = mult[c] + (gradient[c] - fresh[c])


def params():
    return pltpu.CompilerParams(vmem_limit_bytes=VMEM_BYTES)


def local(multiplier, auxiliary, density_start, density_end):
    _, here, batch, rows, cols = multiplier.shape
    time_blocks = lax.axis_size("py")
    row_blocks = lax.axis_size("grp") * lax.axis_size("px")
    levels = here * time_blocks
    row_count = rows * row_blocks
    pair = batch // time_blocks
    width = cols // row_blocks
    lanes = here * pair * rows
    hart_cols = table_halves(cols)
    hart_rows = table_halves(row_count)
    factors = elimination_table(levels, row_count, cols, row_blocks)

    before = moved(auxiliary[0, here - 1] - multiplier[0, here - 1], "py", 1, False)
    rim = moved(
        auxiliary[1, :, :, rows - 1 :] - multiplier[1, :, :, rows - 1 :], ROWS, 1, True
    )
    five = pl.BlockSpec((3, here, pair, rows, cols), lambda p: (0, 0, p, 0, 0))
    plane = pl.BlockSpec((pair, rows, cols), lambda p: (p, 0, 0))
    edge = pl.BlockSpec((here, pair, 1, cols), lambda p: (0, p, 0, 0))
    table = pl.BlockSpec((2, cols, cols), lambda p: (0, 0, 0))
    chunks = pl.BlockSpec((row_blocks, 1, width, lanes), lambda p: (0, p, 0, 0))
    chunked = jax.ShapeDtypeStruct((row_blocks, time_blocks, width, lanes), jnp.float32)
    modes = pl.pallas_call(
        functools.partial(source_kernel, levels),
        grid=(time_blocks,),
        in_specs=[five, five, plane, plane, plane, edge, table],
        out_specs=chunks,
        out_shape=chunked,
        compiler_params=params(),
        name="source",
    )(multiplier, auxiliary, density_start, density_end, before, rim, hart_cols)

    def spread(value):
        flat = value.reshape((row_blocks * time_blocks,) + value.shape[2:])
        return lax.all_to_all(flat, EVERY, 0, 0, tiled=True).reshape(value.shape)

    solved = pl.pallas_call(
        solve_kernel,
        in_specs=[
            pl.BlockSpec(memory_space=pltpu.VMEM),
            pl.BlockSpec(memory_space=pltpu.VMEM),
            pl.BlockSpec(memory_space=pl.ANY),
        ],
        out_specs=pl.BlockSpec(memory_space=pltpu.VMEM),
        out_shape=jax.ShapeDtypeStruct((row_blocks, time_blocks, rows, here * pair * width), jnp.float32),
        scratch_shapes=[
            pltpu.VMEM((levels, pair, width, row_count), jnp.float32),
            pltpu.VMEM(factors.shape[1:], jnp.float32),
            pltpu.SemaphoreType.DMA,
        ],
        compiler_params=params(),
        name="solve",
    )(spread(modes), hart_rows, factors)

    phi_block = pl.BlockSpec((here, pair, rows, cols), lambda p: (0, p, 0, 0))
    back = spread(solved)
    potential = pl.pallas_call(
        potential_kernel,
        grid=(time_blocks,),
        in_specs=[
            pl.BlockSpec((row_blocks, 1, rows, here * pair * width), lambda p: (0, p, 0, 0)),
            table,
        ],
        out_specs=phi_block,
        out_shape=jax.ShapeDtypeStruct((here, batch, rows, cols), jnp.float32),
        compiler_params=params(),
        name="potential",
    )(back, hart_cols)
    later = moved(potential[0], "py", -1, False)
    below = moved(potential[:, :, :1], ROWS, -1, True)
    result = jax.ShapeDtypeStruct(multiplier.shape, jnp.float32)
    mult_next, aux_next = pl.pallas_call(
        functools.partial(step_kernel, levels),
        grid=(time_blocks,),
        in_specs=[five, phi_block, plane, edge],
        out_specs=[five, five],
        out_shape=[result, result],
        compiler_params=params(),
        name="step",
    )(multiplier, potential, later, below)
    return mult_next, aux_next


def solution(mesh):
    field = P(None, "py", None, ROWS, None)
    density = P(None, ROWS, None)
    return jax.shard_map(
        local,
        mesh=mesh,
        in_specs=(field, field, density, density),
        out_specs=(field, field),
        check_vma=False,
    )
```

```python
import functools

import jax
import jax.numpy as jnp
import numpy as np
from jax import lax
from jax.experimental import pallas as pl
from jax.experimental.pallas import tpu as pltpu
from jax.sharding import PartitionSpec as P

NEWTON = 4
ROWS = ("grp", "px")
EVERY = ("grp", "px", "py")
GROUP = 2
VMEM_BYTES = 48 * 1024 * 1024
DIRECT = ((1,), (0,))
CROSS = ((1,), (1,))


def table_parts(table, count):
    rest = np.asarray(table, np.float32)
    parts = []
    for _ in range(count):
        parts.append(rest.astype(jnp.bfloat16))
        rest = rest - parts[-1].astype(np.float32)
    return np.stack(parts)


def parts_of(value, count):
    parts = [value.astype(jnp.bfloat16)]
    for _ in range(count - 1):
        value = value - parts[-1].astype(jnp.float32)
        parts.append(value.astype(jnp.bfloat16))
    return parts


def product(left, right, dims):
    total = None
    count = len(left)
    for order in range(count - 1, -1, -1):
        for i in range(order + 1):
            term = lax.dot_general(
                left[i], right[order - i], (dims, ((), ())), preferred_element_type=jnp.float32
            )
            total = term if total is None else total + term
    return total


def table_list(ref, *index):
    return [ref[index + (i,)] for i in range(ref.shape[len(index)])]


def squared_sines(length, period):
    return 4.0 * np.sin(np.pi * np.arange(length) / period) ** 2


def hartley_table(length):
    index = np.arange(length)
    angles = (index[:, None] * index[None, :] % length) * (2.0 * np.pi / length)
    return (np.cos(angles) + np.sin(angles)) / np.sqrt(length)


def elimination_table(levels, row_count, col_count, blocks):
    eigen = squared_sines(col_count, col_count)[:, None] + squared_sines(row_count, row_count)
    factors = [1.0 / (1.0 + eigen)]
    for _ in range(levels // 2 - 1):
        factors.append(1.0 / (2.0 + eigen - factors[-1]))
    gap = 1.0 - factors[-1] ** 2
    middle = np.where(eigen > 0.0, 1.0 / np.where(eigen > 0.0, gap, 1.0), 0.0)
    table = np.stack(factors + [middle]).astype(np.float32)
    table = table.reshape(levels // 2 + 1, blocks, col_count // blocks, row_count)
    return np.ascontiguousarray(table.transpose(1, 0, 2, 3))


def slots(here, rows, b, kind, index):
    if kind == "level":
        return b * rows + index
    if kind == "later":
        return (2 + b) * rows + index
    base = 4 * rows + b * (rows // 2)
    return base + (index - 1 if kind == "row" else here - 1 + index)


def interior_tables(here, rows, cols, last):
    pair = 2
    lanes = here * pair * rows
    inner = here - 1
    chain = 2.0 * np.eye(inner) - np.eye(inner, k=1) - np.eye(inner, k=-1)
    if last:
        chain[-1, -1] = 1.0
    time_values, time_basis = np.linalg.eigh(chain)
    row_index = np.arange(1, rows)
    row_basis = np.sqrt(2.0 / rows) * np.sin(np.pi * np.outer(row_index, row_index) / rows)
    row_values = squared_sines(rows, 2 * rows)
    col_values = squared_sines(cols, cols)
    basis = np.zeros((here, pair, rows, here, pair, rows))
    inverse = np.zeros((cols, here, pair, rows))
    linked = np.zeros((here, pair, rows, lanes))
    for b in range(pair):
        for k in range(1, here):
            for t in range(1, here):
                basis[t, b, 1:, k, b, 1:] = time_basis[t - 1, k - 1] * row_basis
            inverse[:, k, b, 1:] = 1.0 / (
                col_values[:, None] + time_values[k - 1] + row_values[None, 1:]
            )
        for x in range(1, rows):
            linked[1, b, x, slots(here, rows, b, "level", x)] = 1.0
            if not last:
                linked[here - 1, b, x, slots(here, rows, b, "later", x)] = 1.0
        for t in range(1, here):
            linked[t, b, 1, slots(here, rows, b, "row", t)] = 1.0
            linked[t, b, rows - 1, slots(here, rows, b, "next", t)] = 1.0
    basis = basis.reshape(lanes, lanes)
    linked = linked.reshape(lanes, lanes)
    inverse = inverse.reshape(cols, lanes)
    to_edges = basis.T @ linked
    from_edges = to_edges.T.copy()
    for b in range(pair):
        ones = np.zeros((here, pair, rows))
        ones[1:, b, 1:] = 1.0
        from_edges[slots(here, rows, b, "next", here)] = -(ones.reshape(-1) @ basis)
    return basis, inverse, to_edges, from_edges


def constant_source(here, rows, time_blocks, row_blocks, tables):
    levels, row_count = here * time_blocks, rows * row_blocks
    field = np.zeros((levels + 1, row_count))
    ones = np.zeros((here, 2, rows))
    ones[1:, 0, 1:] = 1.0
    for i in range(time_blocks):
        basis, inverse, to_edges, _ = tables[1 if i == time_blocks - 1 else 0]
        edge = ((ones.reshape(-1) @ basis) * inverse[0]) @ to_edges
        for j in range(row_blocks):
            t0, x0 = i * here, j * rows
            for x in range(rows):
                field[t0, x0 + x] += 1.0 + edge[slots(here, rows, 0, "level", x)]
                field[t0 + here, x0 + x] += edge[slots(here, rows, 0, "later", x)]
            for t in range(here):
                after = (x0 + rows) % row_count
                field[t0 + t, after] += edge[slots(here, rows, 0, "next", t)]
                if t > 0:
                    field[t0 + t, x0] += 1.0 + edge[slots(here, rows, 0, "row", t)]
    return field[:levels] @ hartley_table(row_count)


def exchange_pieces(blocks, width):
    count = len(blocks)
    lanes = count * width
    group = lax.broadcasted_iota(jnp.int32, blocks[0].shape, 1) // width
    step = 1
    while step < count:
        upper = (group // step) % 2 == 1
        fresh = list(blocks)
        for j in range(count):
            if (j // step) % 2 == 0:
                low, high = blocks[j], blocks[j + step]
                fresh[j] = jnp.where(upper, pltpu.roll(high, step * width, 1), low)
                fresh[j + step] = jnp.where(upper, high, pltpu.roll(low, lanes - step * width, 1))
        blocks = fresh
        step *= 2
    return blocks


def source_kernel(
    levels,
    pair,
    mult_ref,
    aux_ref,
    start_hbm,
    end_hbm,
    hart_hbm,
    basis_hbm,
    inverse_hbm,
    edges_hbm,
    out_ref,
    inner_ref,
    density_ref,
    hart_ref,
    basis_ref,
    inverse_ref,
    edges_ref,
    sems,
):
    _, here, batch, rows, cols = mult_ref.shape
    first = lax.axis_index("py") * here
    last = (first + here == levels).astype(jnp.int32)
    step = pl.program_id(0)

    @pl.when(step == 0)
    def _():
        copies = [
            pltpu.make_async_copy(hart_hbm, hart_ref, sems.at[0]),
            pltpu.make_async_copy(basis_hbm.at[last], basis_ref, sems.at[1]),
            pltpu.make_async_copy(inverse_hbm.at[last], inverse_ref, sems.at[2]),
            pltpu.make_async_copy(edges_hbm.at[last], edges_ref, sems.at[3]),
            pltpu.make_async_copy(start_hbm, density_ref.at[0], sems.at[4]),
            pltpu.make_async_copy(end_hbm, density_ref.at[1], sems.at[5]),
        ]
        for copy in copies:
            copy.start()
        for copy in copies:
            copy.wait()

    for q in range(batch // pair):
        source_part(
            first, last, q, step * batch + q * pair, pair, mult_ref, aux_ref, density_ref,
            hart_ref, basis_ref, inverse_ref, edges_ref, out_ref, inner_ref,
        )


def source_part(
    first, last, q, problem, pair, mult_ref, aux_ref, density_ref,
    hart_ref, basis_ref, inverse_ref, edges_ref, out_ref, inner_ref,
):
    here, _, rows, cols = mult_ref.shape[1:]
    lanes = here * pair * rows
    starts = jnp.where(first == 0, 1.0, 0.0)
    ends = last.astype(jnp.float32)
    row_index = lax.broadcasted_iota(jnp.int32, (rows, cols), 0)
    first_row = row_index == 0
    blocks = []
    earlier = [0.0] * pair
    rims = jnp.zeros((rows, cols), jnp.float32)
    for t in range(here):
        for b in range(pair):
            time = aux_ref[0, t, q * pair + b] - mult_ref[0, t, q * pair + b]
            if t == here - 1:
                time = time * (1.0 - ends)
            along = aux_ref[1, t, q * pair + b] - mult_ref[1, t, q * pair + b]
            second = aux_ref[2, t, q * pair + b] - mult_ref[2, t, q * pair + b]
            beside = jnp.where(first_row, 0.0, pltpu.roll(along, 1, 0))
            total = (earlier[b] - time) + (beside - along) + (pltpu.roll(second, 1, 1) - second)
            if t == 0:
                total = total - density_ref[0, problem + b] * starts
            if t == here - 1:
                total = total + density_ref[1, problem + b] * ends
            earlier[b] = time
            blocks.append(total)
            base = b * (rows // 2)
            if t > 0:
                rims = jnp.where(row_index == base + t - 1, total[:1], rims)
            rims = jnp.where(row_index == base + here - 1 + t, along[rows - 1 :], rims)
    spare = jnp.zeros((lanes - (2 * pair + 1) * rows, cols), jnp.float32)
    nodes = jnp.concatenate(blocks + blocks[:pair] + earlier + [rims, spare], axis=0)
    modes = product(table_list(hart_ref), parts_of(nodes, 2), CROSS)
    inner = product(parts_of(modes[:, :lanes], 2), table_list(basis_ref), DIRECT)
    inner_ref[q] = inner
    gone = parts_of(inner * inverse_ref[...], 2)
    edges = modes[:, lanes:] + product(gone, table_list(edges_ref), DIRECT)
    out_ref[:, q] = edges.reshape(out_ref.shape[0], out_ref.shape[2], lanes)


def solve_kernel(in_ref, hart_ref, ones_ref, table_ref, out_ref, field_ref, mean_ref, factor_ref, sem):
    row_blocks, time_blocks, width, lanes = in_ref.shape
    pieces = lanes // width
    levels, pair, _, cols = field_ref.shape
    here = levels // time_blocks
    rows = cols // row_blocks
    half = levels // 2
    mine = lax.axis_index("grp") * lax.axis_size("px") + lax.axis_index("px")
    fetch = pltpu.make_async_copy(table_ref.at[mine], factor_ref, sem)
    fetch.start()
    hart = table_list(hart_ref)
    corner = lax.broadcasted_iota(jnp.int32, (width, cols), 1) % rows == 0

    def shift(value, steps):
        return pltpu.roll(value, steps % cols, 1)

    def offset(b, kind, t):
        return slots(here, rows, b, kind, t) - 4 * rows

    def forward(i, carry):
        groups = [
            exchange_pieces([in_ref[g * pieces + j, i] for j in range(pieces)], width)
            for g in range(row_blocks // pieces)
        ]
        kinds = [jnp.concatenate([group[k] for group in groups], axis=1) for k in range(5)]
        rims = kinds[4]
        field = []
        for t in range(here):
            for b in range(pair):
                value = shift(rims, rows - offset(b, "next", t))
                if t > 0:
                    value = value + shift(rims, -offset(b, "row", t))
                value = jnp.where(corner, value, 0.0)
                if t == 0:
                    value = value + kinds[b] + carry[b]
                field.append(value)
        field = jnp.concatenate(field, axis=0)
        modes = product(parts_of(field, 2), hart[:2], DIRECT)
        field_ref[pl.ds(i * here, here)] = modes.reshape(here, pair, width, cols)
        return tuple(kinds[2 : 2 + pair])

    blank = jnp.zeros((width, cols), jnp.float32)
    lax.fori_loop(0, time_blocks, forward, (blank,) * pair, unroll=True)
    fetch.wait()

    mean_ref[...] = jnp.zeros(mean_ref.shape, jnp.float32)

    @pl.when(mine == 0)
    def _():
        tile = (8, 128)
        zero = (lax.broadcasted_iota(jnp.int32, tile, 0) == 0) & (
            lax.broadcasted_iota(jnp.int32, tile, 1) == 0
        )
        scale = float(np.sqrt(cols)) / (levels * cols)
        for b in range(pair):
            sums = field_ref[0, b, :8, :128]
            for t in range(1, levels):
                sums = sums + field_ref[t, b, :8, :128]
            mean = jnp.sum(jnp.where(zero, sums * scale, 0.0), axis=1, keepdims=True)
            mean_ref[b, :8] = jnp.broadcast_to(mean, (8, cols))
            for t in range(levels):
                field_ref[t, b, :8] = field_ref[t, b, :8] - mean * ones_ref[t : t + 1]

    left = jnp.zeros(field_ref.shape[1:], jnp.float32)
    right = left
    for t in range(half):
        factor = factor_ref[t][None]
        left = (field_ref[t] + left) * factor
        right = (field_ref[levels - 1 - t] + right) * factor
        if t < half - 1:
            field_ref[t] = left
            field_ref[levels - 1 - t] = right
    first = (left + factor * right) * factor_ref[half][None]
    right = right + factor * first
    left = first
    field_ref[half - 1] = left
    field_ref[half] = right
    for t in range(half - 2, -1, -1):
        factor = factor_ref[t][None]
        left = field_ref[t] + factor * left
        right = field_ref[levels - 1 - t] + factor * right
        field_ref[t] = left
        field_ref[levels - 1 - t] = right

    def backward(step, carry):
        i = time_blocks - 1 - step
        field = field_ref[pl.ds(i * here, here)].reshape(here * pair * width, cols)
        values = product(parts_of(field, 3), hart, DIRECT)
        part = [
            [values[(t * pair + b) * width : (t * pair + b + 1) * width] for b in range(pair)]
            for t in range(here)
        ]
        lane = lax.broadcasted_iota(jnp.int32, (width, cols), 1) % rows
        rims = jnp.zeros((width, cols), jnp.float32)
        for b in range(pair):
            for t in range(here):
                at = offset(b, "next", t)
                rims = jnp.where(lane == at, shift(part[t][b], at - rows), rims)
                if t > 0:
                    at = offset(b, "row", t)
                    rims = jnp.where(lane == at, shift(part[t][b], at), rims)
            rims = jnp.where(lane == offset(b, "next", here), mean_ref[b], rims)
        kinds = part[0] + list(carry) + [rims]
        for g in range(row_blocks // pieces):
            cut = [kind[:, g * lanes : (g + 1) * lanes] for kind in kinds]
            cut += [jnp.zeros((width, lanes), jnp.float32)] * (pieces - len(cut))
            for j, value in enumerate(exchange_pieces(cut, width)):
                out_ref[g * pieces + j, i] = value
        return tuple(part[0])

    lax.fori_loop(0, time_blocks, backward, (blank,) * pair, unroll=True)


def step_kernel(
    levels,
    pair,
    mult_ref,
    edge_ref,
    inner_ref,
    hart_ref,
    links_ref,
    inverse_ref,
    basis_ref,
    mult_out,
    aux_out,
):
    for q in range(mult_ref.shape[2] // pair):
        step_part(
            levels, q, pair, mult_ref, edge_ref, inner_ref, hart_ref, links_ref, inverse_ref,
            basis_ref, mult_out, aux_out,
        )


def step_part(
    levels, q, pair, mult_ref, edge_ref, inner_ref, hart_ref, links_ref, inverse_ref, basis_ref,
    mult_out, aux_out,
):
    here, _, rows, cols = mult_ref.shape[1:]
    lanes = here * pair * rows
    first = lax.axis_index("py") * here
    last = (first + here == levels).astype(jnp.int32)
    inside = 1.0 - last.astype(jnp.float32)
    row_index = lax.broadcasted_iota(jnp.int32, (rows, cols), 0)
    edges = edge_ref[:, q].reshape(cols, lanes)
    linked = product(parts_of(edges, 3), table_list(links_ref, last), DIRECT)
    gone = (inner_ref[q] + linked) * inverse_ref[last]
    nodes = product(parts_of(gone, 3), table_list(basis_ref, last), DIRECT)
    whole = jnp.concatenate([nodes, edges], axis=1).T
    values = product(parts_of(whole, 3), table_list(hart_ref), DIRECT)

    def piece(start, count):
        return values[start : start + count]

    rims = lanes + 4 * rows
    phi = []
    for t in range(here):
        for b in range(pair):
            if t == 0:
                phi.append(piece(lanes + b * rows, rows))
            else:
                row = piece(lanes + slots(here, rows, b, "row", t), 1)
                phi.append(jnp.where(row_index == 0, row, piece((t * pair + b) * rows, rows)))
    for b in range(pair):
        phi.append(piece(lanes + (pair + b) * rows, rows))
    for t in range(here):
        for b in range(pair):
            mine = phi[t * pair + b]
            time_rate = phi[(t + 1) * pair + b] - mine
            if t == here - 1:
                time_rate = time_rate * inside
            row = piece(lanes + slots(here, rows, b, "next", t), 1)
            below = jnp.where(row_index == rows - 1, row, pltpu.roll(mine, rows - 1, 0))
            gradient = (time_rate, below - mine, pltpu.roll(mine, cols - 1, 1) - mine)
            mult = [mult_ref[c, t, q * pair + b] for c in range(3)]
            time_part, one, two = (g + m for g, m in zip(gradient, mult))
            kinetic = 0.5 * (one * one + two * two)
            center = 1.0 + time_part
            scaling = jnp.maximum(center, 1.0) + jnp.exp(jnp.log(kinetic) * (1.0 / 3.0))
            twice = center + center
            for _ in range(NEWTON):
                residue = scaling * scaling * (scaling - center) - kinetic
                derivative = scaling * (3.0 * scaling - twice)
                change = residue * pl.reciprocal(derivative, approx=True)
                scaling = jnp.maximum(scaling - change, 1.0)
            feasible = time_part + kinetic <= 0.0
            shrink = jnp.where(feasible, 1.0, 1.0 / scaling)
            fresh = (
                jnp.where(feasible, time_part, time_part - (scaling - 1.0)),
                one * shrink,
                two * shrink,
            )
            for c in range(3):
                aux_out[c, t, q * pair + b] = fresh[c]
                mult_out[c, t, q * pair + b] = mult[c] + (gradient[c] - fresh[c])


def params(size=48):
    return pltpu.CompilerParams(vmem_limit_bytes=size * 1024 * 1024)


def whole_block(array):
    return pl.BlockSpec(array.shape, lambda p: (0,) * array.ndim)


def local(multiplier, auxiliary, density_start, density_end):
    _, here, batch, rows, cols = multiplier.shape
    time_blocks = lax.axis_size("py")
    row_blocks = lax.axis_size("grp") * lax.axis_size("px")
    levels = here * time_blocks
    row_count = rows * row_blocks
    pair = batch // time_blocks
    width = cols // row_blocks
    lanes = here * pair * rows
    both = [interior_tables(here, rows, cols, last) for last in (False, True)]
    hart_cols = table_parts(hartley_table(cols), 3)
    hart_rows = table_parts(hartley_table(row_count), 3)
    basis2 = np.stack([table_parts(one[0], 2) for one in both])
    basis3 = np.stack([table_parts(one[0].T, 3) for one in both])
    inverse = np.stack([one[1] for one in both]).astype(np.float32)
    to_edges = np.stack([table_parts(one[2], 2) for one in both])
    from_edges = np.stack([table_parts(one[3], 3) for one in both])
    ones = constant_source(here, rows, time_blocks, row_blocks, both).astype(np.float32)
    factors = elimination_table(levels, row_count, cols, row_blocks)

    group = GROUP
    five = pl.BlockSpec((3, here, pair * group, rows, cols), lambda p: (0, 0, p, 0, 0))
    chunks = pl.BlockSpec((row_blocks, group, width, lanes), lambda p: (0, p, 0, 0))
    away = pl.BlockSpec(memory_space=pltpu.HBM)
    chunked = jax.ShapeDtypeStruct((row_blocks, time_blocks, width, lanes), jnp.float32)
    kept = pl.BlockSpec((group, cols, lanes), lambda p: (p, 0, 0))
    edges, inner = pl.pallas_call(
        functools.partial(source_kernel, levels, pair),
        grid=(time_blocks // group,),
        in_specs=[five, five] + [away] * 6,
        out_specs=[chunks, kept],
        out_shape=[chunked, jax.ShapeDtypeStruct((time_blocks, cols, lanes), jnp.float32)],
        scratch_shapes=[
            pltpu.VMEM((2,) + density_start.shape, jnp.float32),
            pltpu.VMEM((2, cols, cols), jnp.bfloat16),
            pltpu.VMEM(basis2.shape[1:], jnp.bfloat16),
            pltpu.VMEM(inverse.shape[1:], jnp.float32),
            pltpu.VMEM(to_edges.shape[1:], jnp.bfloat16),
            pltpu.SemaphoreType.DMA((6,)),
        ],
        compiler_params=params(56),
        name="source",
    )(multiplier, auxiliary, density_start, density_end, hart_cols[:2], basis2, inverse, to_edges)

    def spread(value):
        flat = value.reshape((row_blocks * time_blocks,) + value.shape[2:])
        return lax.all_to_all(flat, EVERY, 0, 0, tiled=True).reshape(value.shape)

    vmem = pl.BlockSpec(memory_space=pltpu.VMEM)
    solved = pl.pallas_call(
        solve_kernel,
        in_specs=[vmem, vmem, vmem, pl.BlockSpec(memory_space=pl.ANY)],
        out_specs=vmem,
        out_shape=chunked,
        scratch_shapes=[
            pltpu.VMEM((levels, pair, width, row_count), jnp.float32),
            pltpu.VMEM((pair, width, row_count), jnp.float32),
            pltpu.VMEM(factors.shape[1:], jnp.float32),
            pltpu.SemaphoreType.DMA,
        ],
        compiler_params=params(),
        name="solve",
    )(spread(edges), hart_rows, ones, factors)

    result = jax.ShapeDtypeStruct(multiplier.shape, jnp.float32)
    mult_next, aux_next = pl.pallas_call(
        functools.partial(step_kernel, levels, pair),
        grid=(time_blocks // group,),
        in_specs=[five, chunks, kept]
        + [whole_block(a) for a in (hart_cols, from_edges, inverse, basis3)],
        out_specs=[five, five],
        out_shape=[result, result],
        compiler_params=params(),
        name="step",
    )(multiplier, spread(solved), inner, hart_cols, from_edges, inverse, basis3)
    return mult_next, aux_next


def solution(mesh):
    field = P(None, "py", None, ROWS, None)
    density = P(None, ROWS, None)
    return jax.shard_map(
        local,
        mesh=mesh,
        in_specs=(field, field, density, density),
        out_specs=(field, field),
        check_vma=False,
    )
```

```python
import functools

import jax
import jax.numpy as jnp
import numpy as np
from jax import lax
from jax.experimental import pallas as pl
from jax.experimental.pallas import tpu as pltpu
from jax.sharding import PartitionSpec as P

NEWTON = 4
ROWS = ("grp", "px")
EVERY = ("grp", "px", "py")
GROUP = 2
VMEM_BYTES = 48 * 1024 * 1024
DIRECT = ((1,), (0,))
CROSS = ((1,), (1,))


def table_parts(table, count):
    rest = np.asarray(table, np.float32)
    parts = []
    for _ in range(count):
        parts.append(rest.astype(jnp.bfloat16))
        rest = rest - parts[-1].astype(np.float32)
    return np.stack(parts)


def parts_of(value, count):
    parts = [value.astype(jnp.bfloat16)]
    for _ in range(count - 1):
        value = value - parts[-1].astype(jnp.float32)
        parts.append(value.astype(jnp.bfloat16))
    return parts


def orders(count):
    return [(i, order - i) for order in range(count - 1, -1, -1) for i in range(order + 1)]


def long_table(table, count, axis):
    parts = table_parts(table, count)
    return np.concatenate([parts[j] for _, j in orders(count)], axis=axis)


def long_data(value, count, axis):
    parts = parts_of(value, count)
    return jnp.concatenate([parts[i] for i, _ in orders(count)], axis=axis)


def wide_table(table, count):
    parts = table_parts(table, count)
    none = np.zeros_like(parts[0])
    if count == 2:
        grid = [(0, 1), (0, None)]
    else:
        grid = [(0, 1), (0, 1), (2, None), (0, None)]
    return np.block([[none if k is None else parts[k] for k in row] for row in grid])


def wide_product(value, table, count):
    parts = parts_of(value, count)
    data = parts if count == 2 else [parts[0], parts[1], parts[0], parts[2]]
    both = one_product(jnp.concatenate(data, axis=1), table, DIRECT)
    half = both.shape[1] // 2
    return both[:, :half] + both[:, half:]


def one_product(left, right, dims):
    return lax.dot_general(left, right, (dims, ((), ())), preferred_element_type=jnp.float32)


def squared_sines(length, period):
    return 4.0 * np.sin(np.pi * np.arange(length) / period) ** 2


def hartley_table(length):
    index = np.arange(length)
    angles = (index[:, None] * index[None, :] % length) * (2.0 * np.pi / length)
    return (np.cos(angles) + np.sin(angles)) / np.sqrt(length)


def elimination_table(levels, row_count, col_count, blocks, pieces, pair):
    eigen = squared_sines(col_count, col_count)[:, None] + squared_sines(row_count, row_count)
    factors = [1.0 / (1.0 + eigen)]
    for _ in range(levels // 2 - 1):
        factors.append(1.0 / (2.0 + eigen - factors[-1]))
    gap = 1.0 - factors[-1] ** 2
    middle = np.where(eigen > 0.0, 1.0 / np.where(eigen > 0.0, gap, 1.0), 0.0)
    table = np.stack(factors + [middle]).astype(np.float32)
    table = table.reshape(levels // 2 + 1, pieces, blocks, 1, -1, row_count).transpose(2, 0, 1, 3, 4, 5)
    table = np.broadcast_to(table, table.shape[:3] + (pair,) + table.shape[4:])
    return np.ascontiguousarray(table).reshape(blocks, levels // 2 + 1, -1, row_count)


def slots(here, rows, b, kind, index):
    if kind == "level":
        return b * rows + index
    if kind == "later":
        return (2 + b) * rows + index
    base = 4 * rows + b * (rows // 2)
    return base + (index - 1 if kind == "row" else here - 1 + index)


def interior_tables(here, rows, cols, last):
    pair = 2
    lanes = here * pair * rows
    inner = here - 1
    chain = 2.0 * np.eye(inner) - np.eye(inner, k=1) - np.eye(inner, k=-1)
    if last:
        chain[-1, -1] = 1.0
    time_values, time_basis = np.linalg.eigh(chain)
    row_index = np.arange(1, rows)
    row_basis = np.sqrt(2.0 / rows) * np.sin(np.pi * np.outer(row_index, row_index) / rows)
    row_values = squared_sines(rows, 2 * rows)
    col_values = squared_sines(cols, cols)
    basis = np.zeros((here, pair, rows, here, pair, rows))
    inverse = np.zeros((cols, here, pair, rows))
    linked = np.zeros((here, pair, rows, lanes))
    for b in range(pair):
        for k in range(1, here):
            for t in range(1, here):
                basis[t, b, 1:, k, b, 1:] = time_basis[t - 1, k - 1] * row_basis
            inverse[:, k, b, 1:] = 1.0 / (
                col_values[:, None] + time_values[k - 1] + row_values[None, 1:]
            )
        for x in range(1, rows):
            linked[1, b, x, slots(here, rows, b, "level", x)] = 1.0
            if not last:
                linked[here - 1, b, x, slots(here, rows, b, "later", x)] = 1.0
        for t in range(1, here):
            linked[t, b, 1, slots(here, rows, b, "row", t)] = 1.0
            linked[t, b, rows - 1, slots(here, rows, b, "next", t)] = 1.0
    basis = basis.reshape(lanes, lanes)
    linked = linked.reshape(lanes, lanes)
    inverse = inverse.reshape(cols, lanes)
    to_edges = basis.T @ linked
    from_edges = to_edges.T.copy()
    for b in range(pair):
        ones = np.zeros((here, pair, rows))
        ones[1:, b, 1:] = 1.0
        from_edges[slots(here, rows, b, "next", here)] = -(ones.reshape(-1) @ basis)
    return basis, inverse, to_edges, from_edges


def constant_source(here, rows, time_blocks, row_blocks, tables):
    levels, row_count = here * time_blocks, rows * row_blocks
    field = np.zeros((levels + 1, row_count))
    ones = np.zeros((here, 2, rows))
    ones[1:, 0, 1:] = 1.0
    for i in range(time_blocks):
        basis, inverse, to_edges, _ = tables[1 if i == time_blocks - 1 else 0]
        edge = ((ones.reshape(-1) @ basis) * inverse[0]) @ to_edges
        for j in range(row_blocks):
            t0, x0 = i * here, j * rows
            for x in range(rows):
                field[t0, x0 + x] += 1.0 + edge[slots(here, rows, 0, "level", x)]
                field[t0 + here, x0 + x] += edge[slots(here, rows, 0, "later", x)]
            for t in range(here):
                after = (x0 + rows) % row_count
                field[t0 + t, after] += edge[slots(here, rows, 0, "next", t)]
                if t > 0:
                    field[t0 + t, x0] += 1.0 + edge[slots(here, rows, 0, "row", t)]
    return field[:levels] @ hartley_table(row_count)


def exchange_pieces(blocks, width):
    count = len(blocks)
    lanes = count * width
    group = lax.broadcasted_iota(jnp.int32, blocks[0].shape, 1) // width
    step = 1
    while step < count:
        upper = (group // step) % 2 == 1
        fresh = list(blocks)
        for j in range(count):
            if (j // step) % 2 == 0:
                low, high = blocks[j], blocks[j + step]
                fresh[j] = jnp.where(upper, pltpu.roll(high, step * width, 1), low)
                fresh[j + step] = jnp.where(upper, high, pltpu.roll(low, lanes - step * width, 1))
        blocks = fresh
        step *= 2
    return blocks


def source_kernel(
    levels,
    pair,
    mult_ref,
    aux_ref,
    start_hbm,
    end_hbm,
    hart_hbm,
    basis_hbm,
    inverse_hbm,
    edges_hbm,
    out_ref,
    inner_ref,
    density_ref,
    hart_ref,
    basis_ref,
    inverse_ref,
    edges_ref,
    sems,
):
    _, here, batch, rows, cols = mult_ref.shape
    lanes = here * pair * rows
    pieces = lanes // rows
    each = cols // pieces
    first = lax.axis_index("py") * here
    last = (first + here == levels).astype(jnp.int32)
    starts = jnp.where(first == 0, 1.0, 0.0)
    ends = last.astype(jnp.float32)
    step = pl.program_id(0)

    def tables():
        return [
            pltpu.make_async_copy(hart_hbm, hart_ref, sems.at[2]),
            pltpu.make_async_copy(basis_hbm.at[last], basis_ref, sems.at[3]),
            pltpu.make_async_copy(inverse_hbm.at[last], inverse_ref, sems.at[4]),
            pltpu.make_async_copy(edges_hbm.at[last], edges_ref, sems.at[5]),
        ]

    @pl.when(step == 0)
    def _():
        copies = [
            pltpu.make_async_copy(start_hbm, density_ref.at[0], sems.at[0]),
            pltpu.make_async_copy(end_hbm, density_ref.at[1], sems.at[1]),
        ]
        for copy in copies + tables():
            copy.start()
        for copy in copies:
            copy.wait()

    row_index = lax.broadcasted_iota(jnp.int32, (rows, cols), 0)
    first_row = row_index == 0
    field = []
    for q in range(batch // pair):
        blocks = []
        earlier = [0.0] * pair
        rims = jnp.zeros((rows, cols), jnp.float32)
        for t in range(here):
            for b in range(pair):
                at = q * pair + b
                time = aux_ref[0, t, at] - mult_ref[0, t, at]
                if t == here - 1:
                    time = time * (1.0 - ends)
                along = aux_ref[1, t, at] - mult_ref[1, t, at]
                second = aux_ref[2, t, at] - mult_ref[2, t, at]
                beside = jnp.where(first_row, 0.0, pltpu.roll(along, 1, 0))
                total = (earlier[b] - time) + (beside - along)
                total = total + (pltpu.roll(second, 1, 1) - second)
                if t == 0:
                    total = total - density_ref[0, step * batch + at] * starts
                if t == here - 1:
                    total = total + density_ref[1, step * batch + at] * ends
                earlier[b] = time
                blocks.append(total)
                base = b * (rows // 2)
                if t > 0:
                    rims = jnp.where(row_index == base + t - 1, total[:1], rims)
                rims = jnp.where(row_index == base + here - 1 + t, along[rows - 1 :], rims)
        spare = jnp.zeros((lanes - (2 * pair + 1) * rows, cols), jnp.float32)
        nodes = jnp.concatenate(blocks + blocks[:pair] + earlier + [rims, spare], axis=0)
        field.append(long_data(nodes, 2, 1))

    @pl.when(step == 0)
    def _():
        for copy in tables():
            copy.wait()

    modes = [one_product(hart_ref[...], nodes, CROSS) for nodes in field]
    inner = [wide_product(mode[:, :lanes], basis_ref[...], 2) for mode in modes]
    gone = [wide_product(value * inverse_ref[...], edges_ref[...], 2) for value in inner]
    for q in range(batch // pair):
        inner_ref[q] = inner[q]
        edges = modes[q][:, lanes:] + gone[q]
        blocks = exchange_pieces([edges[j * each : (j + 1) * each] for j in range(pieces)], rows)
        for k in range(out_ref.shape[2]):
            out_ref[:, q, k] = blocks[k].reshape(out_ref.shape[0], out_ref.shape[3], lanes)


def solve_kernel(
    in_ref, hart_ref, back_ref, ones_ref, table_ref, out_ref, field_ref, mean_ref, factor_ref, rim_ref, sem
):
    row_blocks, time_blocks, kinds, few, lanes = in_ref.shape
    levels, high, cols = field_ref.shape
    here = levels // time_blocks
    rows = cols // row_blocks
    pieces = lanes // rows
    tall = (kinds - 1) * few
    count = high // tall
    half = levels // 2
    mine = lax.axis_index("grp") * lax.axis_size("px") + lax.axis_index("px")
    fetch = pltpu.make_async_copy(table_ref.at[mine], factor_ref, sem)
    fetch.start()
    stack = tall // few
    lane = lax.broadcasted_iota(jnp.int32, (tall, cols), 1) % rows
    row = lax.broadcasted_iota(jnp.int32, (tall, cols), 0)
    low = row < tall // 2
    even = (row // few) % 2 == 0

    def shift(value, steps):
        return pltpu.roll(value, steps % cols, 1)

    def swap(value):
        return pltpu.roll(value, tall // 2, 0)

    def offset(kind, t):
        return slots(here, rows, 0, kind, t) - 4 * rows

    def exchange(get):
        groups = [
            exchange_pieces([get(g * pieces + j) for j in range(pieces)], rows)
            for g in range(row_blocks // pieces)
        ]
        return [jnp.concatenate([group[k] for group in groups], axis=1) for k in range(pieces)]

    for h in range(time_blocks // stack):
        times = slice(h * stack, (h + 1) * stack)
        for j, rim in enumerate(exchange(lambda x: in_ref[x, times, kinds - 1].reshape(tall, lanes))):
            rim_ref[h, j, 0] = rim
            rim_ref[h, j, 1] = shift(rim, -(rows // 2))

    def forward(i, carry):
        main = exchange(lambda x: in_ref[x, i, : kinds - 1].reshape(tall, lanes))
        here_rows = slice(i % stack * few, (i % stack + 1) * few)
        field = [[] for _ in range(here)]
        later = []
        for q in range(count):
            one, two = main[2 * q], main[2 * q + 1]
            level = jnp.where(low, one, swap(two)) + carry[q]
            later.append(jnp.where(low, swap(one), two))
            rim = jnp.concatenate(
                [rim_ref[i // stack, 2 * q + j, b, here_rows] for j in range(2) for b in range(2)],
                axis=0,
            )
            for t in range(here):
                value = shift(rim, rows - offset("next", t))
                if t > 0:
                    value = value + shift(rim, -offset("row", t))
                value = jnp.where(lane == 0, value, 0.0)
                field[t].append(value + level if t == 0 else value)
        field = jnp.concatenate(sum(field, []), axis=0)
        modes = one_product(long_data(field, 2, 1), hart_ref[...], DIRECT)
        field_ref[pl.ds(i * here, here)] = modes.reshape(here, high, cols)
        return tuple(later)

    blank = jnp.zeros((tall, cols), jnp.float32)
    carry = (blank,) * count
    for i in range(time_blocks):
        carry = forward(i, carry)
    fetch.wait()

    mean_ref[...] = jnp.zeros(mean_ref.shape, jnp.float32)

    @pl.when(mine == 0)
    def _():
        shape = (tall, 128)
        spot = lax.broadcasted_iota(jnp.int32, shape, 0)
        zero = (spot % few == 0) & (spot < tall // 2)
        zero = zero & (lax.broadcasted_iota(jnp.int32, shape, 1) == 0)
        scale = float(np.sqrt(cols)) / (levels * cols)
        sums = field_ref[0, :tall, :128]
        for t in range(1, levels):
            sums = sums + field_ref[t, :tall, :128]
        mean = jnp.sum(jnp.where(zero, sums * scale, 0.0), axis=1, keepdims=True)
        mean_ref[0] = jnp.broadcast_to(mean, (tall, cols))
        for t in range(levels):
            field_ref[t, :tall] = field_ref[t, :tall] - mean * ones_ref[t : t + 1]

    left = jnp.zeros(field_ref.shape[1:], jnp.float32)
    right = left
    for t in range(half):
        factor = factor_ref[t]
        left = (field_ref[t] + left) * factor
        right = (field_ref[levels - 1 - t] + right) * factor
        if t < half - 1:
            field_ref[t] = left
            field_ref[levels - 1 - t] = right
    first = (left + factor * right) * factor_ref[half]
    right = right + factor * first
    left = first
    field_ref[half - 1] = left
    field_ref[half] = right
    for t in range(half - 2, -1, -1):
        factor = factor_ref[t]
        left = field_ref[t] + factor * left
        right = field_ref[levels - 1 - t] + factor * right
        field_ref[t] = left
        field_ref[levels - 1 - t] = right

    def backward(i, carry):
        here_rows = slice(i % stack * few, (i % stack + 1) * few)
        field = field_ref[pl.ds(i * here, here)].reshape(here * high, cols)
        values = one_product(long_data(field, 3, 1), back_ref[...], DIRECT)
        main, first = [], []
        for q in range(count):
            part = [values[t * high + q * tall : t * high + (q + 1) * tall] for t in range(here)]
            rim = jnp.where(lane == offset("next", here), mean_ref[q], 0.0)
            for t in range(here):
                at = offset("next", t)
                rim = jnp.where(lane == at, shift(part[t], at - rows), rim)
                if t > 0:
                    at = offset("row", t)
                    rim = jnp.where(lane == at, shift(part[t], at), rim)
            rim = jnp.where(even, rim, shift(rim, rows // 2))
            rim = rim + pltpu.roll(rim, tall - few, 0)
            rim_ref[i // stack, 2 * q, 0, here_rows] = rim[:few]
            rim_ref[i // stack, 2 * q + 1, 0, here_rows] = rim[tall // 2 : tall // 2 + few]
            main.append(jnp.where(low, part[0], swap(carry[q])))
            main.append(jnp.where(low, swap(part[0]), carry[q]))
            first.append(part[0])
        for g in range(row_blocks // pieces):
            cut = slice(g * lanes, (g + 1) * lanes)
            for j, value in enumerate(exchange_pieces([a[:, cut] for a in main], rows)):
                out_ref[g * pieces + j, i, : kinds - 1] = value.reshape(kinds - 1, few, lanes)
        return tuple(first)

    carry = (blank,) * count
    for i in range(time_blocks - 1, -1, -1):
        carry = backward(i, carry)
    for h in range(time_blocks // stack):
        times = slice(h * stack, (h + 1) * stack)
        for g in range(row_blocks // pieces):
            cut = slice(g * lanes, (g + 1) * lanes)
            rims = exchange_pieces([rim_ref[h, j, 0, :, cut] for j in range(pieces)], rows)
            for j, value in enumerate(rims):
                out_ref[g * pieces + j, times, kinds - 1] = value.reshape(stack, few, lanes)


def step_kernel(
    levels,
    pair,
    mult_ref,
    edge_ref,
    inner_ref,
    hart_ref,
    links_ref,
    inverse_ref,
    basis_ref,
    mult_out,
    aux_out,
):
    _, here, batch, rows, cols = mult_ref.shape
    lanes = here * pair * rows
    pieces = lanes // rows
    kinds = edge_ref.shape[2]
    first = lax.axis_index("py") * here
    last = (first + here == levels).astype(jnp.int32)
    inside = 1.0 - last.astype(jnp.float32)
    row_index = lax.broadcasted_iota(jnp.int32, (rows, cols), 0)
    edges = []
    for q in range(batch // pair):
        blocks = [edge_ref[:, q, k].reshape(cols // pieces, lanes) for k in range(kinds)]
        blocks += [jnp.zeros((cols // pieces, lanes), jnp.float32)] * (pieces - kinds)
        edges.append(jnp.concatenate(exchange_pieces(blocks, rows), axis=0))
    linked = [wide_product(edge, links_ref[last], 3) for edge in edges]
    gone = [(inner_ref[q] + linked[q]) * inverse_ref[last] for q in range(batch // pair)]
    nodes = [wide_product(value, basis_ref[last], 3) for value in gone]
    whole = [jnp.concatenate(both, axis=1).T[: lanes + kinds * rows] for both in zip(nodes, edges)]
    potential = [one_product(long_data(value, 3, 1), hart_ref[...], DIRECT) for value in whole]
    for q in range(batch // pair):
        step_part(q, pair, potential[q], inside, row_index, mult_ref, mult_out, aux_out)


def step_part(q, pair, values, inside, row_index, mult_ref, mult_out, aux_out):
    _, here, _, rows, cols = mult_ref.shape
    lanes = here * pair * rows

    def piece(start, count):
        return values[start : start + count]

    rims = lanes + 4 * rows
    phi = []
    for t in range(here):
        for b in range(pair):
            if t == 0:
                phi.append(piece(lanes + b * rows, rows))
            else:
                row = piece(lanes + slots(here, rows, b, "row", t), 1)
                phi.append(jnp.where(row_index == 0, row, piece((t * pair + b) * rows, rows)))
    for b in range(pair):
        phi.append(piece(lanes + (pair + b) * rows, rows))
    for t in range(here):
        for b in range(pair):
            mine = phi[t * pair + b]
            time_rate = phi[(t + 1) * pair + b] - mine
            if t == here - 1:
                time_rate = time_rate * inside
            row = piece(lanes + slots(here, rows, b, "next", t), 1)
            below = jnp.where(row_index == rows - 1, row, pltpu.roll(mine, rows - 1, 0))
            gradient = (time_rate, below - mine, pltpu.roll(mine, cols - 1, 1) - mine)
            mult = [mult_ref[c, t, q * pair + b] for c in range(3)]
            time_part, one, two = (g + m for g, m in zip(gradient, mult))
            kinetic = 0.5 * (one * one + two * two)
            center = 1.0 + time_part
            scaling = jnp.maximum(center, 1.0) + jnp.exp(jnp.log(kinetic) * (1.0 / 3.0))
            twice = center + center
            for _ in range(NEWTON):
                residue = scaling * scaling * (scaling - center) - kinetic
                derivative = scaling * (3.0 * scaling - twice)
                change = residue * pl.reciprocal(derivative, approx=True)
                scaling = jnp.maximum(scaling - change, 1.0)
            feasible = time_part + kinetic <= 0.0
            shrink = jnp.where(feasible, 1.0, 1.0 / scaling)
            fresh = (
                jnp.where(feasible, time_part, time_part - (scaling - 1.0)),
                one * shrink,
                two * shrink,
            )
            for c in range(3):
                aux_out[c, t, q * pair + b] = fresh[c]
                mult_out[c, t, q * pair + b] = mult[c] + (gradient[c] - fresh[c])


def params(size=48):
    return pltpu.CompilerParams(vmem_limit_bytes=size * 1024 * 1024)


def whole_block(array):
    return pl.BlockSpec(array.shape, lambda p: (0,) * array.ndim)


def local(multiplier, auxiliary, density_start, density_end):
    _, here, batch, rows, cols = multiplier.shape
    time_blocks = lax.axis_size("py")
    row_blocks = lax.axis_size("grp") * lax.axis_size("px")
    levels = here * time_blocks
    row_count = rows * row_blocks
    pair = batch // time_blocks
    lanes = here * pair * rows
    pieces = lanes // rows
    kinds = 2 * pair + 1
    few = cols // (pieces * row_blocks)
    both = [interior_tables(here, rows, cols, last) for last in (False, True)]
    hart_there = long_table(hartley_table(cols), 2, 1)
    hart_back = long_table(hartley_table(cols), 3, 0)
    rows_there = long_table(hartley_table(row_count), 2, 0)
    rows_back = long_table(hartley_table(row_count), 3, 0)
    basis2 = np.stack([wide_table(one[0], 2) for one in both])
    basis3 = np.stack([wide_table(one[0].T, 3) for one in both])
    inverse = np.stack([one[1] for one in both]).astype(np.float32)
    to_edges = np.stack([wide_table(one[2], 2) for one in both])
    from_edges = np.stack([wide_table(one[3], 3) for one in both])
    ones = constant_source(here, rows, time_blocks, row_blocks, both).astype(np.float32)
    factors = elimination_table(levels, row_count, cols, row_blocks, pieces, pair)

    group = GROUP
    five = pl.BlockSpec((3, here, pair * group, rows, cols), lambda p: (0, 0, p, 0, 0))
    chunks = pl.BlockSpec((row_blocks, group, kinds, few, lanes), lambda p: (0, p, 0, 0, 0))
    away = pl.BlockSpec(memory_space=pltpu.HBM)
    chunked = jax.ShapeDtypeStruct((row_blocks, time_blocks, kinds, few, lanes), jnp.float32)
    kept = pl.BlockSpec((group, cols, lanes), lambda p: (p, 0, 0))
    edges, inner = pl.pallas_call(
        functools.partial(source_kernel, levels, pair),
        grid=(time_blocks // group,),
        in_specs=[five, five] + [away] * 6,
        out_specs=[chunks, kept],
        out_shape=[chunked, jax.ShapeDtypeStruct((time_blocks, cols, lanes), jnp.float32)],
        scratch_shapes=[
            pltpu.VMEM((2,) + density_start.shape, jnp.float32),
            pltpu.VMEM(hart_there.shape, jnp.bfloat16),
            pltpu.VMEM(basis2.shape[1:], jnp.bfloat16),
            pltpu.VMEM(inverse.shape[1:], jnp.float32),
            pltpu.VMEM(to_edges.shape[1:], jnp.bfloat16),
            pltpu.SemaphoreType.DMA((6,)),
        ],
        compiler_params=params(56),
        name="source",
    )(multiplier, auxiliary, density_start, density_end, hart_there, basis2, inverse, to_edges)

    def spread(value):
        flat = value.reshape((row_blocks * time_blocks,) + value.shape[2:])
        return lax.all_to_all(flat, EVERY, 0, 0, tiled=True).reshape(value.shape)

    vmem = pl.BlockSpec(memory_space=pltpu.VMEM)
    solved = pl.pallas_call(
        solve_kernel,
        in_specs=[vmem, vmem, vmem, vmem, pl.BlockSpec(memory_space=pl.ANY)],
        out_specs=vmem,
        out_shape=chunked,
        scratch_shapes=[
            pltpu.VMEM((levels, pair * pieces * few, row_count), jnp.float32),
            pltpu.VMEM((pieces // 2, 2 * pair * few, row_count), jnp.float32),
            pltpu.VMEM(factors.shape[1:], jnp.float32),
            pltpu.VMEM((time_blocks // (2 * pair), pieces, 2, 2 * pair * few, row_count), jnp.float32),
            pltpu.SemaphoreType.DMA,
        ],
        compiler_params=params(),
        name="solve",
    )(spread(edges), rows_there, rows_back, ones, factors)

    result = jax.ShapeDtypeStruct(multiplier.shape, jnp.float32)
    mult_next, aux_next = pl.pallas_call(
        functools.partial(step_kernel, levels, pair),
        grid=(time_blocks // group,),
        in_specs=[five, chunks, kept]
        + [whole_block(a) for a in (hart_back, from_edges, inverse, basis3)],
        out_specs=[five, five],
        out_shape=[result, result],
        compiler_params=params(),
        name="step",
    )(multiplier, spread(solved), inner, hart_back, from_edges, inverse, basis3)
    return mult_next, aux_next


def solution(mesh):
    field = P(None, "py", None, ROWS, None)
    density = P(None, ROWS, None)
    return jax.shard_map(
        local,
        mesh=mesh,
        in_specs=(field, field, density, density),
        out_specs=(field, field),
        check_vma=False,
    )
```

```python
import functools

import jax
import jax.numpy as jnp
import numpy as np
from jax import lax
from jax.experimental import pallas as pl
from jax.experimental.pallas import tpu as pltpu
from jax.sharding import PartitionSpec as P

NEWTON = 4
ROWS = ("grp", "px")
EVERY = ("grp", "px", "py")
PARTS = 2
STEP_PARTS = 2
VMEM_BYTES = 48 * 1024 * 1024
DIRECT = ((1,), (0,))
CROSS = ((1,), (1,))


def table_parts(table, count):
    rest = np.asarray(table, np.float32)
    parts = []
    for _ in range(count):
        parts.append(rest.astype(jnp.bfloat16))
        rest = rest - parts[-1].astype(np.float32)
    return np.stack(parts)


def parts_of(value, count):
    parts = [value.astype(jnp.bfloat16)]
    for _ in range(count - 1):
        value = value - parts[-1].astype(jnp.float32)
        parts.append(value.astype(jnp.bfloat16))
    return parts


def orders(count):
    return [(i, order - i) for order in range(count - 1, -1, -1) for i in range(order + 1)]


def long_table(table, count, axis):
    parts = table_parts(table, count)
    return np.concatenate([parts[j] for _, j in orders(count)], axis=axis)


def long_data(value, count, axis):
    parts = parts_of(value, count)
    return jnp.concatenate([parts[i] for i, _ in orders(count)], axis=axis)


def wide_table(table, count):
    parts = table_parts(table, count)
    none = np.zeros_like(parts[0])
    if count == 2:
        grid = [(0, 1), (0, None)]
    else:
        grid = [(0, 1), (0, 1), (2, None), (0, None)]
    return np.block([[none if k is None else parts[k] for k in row] for row in grid])


def wide_product(value, table, count):
    parts = parts_of(value, count)
    data = parts if count == 2 else [parts[0], parts[1], parts[0], parts[2]]
    both = one_product(jnp.concatenate(data, axis=1), table, DIRECT)
    half = both.shape[1] // 2
    return both[:, :half] + both[:, half:]


def one_product(left, right, dims):
    return lax.dot_general(left, right, (dims, ((), ())), preferred_element_type=jnp.float32)


def squared_sines(length, period):
    return 4.0 * np.sin(np.pi * np.arange(length) / period) ** 2


def hartley_table(length):
    index = np.arange(length)
    angles = (index[:, None] * index[None, :] % length) * (2.0 * np.pi / length)
    return (np.cos(angles) + np.sin(angles)) / np.sqrt(length)


def elimination_table(levels, row_count, col_count, blocks, pieces, pair):
    eigen = squared_sines(col_count, col_count)[:, None] + squared_sines(row_count, row_count)
    factors = [1.0 / (1.0 + eigen)]
    for _ in range(levels // 2 - 1):
        factors.append(1.0 / (2.0 + eigen - factors[-1]))
    gap = 1.0 - factors[-1] ** 2
    middle = np.where(eigen > 0.0, 1.0 / np.where(eigen > 0.0, gap, 1.0), 0.0)
    table = np.stack(factors + [middle]).astype(np.float32)
    table = table.reshape(levels // 2 + 1, pieces, blocks, 1, -1, row_count).transpose(2, 0, 1, 3, 4, 5)
    table = np.broadcast_to(table, table.shape[:3] + (pair,) + table.shape[4:])
    return np.ascontiguousarray(table).reshape(blocks, levels // 2 + 1, -1, row_count)


def slots(here, rows, b, kind, index):
    if kind == "level":
        return b * rows + index
    if kind == "later":
        return (2 + b) * rows + index
    base = 4 * rows + b * (rows // 2)
    return base + (index - 1 if kind == "row" else here - 1 + index)


def interior_tables(here, rows, cols, last):
    pair = 2
    lanes = here * pair * rows
    inner = here - 1
    chain = 2.0 * np.eye(inner) - np.eye(inner, k=1) - np.eye(inner, k=-1)
    if last:
        chain[-1, -1] = 1.0
    time_values, time_basis = np.linalg.eigh(chain)
    row_index = np.arange(1, rows)
    row_basis = np.sqrt(2.0 / rows) * np.sin(np.pi * np.outer(row_index, row_index) / rows)
    row_values = squared_sines(rows, 2 * rows)
    col_values = squared_sines(cols, cols)
    basis = np.zeros((here, pair, rows, here, pair, rows))
    inverse = np.zeros((cols, here, pair, rows))
    linked = np.zeros((here, pair, rows, lanes))
    for b in range(pair):
        for k in range(1, here):
            for t in range(1, here):
                basis[t, b, 1:, k, b, 1:] = time_basis[t - 1, k - 1] * row_basis
            inverse[:, k, b, 1:] = 1.0 / (
                col_values[:, None] + time_values[k - 1] + row_values[None, 1:]
            )
        for x in range(1, rows):
            linked[1, b, x, slots(here, rows, b, "level", x)] = 1.0
            if not last:
                linked[here - 1, b, x, slots(here, rows, b, "later", x)] = 1.0
        for t in range(1, here):
            linked[t, b, 1, slots(here, rows, b, "row", t)] = 1.0
            linked[t, b, rows - 1, slots(here, rows, b, "next", t)] = 1.0
    basis = basis.reshape(lanes, lanes)
    linked = linked.reshape(lanes, lanes)
    inverse = inverse.reshape(cols, lanes)
    to_edges = basis.T @ linked
    from_edges = to_edges.T.copy()
    for b in range(pair):
        ones = np.zeros((here, pair, rows))
        ones[1:, b, 1:] = 1.0
        from_edges[slots(here, rows, b, "next", here)] = -(ones.reshape(-1) @ basis)
    return basis, inverse, to_edges, from_edges


def constant_source(here, rows, time_blocks, row_blocks, tables):
    levels, row_count = here * time_blocks, rows * row_blocks
    field = np.zeros((levels + 1, row_count))
    ones = np.zeros((here, 2, rows))
    ones[1:, 0, 1:] = 1.0
    for i in range(time_blocks):
        basis, inverse, to_edges, _ = tables[1 if i == time_blocks - 1 else 0]
        edge = ((ones.reshape(-1) @ basis) * inverse[0]) @ to_edges
        for j in range(row_blocks):
            t0, x0 = i * here, j * rows
            for x in range(rows):
                field[t0, x0 + x] += 1.0 + edge[slots(here, rows, 0, "level", x)]
                field[t0 + here, x0 + x] += edge[slots(here, rows, 0, "later", x)]
            for t in range(here):
                after = (x0 + rows) % row_count
                field[t0 + t, after] += edge[slots(here, rows, 0, "next", t)]
                if t > 0:
                    field[t0 + t, x0] += 1.0 + edge[slots(here, rows, 0, "row", t)]
    return field[:levels] @ hartley_table(row_count)


def exchange_pieces(blocks, width):
    count = len(blocks)
    lanes = count * width
    group = lax.broadcasted_iota(jnp.int32, blocks[0].shape, 1) // width
    step = 1
    while step < count:
        upper = (group // step) % 2 == 1
        fresh = list(blocks)
        for j in range(count):
            if (j // step) % 2 == 0:
                low, high = blocks[j], blocks[j + step]
                fresh[j] = jnp.where(upper, pltpu.roll(high, step * width, 1), low)
                fresh[j + step] = jnp.where(upper, high, pltpu.roll(low, lanes - step * width, 1))
        blocks = fresh
        step *= 2
    return blocks


def source_kernel(
    levels,
    pair,
    mult_hbm,
    aux_hbm,
    start_hbm,
    end_hbm,
    hart_hbm,
    basis_hbm,
    inverse_hbm,
    edges_hbm,
    out_hbm,
    inner_hbm,
    mult_ref,
    aux_ref,
    density_ref,
    hart_ref,
    basis_ref,
    inverse_ref,
    edges_ref,
    out_ref,
    inner_ref,
    field_sems,
    table_sems,
    out_sems,
):
    _, here, batch, rows, cols = mult_ref.shape
    lanes = here * pair * rows
    pieces = lanes // rows
    each = cols // pieces
    total_pairs = batch // pair
    first = lax.axis_index("py") * here
    at_start = first == 0
    at_end = first + here == levels
    last = at_end.astype(jnp.int32)
    fields = []
    for part in range(PARTS):
        cut = pl.ds(part * batch // PARTS, batch // PARTS)
        fields.append(
            [
                pltpu.make_async_copy(
                    one.at[:, :, cut], other.at[:, :, cut], field_sems.at[n, part]
                )
                for n, (one, other) in enumerate(((mult_hbm, mult_ref), (aux_hbm, aux_ref)))
            ]
        )
    tables = [
        pltpu.make_async_copy(hart_hbm, hart_ref, table_sems.at[0]),
        pltpu.make_async_copy(basis_hbm.at[last], basis_ref, table_sems.at[1]),
        pltpu.make_async_copy(inverse_hbm.at[last], inverse_ref, table_sems.at[2]),
        pltpu.make_async_copy(edges_hbm.at[last], edges_ref, table_sems.at[3]),
    ]
    start_copy = pltpu.make_async_copy(start_hbm, density_ref.at[0], table_sems.at[4])
    end_copy = pltpu.make_async_copy(end_hbm, density_ref.at[1], table_sems.at[5])
    for copy in fields[0] + tables + [start_copy, end_copy] + sum(fields[1:], []):
        copy.start()

    row_index = lax.broadcasted_iota(jnp.int32, (rows, cols), 0)
    first_row = row_index == 0
    outs = []
    for part in range(PARTS):
        for copy in fields[part]:
            copy.wait()
        if part == 0:
            start_copy.wait()
            end_copy.wait()
        mine = range(part * total_pairs // PARTS, (part + 1) * total_pairs // PARTS)
        field = []
        for q in mine:
            blocks = []
            earlier = [0.0] * pair
            rims = jnp.zeros((rows, cols), jnp.float32)
            for t in range(here):
                for b in range(pair):
                    at = q * pair + b
                    time = aux_ref[0, t, at] - mult_ref[0, t, at]
                    if t == here - 1:
                        time = jnp.where(at_end, 0.0, time)
                    along = aux_ref[1, t, at] - mult_ref[1, t, at]
                    second = aux_ref[2, t, at] - mult_ref[2, t, at]
                    beside = jnp.where(first_row, 0.0, pltpu.roll(along, 1, 0))
                    total = (earlier[b] - time) + (beside - along)
                    total = total + (pltpu.roll(second, 1, 1) - second)
                    if t == 0:
                        total = total - jnp.where(at_start, density_ref[0, at], 0.0)
                    if t == here - 1:
                        total = total + jnp.where(at_end, density_ref[1, at], 0.0)
                    earlier[b] = time
                    blocks.append(total)
                    base = b * (rows // 2)
                    if t > 0:
                        rims = jnp.where(row_index == base + t - 1, total[:1], rims)
                    rims = jnp.where(row_index == base + here - 1 + t, along[rows - 1 :], rims)
            spare = jnp.zeros((lanes - (2 * pair + 1) * rows, cols), jnp.float32)
            nodes = jnp.concatenate(blocks + blocks[:pair] + earlier + [rims, spare], axis=0)
            field.append(long_data(nodes, 2, 1))
        if part == 0:
            for copy in tables:
                copy.wait()
        modes = [one_product(hart_ref[...], nodes, CROSS) for nodes in field]
        inner = [wide_product(mode[:, :lanes], basis_ref[...], 2) for mode in modes]
        gone = [wide_product(value * inverse_ref[...], edges_ref[...], 2) for value in inner]
        for n, q in enumerate(mine):
            inner_ref[q] = inner[n]
            edges = modes[n][:, lanes:] + gone[n]
            blocks = exchange_pieces(
                [edges[j * each : (j + 1) * each] for j in range(pieces)], rows
            )
            for k in range(out_ref.shape[2]):
                out_ref[:, q, k] = blocks[k].reshape(out_ref.shape[0], out_ref.shape[3], lanes)
        cut = pl.ds(mine[0], len(mine))
        outs += [
            pltpu.make_async_copy(out_ref.at[:, cut], out_hbm.at[:, cut], out_sems.at[0, part]),
            pltpu.make_async_copy(inner_ref.at[cut], inner_hbm.at[cut], out_sems.at[1, part]),
        ]
        for copy in outs[-2:]:
            copy.start()
    for copy in outs:
        copy.wait()


def solve_kernel(
    in_ref, hart_ref, back_ref, ones_ref, table_ref, out_ref, field_ref, mean_ref, factor_ref, rim_ref, sem
):
    row_blocks, time_blocks, kinds, few, lanes = in_ref.shape
    levels, high, cols = field_ref.shape
    here = levels // time_blocks
    rows = cols // row_blocks
    pieces = lanes // rows
    tall = (kinds - 1) * few
    count = high // tall
    half = levels // 2
    mine = lax.axis_index("grp") * lax.axis_size("px") + lax.axis_index("px")
    fetch = pltpu.make_async_copy(table_ref.at[mine], factor_ref, sem)
    fetch.start()
    stack = tall // few
    lane = lax.broadcasted_iota(jnp.int32, (tall, cols), 1) % rows
    row = lax.broadcasted_iota(jnp.int32, (tall, cols), 0)
    low = row < tall // 2
    even = (row // few) % 2 == 0

    def shift(value, steps):
        return pltpu.roll(value, steps % cols, 1)

    def swap(value):
        return pltpu.roll(value, tall // 2, 0)

    def offset(kind, t):
        return slots(here, rows, 0, kind, t) - 4 * rows

    def exchange(get):
        groups = [
            exchange_pieces([get(g * pieces + j) for j in range(pieces)], rows)
            for g in range(row_blocks // pieces)
        ]
        return [jnp.concatenate([group[k] for group in groups], axis=1) for k in range(pieces)]

    for h in range(time_blocks // stack):
        times = slice(h * stack, (h + 1) * stack)
        for j, rim in enumerate(exchange(lambda x: in_ref[x, times, kinds - 1].reshape(tall, lanes))):
            rim_ref[h, j, 0] = rim
            rim_ref[h, j, 1] = shift(rim, -(rows // 2))

    def forward(i, carry):
        main = exchange(lambda x: in_ref[x, i, : kinds - 1].reshape(tall, lanes))
        here_rows = slice(i % stack * few, (i % stack + 1) * few)
        field = [[] for _ in range(here)]
        later = []
        for q in range(count):
            one, two = main[2 * q], main[2 * q + 1]
            level = jnp.where(low, one, swap(two)) + carry[q]
            later.append(jnp.where(low, swap(one), two))
            rim = jnp.concatenate(
                [rim_ref[i // stack, 2 * q + j, b, here_rows] for j in range(2) for b in range(2)],
                axis=0,
            )
            for t in range(here):
                value = shift(rim, rows - offset("next", t))
                if t > 0:
                    value = value + shift(rim, -offset("row", t))
                value = jnp.where(lane == 0, value, 0.0)
                field[t].append(value + level if t == 0 else value)
        field = jnp.concatenate(sum(field, []), axis=0)
        modes = one_product(long_data(field, 2, 1), hart_ref[...], DIRECT)
        field_ref[pl.ds(i * here, here)] = modes.reshape(here, high, cols)
        return tuple(later)

    blank = jnp.zeros((tall, cols), jnp.float32)
    carry = (blank,) * count
    for i in range(time_blocks):
        carry = forward(i, carry)
    fetch.wait()

    mean_ref[...] = jnp.zeros(mean_ref.shape, jnp.float32)

    @pl.when(mine == 0)
    def _():
        shape = (tall, 128)
        spot = lax.broadcasted_iota(jnp.int32, shape, 0)
        zero = (spot % few == 0) & (spot < tall // 2)
        zero = zero & (lax.broadcasted_iota(jnp.int32, shape, 1) == 0)
        scale = float(np.sqrt(cols)) / (levels * cols)
        sums = field_ref[0, :tall, :128]
        for t in range(1, levels):
            sums = sums + field_ref[t, :tall, :128]
        mean = jnp.sum(jnp.where(zero, sums * scale, 0.0), axis=1, keepdims=True)
        mean_ref[0] = jnp.broadcast_to(mean, (tall, cols))
        for t in range(levels):
            field_ref[t, :tall] = field_ref[t, :tall] - mean * ones_ref[t : t + 1]

    left = jnp.zeros(field_ref.shape[1:], jnp.float32)
    right = left
    for t in range(half):
        factor = factor_ref[t]
        left = (field_ref[t] + left) * factor
        right = (field_ref[levels - 1 - t] + right) * factor
        if t < half - 1:
            field_ref[t] = left
            field_ref[levels - 1 - t] = right
    first = (left + factor * right) * factor_ref[half]
    right = right + factor * first
    left = first
    field_ref[half - 1] = left
    field_ref[half] = right
    for t in range(half - 2, -1, -1):
        factor = factor_ref[t]
        left = field_ref[t] + factor * left
        right = field_ref[levels - 1 - t] + factor * right
        field_ref[t] = left
        field_ref[levels - 1 - t] = right

    def backward(i, carry):
        here_rows = slice(i % stack * few, (i % stack + 1) * few)
        field = field_ref[pl.ds(i * here, here)].reshape(here * high, cols)
        values = one_product(long_data(field, 3, 1), back_ref[...], DIRECT)
        main, first = [], []
        for q in range(count):
            part = [values[t * high + q * tall : t * high + (q + 1) * tall] for t in range(here)]
            rim = jnp.where(lane == offset("next", here), mean_ref[q], 0.0)
            for t in range(here):
                at = offset("next", t)
                rim = jnp.where(lane == at, shift(part[t], at - rows), rim)
                if t > 0:
                    at = offset("row", t)
                    rim = jnp.where(lane == at, shift(part[t], at), rim)
            rim = jnp.where(even, rim, shift(rim, rows // 2))
            rim = rim + pltpu.roll(rim, tall - few, 0)
            rim_ref[i // stack, 2 * q, 0, here_rows] = rim[:few]
            rim_ref[i // stack, 2 * q + 1, 0, here_rows] = rim[tall // 2 : tall // 2 + few]
            main.append(jnp.where(low, part[0], swap(carry[q])))
            main.append(jnp.where(low, swap(part[0]), carry[q]))
            first.append(part[0])
        for g in range(row_blocks // pieces):
            cut = slice(g * lanes, (g + 1) * lanes)
            for j, value in enumerate(exchange_pieces([a[:, cut] for a in main], rows)):
                out_ref[g * pieces + j, i, : kinds - 1] = value.reshape(kinds - 1, few, lanes)
        return tuple(first)

    carry = (blank,) * count
    for i in range(time_blocks - 1, -1, -1):
        carry = backward(i, carry)
    for h in range(time_blocks // stack):
        times = slice(h * stack, (h + 1) * stack)
        for g in range(row_blocks // pieces):
            cut = slice(g * lanes, (g + 1) * lanes)
            rims = exchange_pieces([rim_ref[h, j, 0, :, cut] for j in range(pieces)], rows)
            for j, value in enumerate(rims):
                out_ref[g * pieces + j, times, kinds - 1] = value.reshape(stack, few, lanes)


def step_kernel(
    levels,
    pair,
    mult_in,
    edge_ref,
    inner_ref,
    hart_ref,
    links_ref,
    inverse_ref,
    basis_ref,
    mult_hbm,
    aux_hbm,
    mult_ref,
    mult_out,
    aux_out,
    sems,
):
    _, here, batch, rows, cols = mult_ref.shape
    lanes = here * pair * rows
    pieces = lanes // rows
    kinds = edge_ref.shape[2]
    total_pairs = batch // pair
    first = lax.axis_index("py") * here
    last = (first + here == levels).astype(jnp.int32)
    inside = 1.0 - last.astype(jnp.float32)
    outs = []
    fetches = []
    for q in range(total_pairs):
        cut = pl.ds(q * pair, pair)
        fetches.append(
            pltpu.make_async_copy(mult_in.at[:, :, cut], mult_ref.at[:, :, cut], sems.at[2, q])
        )
        fetches[q].start()
    for part in range(STEP_PARTS):
        mine = range(part * total_pairs // STEP_PARTS, (part + 1) * total_pairs // STEP_PARTS)
        edges = []
        for q in mine:
            blocks = [edge_ref[:, q, k].reshape(cols // pieces, lanes) for k in range(kinds)]
            blocks += [jnp.zeros((cols // pieces, lanes), jnp.float32)] * (pieces - kinds)
            edges.append(jnp.concatenate(exchange_pieces(blocks, rows), axis=0))
        linked = [wide_product(edge, links_ref[last], 3) for edge in edges]
        gone = [(inner_ref[q] + link) * inverse_ref[last] for q, link in zip(mine, linked)]
        nodes = [wide_product(value, basis_ref[last], 3) for value in gone]
        whole = [
            jnp.concatenate(both, axis=1).T[: lanes + kinds * rows] for both in zip(nodes, edges)
        ]
        potential = [one_product(long_data(value, 3, 1), hart_ref[...], DIRECT) for value in whole]
        for q, values in zip(mine, potential):
            fetches[q].wait()
            step_part(q, pair, values, inside, mult_ref, mult_out, aux_out)
            cut = pl.ds(q * pair, pair)
            for n, (one, other) in enumerate(((mult_out, mult_hbm), (aux_out, aux_hbm))):
                copy = pltpu.make_async_copy(one.at[:, :, cut], other.at[:, :, cut], sems.at[n, q])
                copy.start()
                outs.append(copy)
    for copy in outs:
        copy.wait()


def step_part(q, pair, values, inside, mult_ref, mult_out, aux_out):
    _, here, _, rows, cols = mult_ref.shape
    lanes = here * pair * rows
    full = (pair, rows, cols)
    row_index = lax.broadcasted_iota(jnp.int32, full, 1)
    at = slice(q * pair, (q + 1) * pair)

    def level(start):
        return values[start : start + pair * rows].reshape(full)

    def rims(kind, t):
        starts = [lanes + slots(here, rows, b, kind, t) for b in range(pair)]
        rim = [jnp.broadcast_to(values[start : start + 1], (rows, cols)) for start in starts]
        return jnp.concatenate(rim, axis=0).reshape(full)

    phi = [level(lanes)]
    for t in range(1, here):
        phi.append(jnp.where(row_index == 0, rims("row", t), level(t * pair * rows)))
    phi.append(level(lanes + pair * rows))
    for t0 in range(0, here, 1):
        times = range(t0, t0 + 1)
        mine = jnp.concatenate([phi[t] for t in times], axis=0)
        rate = jnp.concatenate([phi[t + 1] for t in times], axis=0) - mine
        if times[-1] == here - 1:
            kept = [rate[: (1 - 1) * pair]] if 1 > 1 else []
            rate = jnp.concatenate(kept + [rate[(1 - 1) * pair :] * inside], axis=0)
        rim = jnp.concatenate([rims("next", t) for t in times], axis=0)
        index = lax.broadcasted_iota(jnp.int32, mine.shape, 1)
        below = jnp.where(index == rows - 1, rim, pltpu.roll(mine, rows - 1, 1))
        gradient = (rate, below - mine, pltpu.roll(mine, cols - 1, 2) - mine)
        target = [
            gradient[c] + jnp.concatenate([mult_ref[c, t, at] for t in times], axis=0)
            for c in range(3)
        ]
        time_part, one, two = target
        kinetic = 0.5 * (one * one + two * two)
        center = 1.0 + time_part
        scaling = jnp.maximum(center, 1.0) + jnp.exp(jnp.log(kinetic) * (1.0 / 3.0))
        for _ in range(NEWTON):
            linear = scaling * (scaling - center)
            residue = scaling * linear - kinetic
            derivative = scaling * scaling + (linear + linear)
            change = residue * pl.reciprocal(derivative, approx=True)
            scaling = jnp.maximum(scaling - change, 1.0)
        scaling = jnp.where(time_part + kinetic <= 0.0, 1.0, scaling)
        shrink = pl.reciprocal(scaling, approx=True)
        shrink = shrink * (2.0 - scaling * shrink)
        shrink = shrink * (2.0 - scaling * shrink)
        moved = scaling - 1.0
        fresh = (time_part - moved, one * shrink, two * shrink)
        for c, past in enumerate((moved, one - fresh[1], two - fresh[2])):
            for n, t in enumerate(times):
                part = slice(n * pair, (n + 1) * pair)
                aux_out[c, t, at] = fresh[c][part]
                mult_out[c, t, at] = past[part]


def params(size=48):
    return pltpu.CompilerParams(vmem_limit_bytes=size * 1024 * 1024)


def local(multiplier, auxiliary, density_start, density_end):
    _, here, batch, rows, cols = multiplier.shape
    time_blocks = lax.axis_size("py")
    row_blocks = lax.axis_size("grp") * lax.axis_size("px")
    levels = here * time_blocks
    row_count = rows * row_blocks
    pair = batch // time_blocks
    lanes = here * pair * rows
    pieces = lanes // rows
    kinds = 2 * pair + 1
    few = cols // (pieces * row_blocks)
    both = [interior_tables(here, rows, cols, last) for last in (False, True)]
    hart_there = long_table(hartley_table(cols), 2, 1)
    hart_back = long_table(hartley_table(cols), 3, 0)
    rows_there = long_table(hartley_table(row_count), 2, 0)
    rows_back = long_table(hartley_table(row_count), 3, 0)
    basis2 = np.stack([wide_table(one[0], 2) for one in both])
    basis3 = np.stack([wide_table(one[0].T, 3) for one in both])
    inverse = np.stack([one[1] for one in both]).astype(np.float32)
    to_edges = np.stack([wide_table(one[2], 2) for one in both])
    from_edges = np.stack([wide_table(one[3], 3) for one in both])
    ones = constant_source(here, rows, time_blocks, row_blocks, both).astype(np.float32)
    factors = elimination_table(levels, row_count, cols, row_blocks, pieces, pair)

    away = pl.BlockSpec(memory_space=pltpu.HBM)
    vmem = pl.BlockSpec(memory_space=pltpu.VMEM)
    chunked = jax.ShapeDtypeStruct((row_blocks, time_blocks, kinds, few, lanes), jnp.float32)
    inner_shape = (time_blocks, cols, lanes)
    edges, inner = pl.pallas_call(
        functools.partial(source_kernel, levels, pair),
        in_specs=[away] * 8,
        out_specs=[away] * 2,
        out_shape=[chunked, jax.ShapeDtypeStruct(inner_shape, jnp.float32)],
        scratch_shapes=[
            pltpu.VMEM(multiplier.shape, jnp.float32),
            pltpu.VMEM(auxiliary.shape, jnp.float32),
            pltpu.VMEM((2,) + density_start.shape, jnp.float32),
            pltpu.VMEM(hart_there.shape, jnp.bfloat16),
            pltpu.VMEM(basis2.shape[1:], jnp.bfloat16),
            pltpu.VMEM(inverse.shape[1:], jnp.float32),
            pltpu.VMEM(to_edges.shape[1:], jnp.bfloat16),
            pltpu.VMEM(chunked.shape, jnp.float32),
            pltpu.VMEM(inner_shape, jnp.float32),
            pltpu.SemaphoreType.DMA((2, PARTS)),
            pltpu.SemaphoreType.DMA((6,)),
            pltpu.SemaphoreType.DMA((2, PARTS)),
        ],
        compiler_params=params(56),
        name="source",
    )(multiplier, auxiliary, density_start, density_end, hart_there, basis2, inverse, to_edges)

    def spread(value):
        flat = value.reshape((row_blocks * time_blocks,) + value.shape[2:])
        return lax.all_to_all(flat, EVERY, 0, 0, tiled=True).reshape(value.shape)

    solved = pl.pallas_call(
        solve_kernel,
        in_specs=[vmem, vmem, vmem, vmem, pl.BlockSpec(memory_space=pl.ANY)],
        out_specs=vmem,
        out_shape=chunked,
        scratch_shapes=[
            pltpu.VMEM((levels, pair * pieces * few, row_count), jnp.float32),
            pltpu.VMEM((pieces // 2, 2 * pair * few, row_count), jnp.float32),
            pltpu.VMEM(factors.shape[1:], jnp.float32),
            pltpu.VMEM((time_blocks // (2 * pair), pieces, 2, 2 * pair * few, row_count), jnp.float32),
            pltpu.SemaphoreType.DMA,
        ],
        compiler_params=params(),
        name="solve",
    )(spread(edges), rows_there, rows_back, ones, factors)

    result = jax.ShapeDtypeStruct(multiplier.shape, jnp.float32)
    mult_next, aux_next = pl.pallas_call(
        functools.partial(step_kernel, levels, pair),
        in_specs=[away] + [vmem] * 6,
        out_specs=[away] * 2,
        scratch_shapes=[
            pltpu.VMEM(multiplier.shape, jnp.float32),
            pltpu.VMEM(multiplier.shape, jnp.float32),
            pltpu.VMEM(multiplier.shape, jnp.float32),
            pltpu.SemaphoreType.DMA((3, time_blocks)),
        ],
        out_shape=[result, result],
        compiler_params=params(),
        name="step",
    )(multiplier, spread(solved), inner, hart_back, from_edges, inverse, basis3)
    return mult_next, aux_next


def solution(mesh):
    field = P(None, "py", None, ROWS, None)
    density = P(None, ROWS, None)
    return jax.shard_map(
        local,
        mesh=mesh,
        in_specs=(field, field, density, density),
        out_specs=(field, field),
        check_vma=False,
    )
```

```python
import functools

import jax
import jax.numpy as jnp
import numpy as np
from jax import lax
from jax.experimental import pallas as pl
from jax.experimental.pallas import tpu as pltpu
from jax.sharding import PartitionSpec as P

NEWTON = 4
ROWS = ("grp", "px")
EVERY = ("px", "grp", "py")
PARTS = 2
FETCHES = 4
STEP_PARTS = 2
VMEM_BYTES = 48 * 1024 * 1024
DIRECT = ((1,), (0,))
CROSS = ((1,), (1,))


def table_parts(table, count):
    rest = np.asarray(table, np.float32)
    parts = []
    for _ in range(count):
        parts.append(rest.astype(jnp.bfloat16))
        rest = rest - parts[-1].astype(np.float32)
    return np.stack(parts)


def parts_of(value, count):
    parts = [value.astype(jnp.bfloat16)]
    for _ in range(count - 1):
        value = value - parts[-1].astype(jnp.float32)
        parts.append(value.astype(jnp.bfloat16))
    return parts


def orders(count):
    return [(i, order - i) for order in range(count - 1, -1, -1) for i in range(order + 1)]


def long_table(table, count, axis):
    parts = table_parts(table, count)
    return np.concatenate([parts[j] for _, j in orders(count)], axis=axis)


def long_data(value, count, axis):
    parts = parts_of(value, count)
    return jnp.concatenate([parts[i] for i, _ in orders(count)], axis=axis)


def wide_table(table, count):
    parts = table_parts(table, count)
    none = np.zeros_like(parts[0])
    if count == 2:
        grid = [(0, 1), (0, None)]
    else:
        grid = [(0, 1), (0, 1), (2, None), (0, None)]
    return np.block([[none if k is None else parts[k] for k in row] for row in grid])


def wide_product(value, table, count):
    parts = parts_of(value, count)
    data = parts if count == 2 else [parts[0], parts[1], parts[0], parts[2]]
    both = one_product(jnp.concatenate(data, axis=1), table, DIRECT)
    half = both.shape[1] // 2
    return both[:, :half] + both[:, half:]


def one_product(left, right, dims):
    return lax.dot_general(left, right, (dims, ((), ())), preferred_element_type=jnp.float32)


def squared_sines(length, period):
    return 4.0 * np.sin(np.pi * np.arange(length) / period) ** 2


def hartley_table(length):
    index = np.arange(length)
    angles = (index[:, None] * index[None, :] % length) * (2.0 * np.pi / length)
    return (np.cos(angles) + np.sin(angles)) / np.sqrt(length)


def elimination_table(levels, row_count, col_count, blocks, pieces, pair):
    eigen = squared_sines(col_count, col_count)[:, None] + squared_sines(row_count, row_count)
    factors = [1.0 / (1.0 + eigen)]
    for _ in range(levels // 2 - 1):
        factors.append(1.0 / (2.0 + eigen - factors[-1]))
    gap = 1.0 - factors[-1] ** 2
    middle = np.where(eigen > 0.0, 1.0 / np.where(eigen > 0.0, gap, 1.0), 0.0)
    table = np.stack(factors + [middle]).astype(np.float32)
    table = table.reshape(levels // 2 + 1, pieces, blocks, 1, -1, row_count).transpose(2, 0, 1, 3, 4, 5)
    table = np.broadcast_to(table, table.shape[:3] + (pair,) + table.shape[4:])
    return np.ascontiguousarray(table).reshape(blocks, levels // 2 + 1, -1, row_count)


def slots(here, rows, b, kind, index):
    if kind == "level":
        return b * rows + index
    if kind == "later":
        return (2 + b) * rows + index
    base = 4 * rows + b * (rows // 2)
    return base + (index - 1 if kind == "row" else here - 1 + index)


def interior_tables(here, rows, cols, last):
    pair = 2
    lanes = here * pair * rows
    inner = here - 1
    chain = 2.0 * np.eye(inner) - np.eye(inner, k=1) - np.eye(inner, k=-1)
    if last:
        chain[-1, -1] = 1.0
    time_values, time_basis = np.linalg.eigh(chain)
    row_index = np.arange(1, rows)
    row_basis = np.sqrt(2.0 / rows) * np.sin(np.pi * np.outer(row_index, row_index) / rows)
    row_values = squared_sines(rows, 2 * rows)
    col_values = squared_sines(cols, cols)
    basis = np.zeros((here, pair, rows, here, pair, rows))
    inverse = np.zeros((cols, here, pair, rows))
    linked = np.zeros((here, pair, rows, lanes))
    for b in range(pair):
        for k in range(1, here):
            for t in range(1, here):
                basis[t, b, 1:, k, b, 1:] = time_basis[t - 1, k - 1] * row_basis
            inverse[:, k, b, 1:] = 1.0 / (
                col_values[:, None] + time_values[k - 1] + row_values[None, 1:]
            )
        for x in range(1, rows):
            linked[1, b, x, slots(here, rows, b, "level", x)] = 1.0
            if not last:
                linked[here - 1, b, x, slots(here, rows, b, "later", x)] = 1.0
        for t in range(1, here):
            linked[t, b, 1, slots(here, rows, b, "row", t)] = 1.0
            linked[t, b, rows - 1, slots(here, rows, b, "next", t)] = 1.0
    basis = basis.reshape(lanes, lanes)
    linked = linked.reshape(lanes, lanes)
    inverse = inverse.reshape(cols, lanes)
    to_edges = basis.T @ linked
    from_edges = to_edges.T.copy()
    for b in range(pair):
        ones = np.zeros((here, pair, rows))
        ones[1:, b, 1:] = 1.0
        from_edges[slots(here, rows, b, "next", here)] = -(ones.reshape(-1) @ basis)
    return basis, inverse, to_edges, from_edges


def constant_source(here, rows, time_blocks, row_blocks, tables):
    levels, row_count = here * time_blocks, rows * row_blocks
    field = np.zeros((levels + 1, row_count))
    ones = np.zeros((here, 2, rows))
    ones[1:, 0, 1:] = 1.0
    for i in range(time_blocks):
        basis, inverse, to_edges, _ = tables[1 if i == time_blocks - 1 else 0]
        edge = ((ones.reshape(-1) @ basis) * inverse[0]) @ to_edges
        for j in range(row_blocks):
            t0, x0 = i * here, j * rows
            for x in range(rows):
                field[t0, x0 + x] += 1.0 + edge[slots(here, rows, 0, "level", x)]
                field[t0 + here, x0 + x] += edge[slots(here, rows, 0, "later", x)]
            for t in range(here):
                after = (x0 + rows) % row_count
                field[t0 + t, after] += edge[slots(here, rows, 0, "next", t)]
                if t > 0:
                    field[t0 + t, x0] += 1.0 + edge[slots(here, rows, 0, "row", t)]
    return field[:levels] @ hartley_table(row_count)


def exchange_pieces(blocks, width):
    count = len(blocks)
    lanes = count * width
    group = lax.broadcasted_iota(jnp.int32, blocks[0].shape, 1) // width
    step = 1
    while step < count:
        upper = (group // step) % 2 == 1
        fresh = list(blocks)
        for j in range(count):
            if (j // step) % 2 == 0:
                low, high = blocks[j], blocks[j + step]
                fresh[j] = jnp.where(upper, pltpu.roll(high, step * width, 1), low)
                fresh[j + step] = jnp.where(upper, high, pltpu.roll(low, lanes - step * width, 1))
        blocks = fresh
        step *= 2
    return blocks


def source_kernel(
    levels,
    pair,
    mult_hbm,
    aux_hbm,
    start_hbm,
    end_hbm,
    hart_hbm,
    basis_hbm,
    inverse_hbm,
    edges_hbm,
    out_hbm,
    inner_hbm,
    mult_ref,
    aux_ref,
    density_ref,
    hart_ref,
    basis_ref,
    inverse_ref,
    edges_ref,
    out_ref,
    inner_ref,
    field_sems,
    table_sems,
    out_sems,
):
    _, here, batch, rows, cols = mult_ref.shape
    lanes = here * pair * rows
    pieces = lanes // rows
    each = cols // pieces
    total_pairs = batch // pair
    first = lax.axis_index("py") * here
    at_start = first == 0
    at_end = first + here == levels
    last = at_end.astype(jnp.int32)
    fields = []
    for part in range(FETCHES):
        cut = pl.ds(part * batch // FETCHES, batch // FETCHES)
        fields.append(
            [
                pltpu.make_async_copy(
                    one.at[:, :, cut], other.at[:, :, cut], field_sems.at[n, part]
                )
                for n, (one, other) in enumerate(((mult_hbm, mult_ref), (aux_hbm, aux_ref)))
            ]
        )
    tables = [
        pltpu.make_async_copy(hart_hbm, hart_ref, table_sems.at[0]),
        pltpu.make_async_copy(basis_hbm.at[last], basis_ref, table_sems.at[1]),
        pltpu.make_async_copy(inverse_hbm.at[last], inverse_ref, table_sems.at[2]),
        pltpu.make_async_copy(edges_hbm.at[last], edges_ref, table_sems.at[3]),
    ]
    start_copy = pltpu.make_async_copy(start_hbm, density_ref.at[0], table_sems.at[4])
    end_copy = pltpu.make_async_copy(end_hbm, density_ref.at[1], table_sems.at[5])
    for copy in fields[0] + [start_copy, end_copy] + fields[1] + tables + sum(fields[2:], []):
        copy.start()

    row_index = lax.broadcasted_iota(jnp.int32, (rows, cols), 0)
    first_row = row_index == 0
    outs = []
    for part in range(PARTS):
        mine = range(part * total_pairs // PARTS, (part + 1) * total_pairs // PARTS)
        field = []
        for q in mine:
            if q * FETCHES % total_pairs == 0:
                for copy in fields[q * FETCHES // total_pairs]:
                    copy.wait()
            if q == 0:
                start_copy.wait()
                end_copy.wait()
            blocks = []
            earlier = [0.0] * pair
            rims = jnp.zeros((rows, cols), jnp.float32)
            for t in range(here):
                for b in range(pair):
                    at = q * pair + b
                    time = aux_ref[0, t, at] - mult_ref[0, t, at]
                    if t == here - 1:
                        time = jnp.where(at_end, 0.0, time)
                    along = aux_ref[1, t, at] - mult_ref[1, t, at]
                    second = aux_ref[2, t, at] - mult_ref[2, t, at]
                    beside = jnp.where(first_row, 0.0, pltpu.roll(along, 1, 0))
                    total = (earlier[b] - time) + (beside - along)
                    total = total + (pltpu.roll(second, 1, 1) - second)
                    if t == 0:
                        total = total - jnp.where(at_start, density_ref[0, at], 0.0)
                    if t == here - 1:
                        total = total + jnp.where(at_end, density_ref[1, at], 0.0)
                    earlier[b] = time
                    blocks.append(total)
                    base = b * (rows // 2)
                    if t > 0:
                        rims = jnp.where(row_index == base + t - 1, total[:1], rims)
                    rims = jnp.where(row_index == base + here - 1 + t, along[rows - 1 :], rims)
            spare = jnp.zeros((lanes - (2 * pair + 1) * rows, cols), jnp.float32)
            nodes = jnp.concatenate(blocks + blocks[:pair] + earlier + [rims, spare], axis=0)
            field.append(long_data(nodes, 2, 1))
        if part == 0:
            for copy in tables:
                copy.wait()
        modes = [one_product(hart_ref[...], nodes, CROSS) for nodes in field]
        inner = [wide_product(mode[:, :lanes], basis_ref[...], 2) for mode in modes]
        gone = [wide_product(value * inverse_ref[...], edges_ref[...], 2) for value in inner]
        for n, q in enumerate(mine):
            inner_ref[q] = inner[n]
            edges = modes[n][:, lanes:] + gone[n]
            blocks = exchange_pieces(
                [edges[j * each : (j + 1) * each] for j in range(pieces)], rows
            )
            for k in range(out_ref.shape[2]):
                out_ref[:, q, k] = blocks[k].reshape(out_ref.shape[0], out_ref.shape[3], lanes)
        cut = pl.ds(mine[0], len(mine))
        outs += [
            pltpu.make_async_copy(out_ref.at[:, cut], out_hbm.at[:, cut], out_sems.at[0, part]),
            pltpu.make_async_copy(inner_ref.at[cut], inner_hbm.at[cut], out_sems.at[1, part]),
        ]
        for copy in outs[-2:]:
            copy.start()
    for copy in outs:
        copy.wait()


def solve_kernel(
    groups, in_ref, hart_ref, back_ref, ones_ref, table_ref, out_ref, field_ref, mean_ref, factor_ref, rim_ref, sem
):
    row_blocks, time_blocks, kinds, few, lanes = in_ref.shape
    levels, high, cols = field_ref.shape
    here = levels // time_blocks
    rows = cols // row_blocks
    pieces = lanes // rows
    tall = (kinds - 1) * few
    count = high // tall
    half = levels // 2
    mine = lax.axis_index("px") * lax.axis_size("grp") + lax.axis_index("grp")
    fetch = pltpu.make_async_copy(table_ref.at[mine], factor_ref, sem)
    fetch.start()
    stack = tall // few
    lane = lax.broadcasted_iota(jnp.int32, (tall, cols), 1) % rows
    row = lax.broadcasted_iota(jnp.int32, (tall, cols), 0)
    low = row < tall // 2
    even = (row // few) % 2 == 0

    def shift(value, steps):
        return pltpu.roll(value, steps % cols, 1)

    def swap(value):
        return pltpu.roll(value, tall // 2, 0)

    def offset(kind, t):
        return slots(here, rows, 0, kind, t) - 4 * rows

    def place(g, j):
        block = g * pieces + j
        return block % (row_blocks // groups) * groups + block // (row_blocks // groups)

    def exchange(get):
        halves = [
            exchange_pieces([get(place(g, j)) for j in range(pieces)], rows)
            for g in range(row_blocks // pieces)
        ]
        return [jnp.concatenate([one[k] for one in halves], axis=1) for k in range(pieces)]

    for h in range(time_blocks // stack):
        times = slice(h * stack, (h + 1) * stack)
        for j, rim in enumerate(exchange(lambda x: in_ref[x, times, kinds - 1].reshape(tall, lanes))):
            rim_ref[h, j, 0] = rim
            rim_ref[h, j, 1] = shift(rim, -(rows // 2))

    def forward(i, carry):
        main = exchange(lambda x: in_ref[x, i, : kinds - 1].reshape(tall, lanes))
        here_rows = slice(i % stack * few, (i % stack + 1) * few)
        field = [[] for _ in range(here)]
        later = []
        for q in range(count):
            one, two = main[2 * q], main[2 * q + 1]
            level = jnp.where(low, one, swap(two)) + carry[q]
            later.append(jnp.where(low, swap(one), two))
            rim = jnp.concatenate(
                [rim_ref[i // stack, 2 * q + j, b, here_rows] for j in range(2) for b in range(2)],
                axis=0,
            )
            for t in range(here):
                value = shift(rim, rows - offset("next", t))
                if t > 0:
                    value = value + shift(rim, -offset("row", t))
                value = jnp.where(lane == 0, value, 0.0)
                field[t].append(value + level if t == 0 else value)
        field = jnp.concatenate(sum(field, []), axis=0)
        modes = one_product(long_data(field, 2, 1), hart_ref[...], DIRECT)
        field_ref[pl.ds(i * here, here)] = modes.reshape(here, high, cols)
        return tuple(later)

    blank = jnp.zeros((tall, cols), jnp.float32)
    carry = (blank,) * count
    for i in range(time_blocks):
        carry = forward(i, carry)
    fetch.wait()

    mean_ref[...] = jnp.zeros(mean_ref.shape, jnp.float32)

    @pl.when(mine == 0)
    def _():
        shape = (tall, 128)
        spot = lax.broadcasted_iota(jnp.int32, shape, 0)
        zero = (spot % few == 0) & (spot < tall // 2)
        zero = zero & (lax.broadcasted_iota(jnp.int32, shape, 1) == 0)
        scale = float(np.sqrt(cols)) / (levels * cols)
        sums = field_ref[0, :tall, :128]
        for t in range(1, levels):
            sums = sums + field_ref[t, :tall, :128]
        mean = jnp.sum(jnp.where(zero, sums * scale, 0.0), axis=1, keepdims=True)
        mean_ref[0] = jnp.broadcast_to(mean, (tall, cols))
        for t in range(levels):
            field_ref[t, :tall] = field_ref[t, :tall] - mean * ones_ref[t : t + 1]

    left = jnp.zeros(field_ref.shape[1:], jnp.float32)
    right = left
    for t in range(half):
        factor = factor_ref[t]
        left = (field_ref[t] + left) * factor
        right = (field_ref[levels - 1 - t] + right) * factor
        if t < half - 1:
            field_ref[t] = left
            field_ref[levels - 1 - t] = right
    first = (left + factor * right) * factor_ref[half]
    right = right + factor * first
    left = first
    field_ref[half - 1] = left
    field_ref[half] = right
    for t in range(half - 2, -1, -1):
        factor = factor_ref[t]
        left = field_ref[t] + factor * left
        right = field_ref[levels - 1 - t] + factor * right
        field_ref[t] = left
        field_ref[levels - 1 - t] = right

    def backward(i, carry):
        here_rows = slice(i % stack * few, (i % stack + 1) * few)
        field = field_ref[pl.ds(i * here, here)].reshape(here * high, cols)
        values = one_product(long_data(field, 3, 1), back_ref[...], DIRECT)
        main, first = [], []
        for q in range(count):
            part = [values[t * high + q * tall : t * high + (q + 1) * tall] for t in range(here)]
            rim = jnp.where(lane == offset("next", here), mean_ref[q], 0.0)
            for t in range(here):
                at = offset("next", t)
                rim = jnp.where(lane == at, shift(part[t], at - rows), rim)
                if t > 0:
                    at = offset("row", t)
                    rim = jnp.where(lane == at, shift(part[t], at), rim)
            rim = jnp.where(even, rim, shift(rim, rows // 2))
            rim = rim + pltpu.roll(rim, tall - few, 0)
            rim_ref[i // stack, 2 * q, 0, here_rows] = rim[:few]
            rim_ref[i // stack, 2 * q + 1, 0, here_rows] = rim[tall // 2 : tall // 2 + few]
            main.append(jnp.where(low, part[0], swap(carry[q])))
            main.append(jnp.where(low, swap(part[0]), carry[q]))
            first.append(part[0])
        for g in range(row_blocks // pieces):
            cut = slice(g * lanes, (g + 1) * lanes)
            for j, value in enumerate(exchange_pieces([a[:, cut] for a in main], rows)):
                out_ref[place(g, j), i, : kinds - 1] = value.reshape(kinds - 1, few, lanes)
        return tuple(first)

    carry = (blank,) * count
    for i in range(time_blocks - 1, -1, -1):
        carry = backward(i, carry)
    for h in range(time_blocks // stack):
        times = slice(h * stack, (h + 1) * stack)
        for g in range(row_blocks // pieces):
            cut = slice(g * lanes, (g + 1) * lanes)
            rims = exchange_pieces([rim_ref[h, j, 0, :, cut] for j in range(pieces)], rows)
            for j, value in enumerate(rims):
                out_ref[place(g, j), times, kinds - 1] = value.reshape(stack, few, lanes)


def step_kernel(
    levels,
    pair,
    mult_in,
    edge_ref,
    inner_ref,
    hart_ref,
    links_ref,
    inverse_ref,
    basis_ref,
    mult_hbm,
    aux_hbm,
    mult_ref,
    mult_out,
    aux_out,
    sems,
):
    _, here, batch, rows, cols = mult_ref.shape
    lanes = here * pair * rows
    pieces = lanes // rows
    kinds = edge_ref.shape[2]
    total_pairs = batch // pair
    first = lax.axis_index("py") * here
    last = (first + here == levels).astype(jnp.int32)
    inside = 1.0 - last.astype(jnp.float32)
    outs = []
    fetches = []
    for q in range(total_pairs):
        cut = pl.ds(q * pair, pair)
        fetches.append(
            pltpu.make_async_copy(mult_in.at[:, :, cut], mult_ref.at[:, :, cut], sems.at[2, q])
        )
        fetches[q].start()
    for part in range(STEP_PARTS):
        mine = range(part * total_pairs // STEP_PARTS, (part + 1) * total_pairs // STEP_PARTS)
        edges = []
        for q in mine:
            blocks = [edge_ref[:, q, k].reshape(cols // pieces, lanes) for k in range(kinds)]
            blocks += [jnp.zeros((cols // pieces, lanes), jnp.float32)] * (pieces - kinds)
            edges.append(jnp.concatenate(exchange_pieces(blocks, rows), axis=0))
        linked = [wide_product(edge, links_ref[last], 3) for edge in edges]
        gone = [(inner_ref[q] + link) * inverse_ref[last] for q, link in zip(mine, linked)]
        nodes = [wide_product(value, basis_ref[last], 3) for value in gone]
        whole = [
            jnp.concatenate(both, axis=1).T[: lanes + kinds * rows] for both in zip(nodes, edges)
        ]
        potential = [one_product(long_data(value, 3, 1), hart_ref[...], DIRECT) for value in whole]
        for q, values in zip(mine, potential):
            fetches[q].wait()
            step_part(q, pair, values, inside, mult_ref, mult_out, aux_out)
            cut = pl.ds(q * pair, pair)
            for n, (one, other) in enumerate(((mult_out, mult_hbm), (aux_out, aux_hbm))):
                copy = pltpu.make_async_copy(one.at[:, :, cut], other.at[:, :, cut], sems.at[n, q])
                copy.start()
                outs.append(copy)
    for copy in outs:
        copy.wait()


def step_part(q, pair, values, inside, mult_ref, mult_out, aux_out):
    _, here, _, rows, cols = mult_ref.shape
    lanes = here * pair * rows
    full = (pair, rows, cols)
    row_index = lax.broadcasted_iota(jnp.int32, full, 1)
    at = slice(q * pair, (q + 1) * pair)

    def level(start):
        return values[start : start + pair * rows].reshape(full)

    def rims(kind, t):
        starts = [lanes + slots(here, rows, b, kind, t) for b in range(pair)]
        rim = [jnp.broadcast_to(values[start : start + 1], (rows, cols)) for start in starts]
        return jnp.concatenate(rim, axis=0).reshape(full)

    phi = [level(lanes)]
    for t in range(1, here):
        phi.append(jnp.where(row_index == 0, rims("row", t), level(t * pair * rows)))
    phi.append(level(lanes + pair * rows))
    for t0 in range(0, here, 1):
        times = range(t0, t0 + 1)
        mine = jnp.concatenate([phi[t] for t in times], axis=0)
        rate = jnp.concatenate([phi[t + 1] for t in times], axis=0) - mine
        if times[-1] == here - 1:
            kept = [rate[: (1 - 1) * pair]] if 1 > 1 else []
            rate = jnp.concatenate(kept + [rate[(1 - 1) * pair :] * inside], axis=0)
        rim = jnp.concatenate([rims("next", t) for t in times], axis=0)
        index = lax.broadcasted_iota(jnp.int32, mine.shape, 1)
        below = jnp.where(index == rows - 1, rim, pltpu.roll(mine, rows - 1, 1))
        gradient = (rate, below - mine, pltpu.roll(mine, cols - 1, 2) - mine)
        target = [
            gradient[c] + jnp.concatenate([mult_ref[c, t, at] for t in times], axis=0)
            for c in range(3)
        ]
        time_part, one, two = target
        kinetic = 0.5 * (one * one + two * two)
        center = 1.0 + time_part
        scaling = jnp.maximum(center, 1.0) + jnp.exp(jnp.log(kinetic) * (1.0 / 3.0))
        for _ in range(NEWTON):
            linear = scaling * (scaling - center)
            residue = scaling * linear - kinetic
            derivative = scaling * scaling + (linear + linear)
            change = residue * pl.reciprocal(derivative, approx=True)
            scaling = jnp.maximum(scaling - change, 1.0)
        scaling = jnp.where(time_part + kinetic <= 0.0, 1.0, scaling)
        shrink = pl.reciprocal(scaling, approx=True)
        shrink = shrink * (2.0 - scaling * shrink)
        shrink = shrink * (2.0 - scaling * shrink)
        moved = scaling - 1.0
        fresh = (time_part - moved, one * shrink, two * shrink)
        for c, past in enumerate((moved, one - fresh[1], two - fresh[2])):
            for n, t in enumerate(times):
                part = slice(n * pair, (n + 1) * pair)
                aux_out[c, t, at] = fresh[c][part]
                mult_out[c, t, at] = past[part]


def params(size=48):
    return pltpu.CompilerParams(vmem_limit_bytes=size * 1024 * 1024)


def local(multiplier, auxiliary, density_start, density_end):
    _, here, batch, rows, cols = multiplier.shape
    time_blocks = lax.axis_size("py")
    row_blocks = lax.axis_size("grp") * lax.axis_size("px")
    levels = here * time_blocks
    row_count = rows * row_blocks
    pair = batch // time_blocks
    lanes = here * pair * rows
    pieces = lanes // rows
    kinds = 2 * pair + 1
    few = cols // (pieces * row_blocks)
    both = [interior_tables(here, rows, cols, last) for last in (False, True)]
    hart_there = long_table(hartley_table(cols), 2, 1)
    hart_back = long_table(hartley_table(cols), 3, 0)
    rows_there = long_table(hartley_table(row_count), 2, 0)
    rows_back = long_table(hartley_table(row_count), 3, 0)
    basis2 = np.stack([wide_table(one[0], 2) for one in both])
    basis3 = np.stack([wide_table(one[0].T, 3) for one in both])
    inverse = np.stack([one[1] for one in both]).astype(np.float32)
    to_edges = np.stack([wide_table(one[2], 2) for one in both])
    from_edges = np.stack([wide_table(one[3], 3) for one in both])
    ones = constant_source(here, rows, time_blocks, row_blocks, both).astype(np.float32)
    factors = elimination_table(levels, row_count, cols, row_blocks, pieces, pair)

    away = pl.BlockSpec(memory_space=pltpu.HBM)
    vmem = pl.BlockSpec(memory_space=pltpu.VMEM)
    chunked = jax.ShapeDtypeStruct((row_blocks, time_blocks, kinds, few, lanes), jnp.float32)
    inner_shape = (time_blocks, cols, lanes)
    edges, inner = pl.pallas_call(
        functools.partial(source_kernel, levels, pair),
        in_specs=[away] * 8,
        out_specs=[away] * 2,
        out_shape=[chunked, jax.ShapeDtypeStruct(inner_shape, jnp.float32)],
        scratch_shapes=[
            pltpu.VMEM(multiplier.shape, jnp.float32),
            pltpu.VMEM(auxiliary.shape, jnp.float32),
            pltpu.VMEM((2,) + density_start.shape, jnp.float32),
            pltpu.VMEM(hart_there.shape, jnp.bfloat16),
            pltpu.VMEM(basis2.shape[1:], jnp.bfloat16),
            pltpu.VMEM(inverse.shape[1:], jnp.float32),
            pltpu.VMEM(to_edges.shape[1:], jnp.bfloat16),
            pltpu.VMEM(chunked.shape, jnp.float32),
            pltpu.VMEM(inner_shape, jnp.float32),
            pltpu.SemaphoreType.DMA((2, FETCHES)),
            pltpu.SemaphoreType.DMA((6,)),
            pltpu.SemaphoreType.DMA((2, PARTS)),
        ],
        compiler_params=params(56),
        name="source",
    )(multiplier, auxiliary, density_start, density_end, hart_there, basis2, inverse, to_edges)

    def spread(value):
        flat = value.reshape((row_blocks * time_blocks,) + value.shape[2:])
        return lax.all_to_all(flat, EVERY, 0, 0, tiled=True).reshape(value.shape)

    solved = pl.pallas_call(
        functools.partial(solve_kernel, lax.axis_size("grp")),
        in_specs=[vmem, vmem, vmem, vmem, pl.BlockSpec(memory_space=pl.ANY)],
        out_specs=vmem,
        out_shape=chunked,
        scratch_shapes=[
            pltpu.VMEM((levels, pair * pieces * few, row_count), jnp.float32),
            pltpu.VMEM((pieces // 2, 2 * pair * few, row_count), jnp.float32),
            pltpu.VMEM(factors.shape[1:], jnp.float32),
            pltpu.VMEM((time_blocks // (2 * pair), pieces, 2, 2 * pair * few, row_count), jnp.float32),
            pltpu.SemaphoreType.DMA,
        ],
        compiler_params=params(),
        name="solve",
    )(spread(edges), rows_there, rows_back, ones, factors)

    result = jax.ShapeDtypeStruct(multiplier.shape, jnp.float32)
    mult_next, aux_next = pl.pallas_call(
        functools.partial(step_kernel, levels, pair),
        in_specs=[away] + [vmem] * 6,
        out_specs=[away] * 2,
        scratch_shapes=[
            pltpu.VMEM(multiplier.shape, jnp.float32),
            pltpu.VMEM(multiplier.shape, jnp.float32),
            pltpu.VMEM(multiplier.shape, jnp.float32),
            pltpu.SemaphoreType.DMA((3, time_blocks)),
        ],
        out_shape=[result, result],
        compiler_params=params(),
        name="step",
    )(multiplier, spread(solved), inner, hart_back, from_edges, inverse, basis3)
    return mult_next, aux_next


def solution(mesh):
    field = P(None, "py", None, ROWS, None)
    density = P(None, ROWS, None)
    return jax.shard_map(
        local,
        mesh=mesh,
        in_specs=(field, field, density, density),
        out_specs=(field, field),
        check_vma=False,
    )
```

```python
import functools

import jax
import jax.numpy as jnp
import numpy as np
from jax import lax
from jax.experimental import pallas as pl
from jax.experimental.pallas import tpu as pltpu
from jax.sharding import PartitionSpec as P

NEWTON = 4
ROWS = ("grp", "px")
EVERY = ("px", "grp", "py")
PARTS = 2
FETCHES = 4
STEP_PARTS = 2
VMEM_BYTES = 48 * 1024 * 1024
DIRECT = ((1,), (0,))
CROSS = ((1,), (1,))


def table_parts(table, count):
    rest = np.asarray(table, np.float32)
    parts = []
    for _ in range(count):
        parts.append(rest.astype(jnp.bfloat16))
        rest = rest - parts[-1].astype(np.float32)
    return np.stack(parts)


def parts_of(value, count):
    parts = [value.astype(jnp.bfloat16)]
    for _ in range(count - 1):
        value = value - parts[-1].astype(jnp.float32)
        parts.append(value.astype(jnp.bfloat16))
    return parts


def orders(count):
    return [(i, order - i) for order in range(count - 1, -1, -1) for i in range(order + 1)]


def long_table(table, count, axis):
    parts = table_parts(table, count)
    return np.concatenate([parts[j] for _, j in orders(count)], axis=axis)


def long_data(value, count, axis):
    parts = parts_of(value, count)
    return jnp.concatenate([parts[i] for i, _ in orders(count)], axis=axis)


def wide_table(table, count):
    parts = table_parts(table, count)
    none = np.zeros_like(parts[0])
    if count == 2:
        grid = [(0, 1), (0, None)]
    else:
        grid = [(0, 1), (0, 1), (2, None), (0, None)]
    return np.block([[none if k is None else parts[k] for k in row] for row in grid])


def wide_product(value, table, count):
    parts = parts_of(value, count)
    data = parts if count == 2 else [parts[0], parts[1], parts[0], parts[2]]
    both = one_product(jnp.concatenate(data, axis=1), table, DIRECT)
    half = both.shape[1] // 2
    return both[:, :half] + both[:, half:]


def one_product(left, right, dims):
    return lax.dot_general(left, right, (dims, ((), ())), preferred_element_type=jnp.float32)


def squared_sines(length, period):
    return 4.0 * np.sin(np.pi * np.arange(length) / period) ** 2


def hartley_table(length):
    index = np.arange(length)
    angles = (index[:, None] * index[None, :] % length) * (2.0 * np.pi / length)
    return (np.cos(angles) + np.sin(angles)) / np.sqrt(length)


def elimination_table(levels, row_count, col_count, blocks, pieces, pair):
    eigen = squared_sines(col_count, col_count)[:, None] + squared_sines(row_count, row_count)
    factors = [1.0 / (1.0 + eigen)]
    for _ in range(levels // 2 - 1):
        factors.append(1.0 / (2.0 + eigen - factors[-1]))
    gap = 1.0 - factors[-1] ** 2
    middle = np.where(eigen > 0.0, 1.0 / np.where(eigen > 0.0, gap, 1.0), 0.0)
    table = np.stack(factors + [middle]).astype(np.float32)
    table = table.reshape(levels // 2 + 1, pieces, blocks, 1, -1, row_count).transpose(2, 0, 1, 3, 4, 5)
    table = np.broadcast_to(table, table.shape[:3] + (pair,) + table.shape[4:])
    return np.ascontiguousarray(table).reshape(blocks, levels // 2 + 1, -1, row_count)


def slots(here, rows, b, kind, index):
    if kind == "level":
        return b * rows + index
    if kind == "later":
        return (2 + b) * rows + index
    base = 4 * rows + b * (rows // 2)
    return base + (index - 1 if kind == "row" else here - 1 + index)


def interior_tables(here, rows, cols, last):
    pair = 2
    lanes = here * pair * rows
    inner = here - 1
    chain = 2.0 * np.eye(inner) - np.eye(inner, k=1) - np.eye(inner, k=-1)
    if last:
        chain[-1, -1] = 1.0
    time_values, time_basis = np.linalg.eigh(chain)
    row_index = np.arange(1, rows)
    row_basis = np.sqrt(2.0 / rows) * np.sin(np.pi * np.outer(row_index, row_index) / rows)
    row_values = squared_sines(rows, 2 * rows)
    col_values = squared_sines(cols, cols)
    basis = np.zeros((here, pair, rows, here, pair, rows))
    inverse = np.zeros((cols, here, pair, rows))
    linked = np.zeros((here, pair, rows, lanes))
    for b in range(pair):
        for k in range(1, here):
            for t in range(1, here):
                basis[t, b, 1:, k, b, 1:] = time_basis[t - 1, k - 1] * row_basis
            inverse[:, k, b, 1:] = 1.0 / (
                col_values[:, None] + time_values[k - 1] + row_values[None, 1:]
            )
        for x in range(1, rows):
            linked[1, b, x, slots(here, rows, b, "level", x)] = 1.0
            if not last:
                linked[here - 1, b, x, slots(here, rows, b, "later", x)] = 1.0
        for t in range(1, here):
            linked[t, b, 1, slots(here, rows, b, "row", t)] = 1.0
            linked[t, b, rows - 1, slots(here, rows, b, "next", t)] = 1.0
    basis = basis.reshape(lanes, lanes)
    linked = linked.reshape(lanes, lanes)
    inverse = inverse.reshape(cols, lanes)
    to_edges = basis.T @ linked
    from_edges = to_edges.T.copy()
    for b in range(pair):
        ones = np.zeros((here, pair, rows))
        ones[1:, b, 1:] = 1.0
        from_edges[slots(here, rows, b, "next", here)] = -(ones.reshape(-1) @ basis)
    return basis, inverse, to_edges, from_edges


def constant_source(here, rows, time_blocks, row_blocks, tables):
    levels, row_count = here * time_blocks, rows * row_blocks
    field = np.zeros((levels + 1, row_count))
    ones = np.zeros((here, 2, rows))
    ones[1:, 0, 1:] = 1.0
    for i in range(time_blocks):
        basis, inverse, to_edges, _ = tables[1 if i == time_blocks - 1 else 0]
        edge = ((ones.reshape(-1) @ basis) * inverse[0]) @ to_edges
        for j in range(row_blocks):
            t0, x0 = i * here, j * rows
            for x in range(rows):
                field[t0, x0 + x] += 1.0 + edge[slots(here, rows, 0, "level", x)]
                field[t0 + here, x0 + x] += edge[slots(here, rows, 0, "later", x)]
            for t in range(here):
                after = (x0 + rows) % row_count
                field[t0 + t, after] += edge[slots(here, rows, 0, "next", t)]
                if t > 0:
                    field[t0 + t, x0] += 1.0 + edge[slots(here, rows, 0, "row", t)]
    return field[:levels] @ hartley_table(row_count)


def exchange_pieces(blocks, width):
    count = len(blocks)
    lanes = count * width
    group = lax.broadcasted_iota(jnp.int32, blocks[0].shape, 1) // width
    step = 1
    while step < count:
        upper = (group // step) % 2 == 1
        fresh = list(blocks)
        for j in range(count):
            if (j // step) % 2 == 0:
                low, high = blocks[j], blocks[j + step]
                fresh[j] = jnp.where(upper, pltpu.roll(high, step * width, 1), low)
                fresh[j + step] = jnp.where(upper, high, pltpu.roll(low, lanes - step * width, 1))
        blocks = fresh
        step *= 2
    return blocks


def source_kernel(
    levels,
    pair,
    mult_hbm,
    aux_hbm,
    start_hbm,
    end_hbm,
    hart_hbm,
    basis_hbm,
    inverse_hbm,
    edges_hbm,
    out_hbm,
    inner_hbm,
    mult_ref,
    aux_ref,
    density_ref,
    hart_ref,
    basis_ref,
    inverse_ref,
    edges_ref,
    out_ref,
    inner_ref,
    field_sems,
    table_sems,
    out_sems,
):
    _, here, batch, rows, cols = mult_ref.shape
    lanes = here * pair * rows
    pieces = lanes // rows
    each = cols // pieces
    total_pairs = batch // pair
    first = lax.axis_index("py") * here
    at_start = first == 0
    at_end = first + here == levels
    last = at_end.astype(jnp.int32)
    fields = []
    for part in range(FETCHES):
        cut = pl.ds(part * batch // FETCHES, batch // FETCHES)
        fields.append(
            [
                pltpu.make_async_copy(
                    one.at[:, :, cut], other.at[:, :, cut], field_sems.at[n, part]
                )
                for n, (one, other) in enumerate(((mult_hbm, mult_ref), (aux_hbm, aux_ref)))
            ]
        )
    tables = [
        pltpu.make_async_copy(hart_hbm, hart_ref, table_sems.at[0]),
        pltpu.make_async_copy(basis_hbm.at[last], basis_ref, table_sems.at[1]),
        pltpu.make_async_copy(inverse_hbm.at[last], inverse_ref, table_sems.at[2]),
        pltpu.make_async_copy(edges_hbm.at[last], edges_ref, table_sems.at[3]),
    ]
    start_copy = pltpu.make_async_copy(start_hbm, density_ref.at[0], table_sems.at[4])
    end_copy = pltpu.make_async_copy(end_hbm, density_ref.at[1], table_sems.at[5])
    for copy in fields[0] + [start_copy, end_copy] + fields[1] + tables + sum(fields[2:], []):
        copy.start()

    row_index = lax.broadcasted_iota(jnp.int32, (rows, cols), 0)
    first_row = row_index == 0
    outs = []
    for part in range(PARTS):
        mine = range(part * total_pairs // PARTS, (part + 1) * total_pairs // PARTS)
        field = []
        for q in mine:
            if q * FETCHES % total_pairs == 0:
                for copy in fields[q * FETCHES // total_pairs]:
                    copy.wait()
            if q == 0:
                start_copy.wait()
                end_copy.wait()
            blocks = []
            earlier = [0.0] * pair
            rims = jnp.zeros((rows, cols), jnp.float32)
            for t in range(here):
                for b in range(pair):
                    at = q * pair + b
                    time = aux_ref[0, t, at] - mult_ref[0, t, at]
                    if t == here - 1:
                        time = jnp.where(at_end, 0.0, time)
                    along = aux_ref[1, t, at] - mult_ref[1, t, at]
                    second = aux_ref[2, t, at] - mult_ref[2, t, at]
                    beside = jnp.where(first_row, 0.0, pltpu.roll(along, 1, 0))
                    total = (earlier[b] - time) + (beside - along)
                    total = total + (pltpu.roll(second, 1, 1) - second)
                    if t == 0:
                        total = total - jnp.where(at_start, density_ref[0, at], 0.0)
                    if t == here - 1:
                        total = total + jnp.where(at_end, density_ref[1, at], 0.0)
                    earlier[b] = time
                    blocks.append(total)
                    base = b * (rows // 2)
                    if t > 0:
                        rims = jnp.where(row_index == base + t - 1, total[:1], rims)
                    rims = jnp.where(row_index == base + here - 1 + t, along[rows - 1 :], rims)
            spare = jnp.zeros((lanes - (2 * pair + 1) * rows, cols), jnp.float32)
            nodes = jnp.concatenate(blocks + blocks[:pair] + earlier + [rims, spare], axis=0)
            field.append(long_data(nodes, 2, 1))
        if part == 0:
            for copy in tables:
                copy.wait()
        modes = [one_product(hart_ref[...], nodes, CROSS) for nodes in field]
        inner = [wide_product(mode[:, :lanes], basis_ref[...], 2) for mode in modes]
        gone = [wide_product(value * inverse_ref[...], edges_ref[...], 2) for value in inner]
        for n, q in enumerate(mine):
            inner_ref[q] = inner[n]
            edges = modes[n][:, lanes:] + gone[n]
            blocks = exchange_pieces(
                [edges[j * each : (j + 1) * each] for j in range(pieces)], rows
            )
            for k in range(out_ref.shape[2]):
                out_ref[:, q, k] = blocks[k].reshape(out_ref.shape[0], out_ref.shape[3], lanes)
        cut = pl.ds(mine[0], len(mine))
        outs += [
            pltpu.make_async_copy(out_ref.at[:, cut], out_hbm.at[:, cut], out_sems.at[0, part]),
            pltpu.make_async_copy(inner_ref.at[cut], inner_hbm.at[cut], out_sems.at[1, part]),
        ]
        for copy in outs[-2:]:
            copy.start()
    for copy in outs:
        copy.wait()


def solve_kernel(
    groups, in_ref, hart_ref, back_ref, ones_ref, table_ref, out_ref, field_ref, mean_ref, factor_ref, rim_ref, sem
):
    row_blocks, time_blocks, kinds, few, lanes = in_ref.shape
    levels, high, cols = field_ref.shape
    here = levels // time_blocks
    rows = cols // row_blocks
    pieces = lanes // rows
    tall = (kinds - 1) * few
    count = high // tall
    half = levels // 2
    mine = lax.axis_index("px") * lax.axis_size("grp") + lax.axis_index("grp")
    fetch = pltpu.make_async_copy(table_ref.at[mine], factor_ref, sem)
    fetch.start()
    stack = tall // few
    lane = lax.broadcasted_iota(jnp.int32, (tall, cols), 1) % rows
    row = lax.broadcasted_iota(jnp.int32, (tall, cols), 0)
    low = row < tall // 2
    even = (row // few) % 2 == 0

    def shift(value, steps):
        return pltpu.roll(value, steps % cols, 1)

    def swap(value):
        return pltpu.roll(value, tall // 2, 0)

    def place(g, j):
        block = g * pieces + j
        return block % (row_blocks // groups) * groups + block // (row_blocks // groups)

    def exchange(get):
        halves = [
            exchange_pieces([get(place(g, j)) for j in range(pieces)], rows)
            for g in range(row_blocks // pieces)
        ]
        return [jnp.concatenate([one[k] for one in halves], axis=1) for k in range(pieces)]

    for h in range(time_blocks // stack):
        times = slice(h * stack, (h + 1) * stack)
        for j, rim in enumerate(exchange(lambda x: in_ref[x, times, kinds - 1].reshape(tall, lanes))):
            rim_ref[h, j, 0] = rim
            rim_ref[h, j, 1] = shift(rim, -(rows // 2))

    def forward(i, carry):
        main = exchange(lambda x: in_ref[x, i, : kinds - 1].reshape(tall, lanes))
        here_rows = slice(i % stack * few, (i % stack + 1) * few)
        field = [[] for _ in range(here)]
        later = []
        for q in range(count):
            one, two = main[2 * q], main[2 * q + 1]
            level = jnp.where(low, one, swap(two)) + carry[q]
            later.append(jnp.where(low, swap(one), two))
            rim = jnp.concatenate(
                [rim_ref[i // stack, 2 * q + j, b, here_rows] for j in range(2) for b in range(2)],
                axis=0,
            )
            rim = jnp.where(lane < here - 1, rim, 0.0) + shift(rim, rows - here)
            for t in range(here):
                value = jnp.where(lane == 0, rim if t == 1 else shift(rim, 1 - t), 0.0)
                field[t].append(value + level if t == 0 else value)
        field = jnp.concatenate(sum(field, []), axis=0)
        modes = one_product(long_data(field, 2, 1), hart_ref[...], DIRECT)
        field_ref[pl.ds(i * here, here)] = modes.reshape(here, high, cols)
        return tuple(later)

    blank = jnp.zeros((tall, cols), jnp.float32)
    carry = (blank,) * count
    for i in range(time_blocks):
        carry = forward(i, carry)
    fetch.wait()

    mean_ref[...] = jnp.zeros(mean_ref.shape, jnp.float32)

    @pl.when(mine == 0)
    def _():
        shape = (tall, 128)
        spot = lax.broadcasted_iota(jnp.int32, shape, 0)
        zero = (spot % few == 0) & (spot < tall // 2)
        zero = zero & (lax.broadcasted_iota(jnp.int32, shape, 1) == 0)
        scale = float(np.sqrt(cols)) / (levels * cols)
        sums = field_ref[0, :tall, :128]
        for t in range(1, levels):
            sums = sums + field_ref[t, :tall, :128]
        mean = jnp.sum(jnp.where(zero, sums * scale, 0.0), axis=1, keepdims=True)
        mean_ref[0] = jnp.broadcast_to(mean, (tall, cols))
        for t in range(levels):
            field_ref[t, :tall] = field_ref[t, :tall] - mean * ones_ref[t : t + 1]

    left = jnp.zeros(field_ref.shape[1:], jnp.float32)
    right = left
    for t in range(half):
        factor = factor_ref[t]
        left = (field_ref[t] + left) * factor
        right = (field_ref[levels - 1 - t] + right) * factor
        if t < half - 1:
            field_ref[t] = left
            field_ref[levels - 1 - t] = right
    first = (left + factor * right) * factor_ref[half]
    right = right + factor * first
    left = first
    field_ref[half - 1] = left
    field_ref[half] = right
    for t in range(half - 2, -1, -1):
        factor = factor_ref[t]
        left = field_ref[t] + factor * left
        right = field_ref[levels - 1 - t] + factor * right
        field_ref[t] = left
        field_ref[levels - 1 - t] = right

    def backward(i, carry):
        here_rows = slice(i % stack * few, (i % stack + 1) * few)
        field = field_ref[pl.ds(i * here, here)].reshape(here * high, cols)
        values = one_product(long_data(field, 3, 1), back_ref[...], DIRECT)
        main, first = [], []
        for q in range(count):
            part = [values[t * high + q * tall : t * high + (q + 1) * tall] for t in range(here)]
            rim = jnp.where(lane == rows - 1, shift(part[0], -1), part[1])
            for t in range(2, here):
                rim = jnp.where(lane == t - 1, shift(part[t], t - 1), rim)
            after = jnp.where(lane < 2 * here - 1, shift(rim, here - rows), mean_ref[q])
            rim = jnp.where(lane < here - 1, rim, after)
            rim = jnp.where(lane < 2 * here, rim, 0.0)
            rim = jnp.where(even, rim, shift(rim, rows // 2))
            rim = rim + pltpu.roll(rim, tall - few, 0)
            rim_ref[i // stack, 2 * q, 0, here_rows] = rim[:few]
            rim_ref[i // stack, 2 * q + 1, 0, here_rows] = rim[tall // 2 : tall // 2 + few]
            main.append(jnp.where(low, part[0], swap(carry[q])))
            main.append(jnp.where(low, swap(part[0]), carry[q]))
            first.append(part[0])
        for g in range(row_blocks // pieces):
            cut = slice(g * lanes, (g + 1) * lanes)
            for j, value in enumerate(exchange_pieces([a[:, cut] for a in main], rows)):
                out_ref[place(g, j), i, : kinds - 1] = value.reshape(kinds - 1, few, lanes)
        return tuple(first)

    carry = (blank,) * count
    for i in range(time_blocks - 1, -1, -1):
        carry = backward(i, carry)
    for h in range(time_blocks // stack):
        times = slice(h * stack, (h + 1) * stack)
        for g in range(row_blocks // pieces):
            cut = slice(g * lanes, (g + 1) * lanes)
            rims = exchange_pieces([rim_ref[h, j, 0, :, cut] for j in range(pieces)], rows)
            for j, value in enumerate(rims):
                out_ref[place(g, j), times, kinds - 1] = value.reshape(stack, few, lanes)


def step_kernel(
    levels,
    pair,
    mult_in,
    edge_ref,
    inner_ref,
    hart_ref,
    links_ref,
    inverse_ref,
    basis_ref,
    mult_hbm,
    aux_hbm,
    mult_ref,
    mult_out,
    aux_out,
    sems,
):
    _, here, batch, rows, cols = mult_ref.shape
    lanes = here * pair * rows
    pieces = lanes // rows
    kinds = edge_ref.shape[2]
    total_pairs = batch // pair
    first = lax.axis_index("py") * here
    last = (first + here == levels).astype(jnp.int32)
    inside = 1.0 - last.astype(jnp.float32)
    outs = []
    fetches = []
    for q in range(total_pairs):
        cut = pl.ds(q * pair, pair)
        fetches.append(
            pltpu.make_async_copy(mult_in.at[:, :, cut], mult_ref.at[:, :, cut], sems.at[2, q])
        )
        fetches[q].start()
    for part in range(STEP_PARTS):
        mine = range(part * total_pairs // STEP_PARTS, (part + 1) * total_pairs // STEP_PARTS)
        edges = []
        for q in mine:
            blocks = [edge_ref[:, q, k].reshape(cols // pieces, lanes) for k in range(kinds)]
            blocks += [jnp.zeros((cols // pieces, lanes), jnp.float32)] * (pieces - kinds)
            edges.append(jnp.concatenate(exchange_pieces(blocks, rows), axis=0))
        linked = [wide_product(edge, links_ref[last], 3) for edge in edges]
        gone = [(inner_ref[q] + link) * inverse_ref[last] for q, link in zip(mine, linked)]
        nodes = [wide_product(value, basis_ref[last], 3) for value in gone]
        whole = [
            jnp.concatenate(both, axis=1).T[: lanes + kinds * rows] for both in zip(nodes, edges)
        ]
        potential = [one_product(long_data(value, 3, 1), hart_ref[...], DIRECT) for value in whole]
        for q, values in zip(mine, potential):
            fetches[q].wait()
            step_part(q, pair, values, inside, mult_ref, mult_out, aux_out)
            cut = pl.ds(q * pair, pair)
            for n, (one, other) in enumerate(((mult_out, mult_hbm), (aux_out, aux_hbm))):
                copy = pltpu.make_async_copy(one.at[:, :, cut], other.at[:, :, cut], sems.at[n, q])
                copy.start()
                outs.append(copy)
    for copy in outs:
        copy.wait()


def step_part(q, pair, values, inside, mult_ref, mult_out, aux_out):
    _, here, _, rows, cols = mult_ref.shape
    lanes = here * pair * rows
    full = (pair, rows, cols)
    row_index = lax.broadcasted_iota(jnp.int32, full, 1)
    at = slice(q * pair, (q + 1) * pair)

    def level(start):
        return values[start : start + pair * rows].reshape(full)

    def rims(kind, t):
        starts = [lanes + slots(here, rows, b, kind, t) for b in range(pair)]
        rim = [jnp.broadcast_to(values[start : start + 1], (rows, cols)) for start in starts]
        return jnp.concatenate(rim, axis=0).reshape(full)

    phi = [level(lanes)]
    for t in range(1, here):
        phi.append(jnp.where(row_index == 0, rims("row", t), level(t * pair * rows)))
    phi.append(level(lanes + pair * rows))
    for t0 in range(0, here, 1):
        times = range(t0, t0 + 1)
        mine = jnp.concatenate([phi[t] for t in times], axis=0)
        rate = jnp.concatenate([phi[t + 1] for t in times], axis=0) - mine
        if times[-1] == here - 1:
            kept = [rate[: (1 - 1) * pair]] if 1 > 1 else []
            rate = jnp.concatenate(kept + [rate[(1 - 1) * pair :] * inside], axis=0)
        rim = jnp.concatenate([rims("next", t) for t in times], axis=0)
        index = lax.broadcasted_iota(jnp.int32, mine.shape, 1)
        below = jnp.where(index == rows - 1, rim, pltpu.roll(mine, rows - 1, 1))
        gradient = (rate, below - mine, pltpu.roll(mine, cols - 1, 2) - mine)
        target = [
            gradient[c] + jnp.concatenate([mult_ref[c, t, at] for t in times], axis=0)
            for c in range(3)
        ]
        time_part, one, two = target
        kinetic = 0.5 * (one * one + two * two)
        center = 1.0 + time_part
        scaling = jnp.maximum(center, 1.0) + jnp.exp(jnp.log(kinetic) * (1.0 / 3.0))
        for _ in range(NEWTON):
            linear = scaling * (scaling - center)
            residue = scaling * linear - kinetic
            derivative = scaling * scaling + (linear + linear)
            change = residue * pl.reciprocal(derivative, approx=True)
            scaling = jnp.maximum(scaling - change, 1.0)
        scaling = jnp.where(time_part + kinetic <= 0.0, 1.0, scaling)
        shrink = pl.reciprocal(scaling, approx=True)
        shrink = shrink * (2.0 - scaling * shrink)
        shrink = shrink * (2.0 - scaling * shrink)
        moved = scaling - 1.0
        fresh = (time_part - moved, one * shrink, two * shrink)
        for c, past in enumerate((moved, one - fresh[1], two - fresh[2])):
            for n, t in enumerate(times):
                part = slice(n * pair, (n + 1) * pair)
                aux_out[c, t, at] = fresh[c][part]
                mult_out[c, t, at] = past[part]


def params(size=48):
    return pltpu.CompilerParams(vmem_limit_bytes=size * 1024 * 1024)


def local(multiplier, auxiliary, density_start, density_end):
    _, here, batch, rows, cols = multiplier.shape
    time_blocks = lax.axis_size("py")
    row_blocks = lax.axis_size("grp") * lax.axis_size("px")
    levels = here * time_blocks
    row_count = rows * row_blocks
    pair = batch // time_blocks
    lanes = here * pair * rows
    pieces = lanes // rows
    kinds = 2 * pair + 1
    few = cols // (pieces * row_blocks)
    both = [interior_tables(here, rows, cols, last) for last in (False, True)]
    hart_there = long_table(hartley_table(cols), 2, 1)
    hart_back = long_table(hartley_table(cols), 3, 0)
    rows_there = long_table(hartley_table(row_count), 2, 0)
    rows_back = long_table(hartley_table(row_count), 3, 0)
    basis2 = np.stack([wide_table(one[0], 2) for one in both])
    basis3 = np.stack([wide_table(one[0].T, 3) for one in both])
    inverse = np.stack([one[1] for one in both]).astype(np.float32)
    to_edges = np.stack([wide_table(one[2], 2) for one in both])
    from_edges = np.stack([wide_table(one[3], 3) for one in both])
    ones = constant_source(here, rows, time_blocks, row_blocks, both).astype(np.float32)
    factors = elimination_table(levels, row_count, cols, row_blocks, pieces, pair)

    away = pl.BlockSpec(memory_space=pltpu.HBM)
    vmem = pl.BlockSpec(memory_space=pltpu.VMEM)
    chunked = jax.ShapeDtypeStruct((row_blocks, time_blocks, kinds, few, lanes), jnp.float32)
    inner_shape = (time_blocks, cols, lanes)
    edges, inner = pl.pallas_call(
        functools.partial(source_kernel, levels, pair),
        in_specs=[away] * 8,
        out_specs=[away] * 2,
        out_shape=[chunked, jax.ShapeDtypeStruct(inner_shape, jnp.float32)],
        scratch_shapes=[
            pltpu.VMEM(multiplier.shape, jnp.float32),
            pltpu.VMEM(auxiliary.shape, jnp.float32),
            pltpu.VMEM((2,) + density_start.shape, jnp.float32),
            pltpu.VMEM(hart_there.shape, jnp.bfloat16),
            pltpu.VMEM(basis2.shape[1:], jnp.bfloat16),
            pltpu.VMEM(inverse.shape[1:], jnp.float32),
            pltpu.VMEM(to_edges.shape[1:], jnp.bfloat16),
            pltpu.VMEM(chunked.shape, jnp.float32),
            pltpu.VMEM(inner_shape, jnp.float32),
            pltpu.SemaphoreType.DMA((2, FETCHES)),
            pltpu.SemaphoreType.DMA((6,)),
            pltpu.SemaphoreType.DMA((2, PARTS)),
        ],
        compiler_params=params(56),
        name="source",
    )(multiplier, auxiliary, density_start, density_end, hart_there, basis2, inverse, to_edges)

    def spread(value):
        flat = value.reshape((row_blocks * time_blocks,) + value.shape[2:])
        return lax.all_to_all(flat, EVERY, 0, 0, tiled=True).reshape(value.shape)

    solved = pl.pallas_call(
        functools.partial(solve_kernel, lax.axis_size("grp")),
        in_specs=[vmem, vmem, vmem, vmem, pl.BlockSpec(memory_space=pl.ANY)],
        out_specs=vmem,
        out_shape=chunked,
        scratch_shapes=[
            pltpu.VMEM((levels, pair * pieces * few, row_count), jnp.float32),
            pltpu.VMEM((pieces // 2, 2 * pair * few, row_count), jnp.float32),
            pltpu.VMEM(factors.shape[1:], jnp.float32),
            pltpu.VMEM((time_blocks // (2 * pair), pieces, 2, 2 * pair * few, row_count), jnp.float32),
            pltpu.SemaphoreType.DMA,
        ],
        compiler_params=params(),
        name="solve",
    )(spread(edges), rows_there, rows_back, ones, factors)

    result = jax.ShapeDtypeStruct(multiplier.shape, jnp.float32)
    mult_next, aux_next = pl.pallas_call(
        functools.partial(step_kernel, levels, pair),
        in_specs=[away] + [vmem] * 6,
        out_specs=[away] * 2,
        scratch_shapes=[
            pltpu.VMEM(multiplier.shape, jnp.float32),
            pltpu.VMEM(multiplier.shape, jnp.float32),
            pltpu.VMEM(multiplier.shape, jnp.float32),
            pltpu.SemaphoreType.DMA((3, time_blocks)),
        ],
        out_shape=[result, result],
        compiler_params=params(),
        name="step",
    )(multiplier, spread(solved), inner, hart_back, from_edges, inverse, basis3)
    return mult_next, aux_next


def solution(mesh):
    field = P(None, "py", None, ROWS, None)
    density = P(None, ROWS, None)
    return jax.shard_map(
        local,
        mesh=mesh,
        in_specs=(field, field, density, density),
        out_specs=(field, field),
        check_vma=False,
    )
```

```python
import functools

import jax
import jax.numpy as jnp
import numpy as np
from jax import lax
from jax.experimental import pallas as pl
from jax.experimental.pallas import tpu as pltpu
from jax.sharding import PartitionSpec as P

NEWTON = 4
ROWS = ("grp", "px")
EVERY = ("px", "grp", "py")
PARTS = 2
FETCHES = 4
STEP_PARTS = 2
VMEM_BYTES = 48 * 1024 * 1024
DIRECT = ((1,), (0,))
CROSS = ((1,), (1,))


def table_parts(table, count):
    rest = np.asarray(table, np.float32)
    parts = []
    for _ in range(count):
        parts.append(rest.astype(jnp.bfloat16))
        rest = rest - parts[-1].astype(np.float32)
    return np.stack(parts)


def parts_of(value, count):
    parts = [value.astype(jnp.bfloat16)]
    for _ in range(count - 1):
        value = value - parts[-1].astype(jnp.float32)
        parts.append(value.astype(jnp.bfloat16))
    return parts


def orders(count):
    return [(i, order - i) for order in range(count - 1, -1, -1) for i in range(order + 1)]


def long_table(table, count, axis):
    parts = table_parts(table, count)
    return np.concatenate([parts[j] for _, j in orders(count)], axis=axis)


def long_data(value, count, axis):
    parts = parts_of(value, count)
    return jnp.concatenate([parts[i] for i, _ in orders(count)], axis=axis)


def wide_table(table, count):
    parts = table_parts(table, count)
    none = np.zeros_like(parts[0])
    if count == 2:
        grid = [(0, 1), (0, None)]
    else:
        grid = [(0, 1), (0, 1), (2, None), (0, None)]
    return np.block([[none if k is None else parts[k] for k in row] for row in grid])


def wide_product(value, table, count):
    parts = parts_of(value, count)
    data = parts if count == 2 else [parts[0], parts[1], parts[0], parts[2]]
    both = one_product(jnp.concatenate(data, axis=1), table, DIRECT)
    half = both.shape[1] // 2
    return both[:, :half] + both[:, half:]


def one_product(left, right, dims):
    return lax.dot_general(left, right, (dims, ((), ())), preferred_element_type=jnp.float32)


def squared_sines(length, period):
    return 4.0 * np.sin(np.pi * np.arange(length) / period) ** 2


def hartley_table(length):
    index = np.arange(length)
    angles = (index[:, None] * index[None, :] % length) * (2.0 * np.pi / length)
    return (np.cos(angles) + np.sin(angles)) / np.sqrt(length)


def elimination_table(levels, row_count, col_count, blocks, pieces, pair):
    eigen = squared_sines(col_count, col_count)[:, None] + squared_sines(row_count, row_count)
    factors = [1.0 / (1.0 + eigen)]
    for _ in range(levels // 2 - 1):
        factors.append(1.0 / (2.0 + eigen - factors[-1]))
    gap = 1.0 - factors[-1] ** 2
    middle = np.where(eigen > 0.0, 1.0 / np.where(eigen > 0.0, gap, 1.0), 0.0)
    table = np.stack(factors + [middle]).astype(np.float32)
    table = table.reshape(levels // 2 + 1, pieces, blocks, 1, -1, row_count).transpose(2, 0, 1, 3, 4, 5)
    table = np.broadcast_to(table, table.shape[:3] + (pair,) + table.shape[4:])
    return np.ascontiguousarray(table).reshape(blocks, levels // 2 + 1, -1, row_count)


def slots(here, rows, b, kind, index):
    if kind == "level":
        return b * rows + index
    if kind == "later":
        return (2 + b) * rows + index
    base = 4 * rows + b * (rows // 2)
    return base + (index - 1 if kind == "row" else here - 1 + index)


def interior_tables(here, rows, cols, last):
    pair = 2
    lanes = here * pair * rows
    inner = here - 1
    chain = 2.0 * np.eye(inner) - np.eye(inner, k=1) - np.eye(inner, k=-1)
    if last:
        chain[-1, -1] = 1.0
    time_values, time_basis = np.linalg.eigh(chain)
    row_index = np.arange(1, rows)
    row_basis = np.sqrt(2.0 / rows) * np.sin(np.pi * np.outer(row_index, row_index) / rows)
    row_values = squared_sines(rows, 2 * rows)
    col_values = squared_sines(cols, cols)
    basis = np.zeros((here, pair, rows, here, pair, rows))
    inverse = np.zeros((cols, here, pair, rows))
    linked = np.zeros((here, pair, rows, lanes))
    for b in range(pair):
        for k in range(1, here):
            for t in range(1, here):
                basis[t, b, 1:, k, b, 1:] = time_basis[t - 1, k - 1] * row_basis
            inverse[:, k, b, 1:] = 1.0 / (
                col_values[:, None] + time_values[k - 1] + row_values[None, 1:]
            )
        for x in range(1, rows):
            linked[1, b, x, slots(here, rows, b, "level", x)] = 1.0
            if not last:
                linked[here - 1, b, x, slots(here, rows, b, "later", x)] = 1.0
        for t in range(1, here):
            linked[t, b, 1, slots(here, rows, b, "row", t)] = 1.0
            linked[t, b, rows - 1, slots(here, rows, b, "next", t)] = 1.0
    basis = basis.reshape(lanes, lanes)
    linked = linked.reshape(lanes, lanes)
    inverse = inverse.reshape(cols, lanes)
    to_edges = basis.T @ linked
    from_edges = to_edges.T.copy()
    for b in range(pair):
        ones = np.zeros((here, pair, rows))
        ones[1:, b, 1:] = 1.0
        from_edges[slots(here, rows, b, "next", here)] = -(ones.reshape(-1) @ basis)
    return basis, inverse, to_edges, from_edges


def constant_source(here, rows, time_blocks, row_blocks, tables):
    levels, row_count = here * time_blocks, rows * row_blocks
    field = np.zeros((levels + 1, row_count))
    ones = np.zeros((here, 2, rows))
    ones[1:, 0, 1:] = 1.0
    for i in range(time_blocks):
        basis, inverse, to_edges, _ = tables[1 if i == time_blocks - 1 else 0]
        edge = ((ones.reshape(-1) @ basis) * inverse[0]) @ to_edges
        for j in range(row_blocks):
            t0, x0 = i * here, j * rows
            for x in range(rows):
                field[t0, x0 + x] += 1.0 + edge[slots(here, rows, 0, "level", x)]
                field[t0 + here, x0 + x] += edge[slots(here, rows, 0, "later", x)]
            for t in range(here):
                after = (x0 + rows) % row_count
                field[t0 + t, after] += edge[slots(here, rows, 0, "next", t)]
                if t > 0:
                    field[t0 + t, x0] += 1.0 + edge[slots(here, rows, 0, "row", t)]
    return field[:levels] @ hartley_table(row_count)


def exchange_pieces(blocks, width):
    count = len(blocks)
    lanes = count * width
    group = lax.broadcasted_iota(jnp.int32, blocks[0].shape, 1) // width
    step = 1
    while step < count:
        upper = (group // step) % 2 == 1
        fresh = list(blocks)
        for j in range(count):
            if (j // step) % 2 == 0:
                low, high = blocks[j], blocks[j + step]
                fresh[j] = jnp.where(upper, pltpu.roll(high, step * width, 1), low)
                fresh[j + step] = jnp.where(upper, high, pltpu.roll(low, lanes - step * width, 1))
        blocks = fresh
        step *= 2
    return blocks


def source_kernel(
    levels,
    pair,
    mult_hbm,
    aux_hbm,
    start_hbm,
    end_hbm,
    hart_hbm,
    basis_hbm,
    inverse_hbm,
    edges_hbm,
    factors_hbm,
    out_hbm,
    inner_hbm,
    factor_hbm,
    mult_ref,
    aux_ref,
    density_ref,
    hart_ref,
    basis_ref,
    inverse_ref,
    edges_ref,
    out_ref,
    inner_ref,
    field_sems,
    table_sems,
    out_sems,
):
    _, here, batch, rows, cols = mult_ref.shape
    lanes = here * pair * rows
    pieces = lanes // rows
    each = cols // pieces
    total_pairs = batch // pair
    first = lax.axis_index("py") * here
    at_start = first == 0
    at_end = first + here == levels
    last = at_end.astype(jnp.int32)
    fields = []
    for part in range(FETCHES):
        cut = pl.ds(part * batch // FETCHES, batch // FETCHES)
        fields.append(
            [
                pltpu.make_async_copy(
                    one.at[:, :, cut], other.at[:, :, cut], field_sems.at[n, part]
                )
                for n, (one, other) in enumerate(((mult_hbm, mult_ref), (aux_hbm, aux_ref)))
            ]
        )
    tables = [
        pltpu.make_async_copy(hart_hbm, hart_ref, table_sems.at[0]),
        pltpu.make_async_copy(basis_hbm.at[last], basis_ref, table_sems.at[1]),
        pltpu.make_async_copy(inverse_hbm.at[last], inverse_ref, table_sems.at[2]),
        pltpu.make_async_copy(edges_hbm.at[last], edges_ref, table_sems.at[3]),
    ]
    modes_here = lax.axis_index("px") * lax.axis_size("grp") + lax.axis_index("grp")
    factor_copy = pltpu.make_async_copy(factors_hbm.at[modes_here], factor_hbm, table_sems.at[6])
    start_copy = pltpu.make_async_copy(start_hbm, density_ref.at[0], table_sems.at[4])
    end_copy = pltpu.make_async_copy(end_hbm, density_ref.at[1], table_sems.at[5])
    for copy in fields[0] + [start_copy, end_copy] + fields[1] + tables + sum(fields[2:], []) + [factor_copy]:
        copy.start()

    row_index = lax.broadcasted_iota(jnp.int32, (rows, cols), 0)
    first_row = row_index == 0
    outs = [factor_copy]
    for part in range(PARTS):
        mine = range(part * total_pairs // PARTS, (part + 1) * total_pairs // PARTS)
        field = []
        for q in mine:
            if q * FETCHES % total_pairs == 0:
                for copy in fields[q * FETCHES // total_pairs]:
                    copy.wait()
            if q == 0:
                start_copy.wait()
                end_copy.wait()
            blocks = []
            earlier = [0.0] * pair
            rims = jnp.zeros((rows, cols), jnp.float32)
            for t in range(here):
                for b in range(pair):
                    at = q * pair + b
                    time = aux_ref[0, t, at] - mult_ref[0, t, at]
                    if t == here - 1:
                        time = jnp.where(at_end, 0.0, time)
                    along = aux_ref[1, t, at] - mult_ref[1, t, at]
                    second = aux_ref[2, t, at] - mult_ref[2, t, at]
                    beside = jnp.where(first_row, 0.0, pltpu.roll(along, 1, 0))
                    total = (earlier[b] - time) + (beside - along)
                    total = total + (pltpu.roll(second, 1, 1) - second)
                    if t == 0:
                        total = total - jnp.where(at_start, density_ref[0, at], 0.0)
                    if t == here - 1:
                        total = total + jnp.where(at_end, density_ref[1, at], 0.0)
                    earlier[b] = time
                    blocks.append(total)
                    base = b * (rows // 2)
                    if t > 0:
                        rims = jnp.where(row_index == base + t - 1, total[:1], rims)
                    rims = jnp.where(row_index == base + here - 1 + t, along[rows - 1 :], rims)
            spare = jnp.zeros((lanes - (2 * pair + 1) * rows, cols), jnp.float32)
            nodes = jnp.concatenate(blocks + blocks[:pair] + earlier + [rims, spare], axis=0)
            field.append(long_data(nodes, 2, 1))
        if part == 0:
            for copy in tables:
                copy.wait()
        modes = [one_product(hart_ref[...], nodes, CROSS) for nodes in field]
        inner = [wide_product(mode[:, :lanes], basis_ref[...], 2) for mode in modes]
        for n, q in enumerate(mine):
            inner_ref[q] = inner[n]
            outs.append(pltpu.make_async_copy(inner_ref.at[q], inner_hbm.at[q], out_sems.at[1, q]))
            outs[-1].start()
        gone = [wide_product(value * inverse_ref[...], edges_ref[...], 2) for value in inner]
        for n, q in enumerate(mine):
            edges = modes[n][:, lanes:] + gone[n]
            blocks = exchange_pieces(
                [edges[j * each : (j + 1) * each] for j in range(pieces)], rows
            )
            for k in range(out_ref.shape[2]):
                out_ref[:, q, k] = blocks[k].reshape(out_ref.shape[0], out_ref.shape[3], lanes)
            outs.append(
                pltpu.make_async_copy(out_ref.at[:, q], out_hbm.at[:, q], out_sems.at[0, q])
            )
            outs[-1].start()
    for copy in outs:
        copy.wait()


def solve_kernel(
    groups, in_ref, hart_ref, back_ref, ones_ref, factor_ref, out_ref, field_ref, mean_ref, rim_ref
):
    row_blocks, time_blocks, kinds, few, lanes = in_ref.shape
    levels, high, cols = field_ref.shape
    here = levels // time_blocks
    rows = cols // row_blocks
    pieces = lanes // rows
    tall = (kinds - 1) * few
    count = high // tall
    half = levels // 2
    mine = lax.axis_index("px") * lax.axis_size("grp") + lax.axis_index("grp")
    stack = tall // few
    lane = lax.broadcasted_iota(jnp.int32, (tall, cols), 1) % rows
    row = lax.broadcasted_iota(jnp.int32, (tall, cols), 0)
    low = row < tall // 2
    even = (row // few) % 2 == 0

    def shift(value, steps):
        return pltpu.roll(value, steps % cols, 1)

    def swap(value):
        return pltpu.roll(value, tall // 2, 0)

    def place(g, j):
        block = g * pieces + j
        return block % (row_blocks // groups) * groups + block // (row_blocks // groups)

    def exchange(get):
        halves = [
            exchange_pieces([get(place(g, j)) for j in range(pieces)], rows)
            for g in range(row_blocks // pieces)
        ]
        return [jnp.concatenate([one[k] for one in halves], axis=1) for k in range(pieces)]

    for h in range(time_blocks // stack):
        times = slice(h * stack, (h + 1) * stack)
        for j, rim in enumerate(exchange(lambda x: in_ref[x, times, kinds - 1].reshape(tall, lanes))):
            rim_ref[h, j, 0] = rim
            rim_ref[h, j, 1] = shift(rim, -(rows // 2))

    def forward(i, carry):
        main = exchange(lambda x: in_ref[x, i, : kinds - 1].reshape(tall, lanes))
        here_rows = slice(i % stack * few, (i % stack + 1) * few)
        field = [[] for _ in range(here)]
        later = []
        for q in range(count):
            one, two = main[2 * q], main[2 * q + 1]
            level = jnp.where(low, one, swap(two)) + carry[q]
            later.append(jnp.where(low, swap(one), two))
            rim = jnp.concatenate(
                [rim_ref[i // stack, 2 * q + j, b, here_rows] for j in range(2) for b in range(2)],
                axis=0,
            )
            rim = jnp.where(lane < here - 1, rim, 0.0) + shift(rim, rows - here)
            for t in range(here):
                value = jnp.where(lane == 0, rim if t == 1 else shift(rim, 1 - t), 0.0)
                field[t].append(value + level if t == 0 else value)
        field = jnp.concatenate(sum(field, []), axis=0)
        modes = one_product(long_data(field, 2, 1), hart_ref[...], DIRECT)
        field_ref[pl.ds(i * here, here)] = modes.reshape(here, high, cols)
        return tuple(later)

    blank = jnp.zeros((tall, cols), jnp.float32)
    carry = (blank,) * count
    for i in range(time_blocks):
        carry = forward(i, carry)

    mean_ref[...] = jnp.zeros(mean_ref.shape, jnp.float32)

    @pl.when(mine == 0)
    def _():
        shape = (tall, 128)
        spot = lax.broadcasted_iota(jnp.int32, shape, 0)
        zero = (spot % few == 0) & (spot < tall // 2)
        zero = zero & (lax.broadcasted_iota(jnp.int32, shape, 1) == 0)
        scale = float(np.sqrt(cols)) / (levels * cols)
        sums = field_ref[0, :tall, :128]
        for t in range(1, levels):
            sums = sums + field_ref[t, :tall, :128]
        mean = jnp.sum(jnp.where(zero, sums * scale, 0.0), axis=1, keepdims=True)
        mean_ref[0] = jnp.broadcast_to(mean, (tall, cols))
        for t in range(levels):
            field_ref[t, :tall] = field_ref[t, :tall] - mean * ones_ref[t : t + 1]

    left = jnp.zeros(field_ref.shape[1:], jnp.float32)
    right = left
    for t in range(half):
        factor = factor_ref[t]
        left = (field_ref[t] + left) * factor
        right = (field_ref[levels - 1 - t] + right) * factor
        if t < half - 1:
            field_ref[t] = left
            field_ref[levels - 1 - t] = right
    first = (left + factor * right) * factor_ref[half]
    right = right + factor * first
    left = first
    field_ref[half - 1] = left
    field_ref[half] = right
    for t in range(half - 2, -1, -1):
        factor = factor_ref[t]
        left = field_ref[t] + factor * left
        right = field_ref[levels - 1 - t] + factor * right
        field_ref[t] = left
        field_ref[levels - 1 - t] = right

    def backward(i, carry):
        here_rows = slice(i % stack * few, (i % stack + 1) * few)
        field = field_ref[pl.ds(i * here, here)].reshape(here * high, cols)
        values = one_product(long_data(field, 3, 1), back_ref[...], DIRECT)
        main, first = [], []
        for q in range(count):
            part = [values[t * high + q * tall : t * high + (q + 1) * tall] for t in range(here)]
            rim = jnp.where(lane == rows - 1, shift(part[0], -1), part[1])
            for t in range(2, here):
                rim = jnp.where(lane == t - 1, shift(part[t], t - 1), rim)
            after = jnp.where(lane < 2 * here - 1, shift(rim, here - rows), mean_ref[q])
            rim = jnp.where(lane < here - 1, rim, after)
            rim = jnp.where(lane < 2 * here, rim, 0.0)
            rim = jnp.where(even, rim, shift(rim, rows // 2))
            rim = rim + pltpu.roll(rim, tall - few, 0)
            rim_ref[i // stack, 2 * q, 0, here_rows] = rim[:few]
            rim_ref[i // stack, 2 * q + 1, 0, here_rows] = rim[tall // 2 : tall // 2 + few]
            main.append(jnp.where(low, part[0], swap(carry[q])))
            main.append(jnp.where(low, swap(part[0]), carry[q]))
            first.append(part[0])
        for g in range(row_blocks // pieces):
            cut = slice(g * lanes, (g + 1) * lanes)
            for j, value in enumerate(exchange_pieces([a[:, cut] for a in main], rows)):
                out_ref[place(g, j), i, : kinds - 1] = value.reshape(kinds - 1, few, lanes)
        return tuple(first)

    carry = (blank,) * count
    for i in range(time_blocks - 1, -1, -1):
        carry = backward(i, carry)
    for h in range(time_blocks // stack):
        times = slice(h * stack, (h + 1) * stack)
        for g in range(row_blocks // pieces):
            cut = slice(g * lanes, (g + 1) * lanes)
            rims = exchange_pieces([rim_ref[h, j, 0, :, cut] for j in range(pieces)], rows)
            for j, value in enumerate(rims):
                out_ref[place(g, j), times, kinds - 1] = value.reshape(stack, few, lanes)


def step_kernel(
    levels,
    pair,
    mult_in,
    edge_ref,
    inner_ref,
    hart_ref,
    links_ref,
    inverse_ref,
    basis_ref,
    mult_hbm,
    aux_hbm,
    mult_ref,
    mult_out,
    aux_out,
    sems,
):
    _, here, batch, rows, cols = mult_ref.shape
    lanes = here * pair * rows
    pieces = lanes // rows
    kinds = edge_ref.shape[2]
    total_pairs = batch // pair
    first = lax.axis_index("py") * here
    last = (first + here == levels).astype(jnp.int32)
    inside = 1.0 - last.astype(jnp.float32)
    outs = []
    fetches = []
    for q in range(total_pairs):
        cut = pl.ds(q * pair, pair)
        fetches.append(
            pltpu.make_async_copy(mult_in.at[:, :, cut], mult_ref.at[:, :, cut], sems.at[2, q])
        )
        fetches[q].start()
    for part in range(STEP_PARTS):
        mine = range(part * total_pairs // STEP_PARTS, (part + 1) * total_pairs // STEP_PARTS)
        edges = []
        for q in mine:
            blocks = [edge_ref[:, q, k].reshape(cols // pieces, lanes) for k in range(kinds)]
            blocks += [jnp.zeros((cols // pieces, lanes), jnp.float32)] * (pieces - kinds)
            edges.append(jnp.concatenate(exchange_pieces(blocks, rows), axis=0))
        linked = [wide_product(edge, links_ref[last], 3) for edge in edges]
        gone = [(inner_ref[q] + link) * inverse_ref[last] for q, link in zip(mine, linked)]
        nodes = [wide_product(value, basis_ref[last], 3) for value in gone]
        whole = [
            jnp.concatenate(both, axis=1).T[: lanes + kinds * rows] for both in zip(nodes, edges)
        ]
        potential = [one_product(long_data(value, 3, 1), hart_ref[...], DIRECT) for value in whole]
        for q, values in zip(mine, potential):
            fetches[q].wait()
            step_part(q, pair, values, inside, mult_ref, mult_out, aux_out)
            cut = pl.ds(q * pair, pair)
            for n, (one, other) in enumerate(((mult_out, mult_hbm), (aux_out, aux_hbm))):
                copy = pltpu.make_async_copy(one.at[:, :, cut], other.at[:, :, cut], sems.at[n, q])
                copy.start()
                outs.append(copy)
    for copy in outs:
        copy.wait()


def step_part(q, pair, values, inside, mult_ref, mult_out, aux_out):
    _, here, _, rows, cols = mult_ref.shape
    lanes = here * pair * rows
    full = (pair, rows, cols)
    row_index = lax.broadcasted_iota(jnp.int32, full, 1)
    at = slice(q * pair, (q + 1) * pair)

    def level(start):
        return values[start : start + pair * rows].reshape(full)

    def rims(kind, t):
        starts = [lanes + slots(here, rows, b, kind, t) for b in range(pair)]
        rim = [jnp.broadcast_to(values[start : start + 1], (rows, cols)) for start in starts]
        return jnp.concatenate(rim, axis=0).reshape(full)

    phi = [level(lanes)]
    for t in range(1, here):
        phi.append(jnp.where(row_index == 0, rims("row", t), level(t * pair * rows)))
    phi.append(level(lanes + pair * rows))
    for t0 in range(0, here, 1):
        times = range(t0, t0 + 1)
        mine = jnp.concatenate([phi[t] for t in times], axis=0)
        rate = jnp.concatenate([phi[t + 1] for t in times], axis=0) - mine
        if times[-1] == here - 1:
            kept = [rate[: (1 - 1) * pair]] if 1 > 1 else []
            rate = jnp.concatenate(kept + [rate[(1 - 1) * pair :] * inside], axis=0)
        rim = jnp.concatenate([rims("next", t) for t in times], axis=0)
        index = lax.broadcasted_iota(jnp.int32, mine.shape, 1)
        below = jnp.where(index == rows - 1, rim, pltpu.roll(mine, rows - 1, 1))
        gradient = (rate, below - mine, pltpu.roll(mine, cols - 1, 2) - mine)
        target = [
            gradient[c] + jnp.concatenate([mult_ref[c, t, at] for t in times], axis=0)
            for c in range(3)
        ]
        time_part, one, two = target
        kinetic = 0.5 * (one * one + two * two)
        center = 1.0 + time_part
        scaling = jnp.maximum(center, 1.0) + jnp.exp(jnp.log(kinetic) * (1.0 / 3.0))
        for _ in range(NEWTON):
            linear = scaling * (scaling - center)
            residue = scaling * linear - kinetic
            derivative = scaling * scaling + (linear + linear)
            change = residue * pl.reciprocal(derivative, approx=True)
            scaling = jnp.maximum(scaling - change, 1.0)
        scaling = jnp.where(time_part + kinetic <= 0.0, 1.0, scaling)
        shrink = pl.reciprocal(scaling, approx=True)
        shrink = shrink * (2.0 - scaling * shrink)
        shrink = shrink * (2.0 - scaling * shrink)
        moved = scaling - 1.0
        fresh = (time_part - moved, one * shrink, two * shrink)
        for c, past in enumerate((moved, one - fresh[1], two - fresh[2])):
            for n, t in enumerate(times):
                part = slice(n * pair, (n + 1) * pair)
                aux_out[c, t, at] = fresh[c][part]
                mult_out[c, t, at] = past[part]


def params(size=48):
    return pltpu.CompilerParams(vmem_limit_bytes=size * 1024 * 1024)


def local(multiplier, auxiliary, density_start, density_end):
    _, here, batch, rows, cols = multiplier.shape
    time_blocks = lax.axis_size("py")
    row_blocks = lax.axis_size("grp") * lax.axis_size("px")
    levels = here * time_blocks
    row_count = rows * row_blocks
    pair = batch // time_blocks
    lanes = here * pair * rows
    pieces = lanes // rows
    kinds = 2 * pair + 1
    few = cols // (pieces * row_blocks)
    both = [interior_tables(here, rows, cols, last) for last in (False, True)]
    hart_there = long_table(hartley_table(cols), 2, 1)
    hart_back = long_table(hartley_table(cols), 3, 0)
    rows_there = long_table(hartley_table(row_count), 2, 0)
    rows_back = long_table(hartley_table(row_count), 3, 0)
    basis2 = np.stack([wide_table(one[0], 2) for one in both])
    basis3 = np.stack([wide_table(one[0].T, 3) for one in both])
    inverse = np.stack([one[1] for one in both]).astype(np.float32)
    to_edges = np.stack([wide_table(one[2], 2) for one in both])
    from_edges = np.stack([wide_table(one[3], 3) for one in both])
    ones = constant_source(here, rows, time_blocks, row_blocks, both).astype(np.float32)
    factors = elimination_table(levels, row_count, cols, row_blocks, pieces, pair)

    away = pl.BlockSpec(memory_space=pltpu.HBM)
    vmem = pl.BlockSpec(memory_space=pltpu.VMEM)
    chunked = jax.ShapeDtypeStruct((row_blocks, time_blocks, kinds, few, lanes), jnp.float32)
    inner_shape = (time_blocks, cols, lanes)
    edges, inner, factor = pl.pallas_call(
        functools.partial(source_kernel, levels, pair),
        in_specs=[away] * 9,
        out_specs=[away] * 3,
        out_shape=[
            chunked,
            jax.ShapeDtypeStruct(inner_shape, jnp.float32),
            jax.ShapeDtypeStruct(factors.shape[1:], jnp.float32),
        ],
        scratch_shapes=[
            pltpu.VMEM(multiplier.shape, jnp.float32),
            pltpu.VMEM(auxiliary.shape, jnp.float32),
            pltpu.VMEM((2,) + density_start.shape, jnp.float32),
            pltpu.VMEM(hart_there.shape, jnp.bfloat16),
            pltpu.VMEM(basis2.shape[1:], jnp.bfloat16),
            pltpu.VMEM(inverse.shape[1:], jnp.float32),
            pltpu.VMEM(to_edges.shape[1:], jnp.bfloat16),
            pltpu.VMEM(chunked.shape, jnp.float32),
            pltpu.VMEM(inner_shape, jnp.float32),
            pltpu.SemaphoreType.DMA((2, FETCHES)),
            pltpu.SemaphoreType.DMA((7,)),
            pltpu.SemaphoreType.DMA((2, time_blocks)),
        ],
        compiler_params=params(56),
        name="source",
    )(multiplier, auxiliary, density_start, density_end, hart_there, basis2, inverse, to_edges, factors)

    def spread(value):
        flat = value.reshape((row_blocks * time_blocks,) + value.shape[2:])
        return lax.all_to_all(flat, EVERY, 0, 0, tiled=True).reshape(value.shape)

    solved = pl.pallas_call(
        functools.partial(solve_kernel, lax.axis_size("grp")),
        in_specs=[vmem] * 5,
        out_specs=vmem,
        out_shape=chunked,
        scratch_shapes=[
            pltpu.VMEM((levels, pair * pieces * few, row_count), jnp.float32),
            pltpu.VMEM((pieces // 2, 2 * pair * few, row_count), jnp.float32),
            pltpu.VMEM((time_blocks // (2 * pair), pieces, 2, 2 * pair * few, row_count), jnp.float32),
        ],
        compiler_params=params(),
        name="solve",
    )(spread(edges), rows_there, rows_back, ones, factor)

    result = jax.ShapeDtypeStruct(multiplier.shape, jnp.float32)
    mult_next, aux_next = pl.pallas_call(
        functools.partial(step_kernel, levels, pair),
        in_specs=[away] + [vmem] * 6,
        out_specs=[away] * 2,
        scratch_shapes=[
            pltpu.VMEM(multiplier.shape, jnp.float32),
            pltpu.VMEM(multiplier.shape, jnp.float32),
            pltpu.VMEM(multiplier.shape, jnp.float32),
            pltpu.SemaphoreType.DMA((3, time_blocks)),
        ],
        out_shape=[result, result],
        compiler_params=params(),
        name="step",
    )(multiplier, spread(solved), inner, hart_back, from_edges, inverse, basis3)
    return mult_next, aux_next


def solution(mesh):
    field = P(None, "py", None, ROWS, None)
    density = P(None, ROWS, None)
    return jax.shard_map(
        local,
        mesh=mesh,
        in_specs=(field, field, density, density),
        out_specs=(field, field),
        check_vma=False,
    )
```

```python
import functools

import jax
import jax.numpy as jnp
import numpy as np
from jax import lax
from jax.experimental import pallas as pl
from jax.experimental.pallas import tpu as pltpu
from jax.sharding import PartitionSpec as P

NEWTON = 4
ROWS = ("grp", "px")
EVERY = ("px", "grp", "py")
PARTS = 2
FETCHES = 4
STEP_PARTS = 2
VMEM_BYTES = 48 * 1024 * 1024
DIRECT = ((1,), (0,))
CROSS = ((1,), (1,))


def table_parts(table, count):
    rest = np.asarray(table, np.float32)
    parts = []
    for _ in range(count):
        parts.append(rest.astype(jnp.bfloat16))
        rest = rest - parts[-1].astype(np.float32)
    return np.stack(parts)


def parts_of(value, count):
    parts = [value.astype(jnp.bfloat16)]
    for _ in range(count - 1):
        value = value - parts[-1].astype(jnp.float32)
        parts.append(value.astype(jnp.bfloat16))
    return parts


def orders(count):
    return [(i, order - i) for order in range(count - 1, -1, -1) for i in range(order + 1)]


def long_table(table, count, axis):
    parts = table_parts(table, count)
    return np.concatenate([parts[j] for _, j in orders(count)], axis=axis)


def long_data(value, count, axis):
    parts = parts_of(value, count)
    return jnp.concatenate([parts[i] for i, _ in orders(count)], axis=axis)


def wide_table(table, count):
    parts = table_parts(table, count)
    none = np.zeros_like(parts[0])
    if count == 2:
        grid = [(0, 1), (0, None)]
    else:
        grid = [(0, 1), (0, 1), (2, None), (0, None)]
    return np.block([[none if k is None else parts[k] for k in row] for row in grid])


def wide_product(value, table, count):
    parts = parts_of(value, count)
    data = parts if count == 2 else [parts[0], parts[1], parts[0], parts[2]]
    both = one_product(jnp.concatenate(data, axis=1), table, DIRECT)
    half = both.shape[1] // 2
    return both[:, :half] + both[:, half:]


def one_product(left, right, dims):
    return lax.dot_general(left, right, (dims, ((), ())), preferred_element_type=jnp.float32)


def squared_sines(length, period):
    return 4.0 * np.sin(np.pi * np.arange(length) / period) ** 2


def hartley_table(length):
    index = np.arange(length)
    angles = (index[:, None] * index[None, :] % length) * (2.0 * np.pi / length)
    return (np.cos(angles) + np.sin(angles)) / np.sqrt(length)


def elimination_table(levels, row_count, col_count, blocks, pieces, pair):
    eigen = squared_sines(col_count, col_count)[:, None] + squared_sines(row_count, row_count)
    factors = [1.0 / (1.0 + eigen)]
    for _ in range(levels // 2 - 1):
        factors.append(1.0 / (2.0 + eigen - factors[-1]))
    gap = 1.0 - factors[-1] ** 2
    middle = np.where(eigen > 0.0, 1.0 / np.where(eigen > 0.0, gap, 1.0), 0.0)
    table = np.stack(factors + [middle]).astype(np.float32)
    table = table.reshape(levels // 2 + 1, pieces, blocks, 1, -1, row_count).transpose(2, 0, 1, 3, 4, 5)
    table = np.broadcast_to(table, table.shape[:3] + (pair,) + table.shape[4:])
    return np.ascontiguousarray(table).reshape(blocks, levels // 2 + 1, -1, row_count)


def slots(here, rows, b, kind, index):
    if kind == "level":
        return b * rows + index
    if kind == "later":
        return (2 + b) * rows + index
    base = 4 * rows + b * (rows // 2)
    return base + (index - 1 if kind == "row" else here - 1 + index)


def interior_tables(here, rows, cols, last):
    pair = 2
    lanes = here * pair * rows
    inner = here - 1
    chain = 2.0 * np.eye(inner) - np.eye(inner, k=1) - np.eye(inner, k=-1)
    if last:
        chain[-1, -1] = 1.0
    time_values, time_basis = np.linalg.eigh(chain)
    row_index = np.arange(1, rows)
    row_basis = np.sqrt(2.0 / rows) * np.sin(np.pi * np.outer(row_index, row_index) / rows)
    row_values = squared_sines(rows, 2 * rows)
    col_values = squared_sines(cols, cols)
    basis = np.zeros((here, pair, rows, here, pair, rows))
    inverse = np.zeros((cols, here, pair, rows))
    linked = np.zeros((here, pair, rows, lanes))
    for b in range(pair):
        for k in range(1, here):
            for t in range(1, here):
                basis[t, b, 1:, k, b, 1:] = time_basis[t - 1, k - 1] * row_basis
            inverse[:, k, b, 1:] = 1.0 / (
                col_values[:, None] + time_values[k - 1] + row_values[None, 1:]
            )
        for x in range(1, rows):
            linked[1, b, x, slots(here, rows, b, "level", x)] = 1.0
            if not last:
                linked[here - 1, b, x, slots(here, rows, b, "later", x)] = 1.0
        for t in range(1, here):
            linked[t, b, 1, slots(here, rows, b, "row", t)] = 1.0
            linked[t, b, rows - 1, slots(here, rows, b, "next", t)] = 1.0
    basis = basis.reshape(lanes, lanes)
    linked = linked.reshape(lanes, lanes)
    inverse = inverse.reshape(cols, lanes)
    to_edges = basis.T @ linked
    from_edges = to_edges.T.copy()
    for b in range(pair):
        ones = np.zeros((here, pair, rows))
        ones[1:, b, 1:] = 1.0
        from_edges[slots(here, rows, b, "next", here)] = -(ones.reshape(-1) @ basis)
    return basis, inverse, to_edges, from_edges


def constant_source(here, rows, time_blocks, row_blocks, tables):
    levels, row_count = here * time_blocks, rows * row_blocks
    field = np.zeros((levels + 1, row_count))
    ones = np.zeros((here, 2, rows))
    ones[1:, 0, 1:] = 1.0
    for i in range(time_blocks):
        basis, inverse, to_edges, _ = tables[1 if i == time_blocks - 1 else 0]
        edge = ((ones.reshape(-1) @ basis) * inverse[0]) @ to_edges
        for j in range(row_blocks):
            t0, x0 = i * here, j * rows
            for x in range(rows):
                field[t0, x0 + x] += 1.0 + edge[slots(here, rows, 0, "level", x)]
                field[t0 + here, x0 + x] += edge[slots(here, rows, 0, "later", x)]
            for t in range(here):
                after = (x0 + rows) % row_count
                field[t0 + t, after] += edge[slots(here, rows, 0, "next", t)]
                if t > 0:
                    field[t0 + t, x0] += 1.0 + edge[slots(here, rows, 0, "row", t)]
    return field[:levels] @ hartley_table(row_count)


def exchange_pieces(blocks, width):
    count = len(blocks)
    lanes = count * width
    group = lax.broadcasted_iota(jnp.int32, blocks[0].shape, 1) // width
    step = 1
    while step < count:
        upper = (group // step) % 2 == 1
        fresh = list(blocks)
        for j in range(count):
            if (j // step) % 2 == 0:
                low, high = blocks[j], blocks[j + step]
                fresh[j] = jnp.where(upper, pltpu.roll(high, step * width, 1), low)
                fresh[j + step] = jnp.where(upper, high, pltpu.roll(low, lanes - step * width, 1))
        blocks = fresh
        step *= 2
    return blocks


def source_kernel(
    levels,
    pair,
    mult_hbm,
    aux_hbm,
    start_hbm,
    end_hbm,
    hart_hbm,
    basis_hbm,
    inverse_hbm,
    edges_hbm,
    factors_hbm,
    out_hbm,
    inner_hbm,
    factor_hbm,
    mult_ref,
    aux_ref,
    density_ref,
    hart_ref,
    basis_ref,
    inverse_ref,
    edges_ref,
    factor_ref,
    out_ref,
    inner_ref,
    field_sems,
    table_sems,
    out_sems,
):
    _, here, batch, rows, cols = mult_ref.shape
    lanes = here * pair * rows
    pieces = lanes // rows
    each = cols // pieces
    total_pairs = batch // pair
    first = lax.axis_index("py") * here
    at_start = first == 0
    at_end = first + here == levels
    last = at_end.astype(jnp.int32)
    fields = []
    for part in range(FETCHES):
        cut = pl.ds(part * batch // FETCHES, batch // FETCHES)
        fields.append(
            [
                pltpu.make_async_copy(
                    one.at[:, :, cut], other.at[:, :, cut], field_sems.at[n, part]
                )
                for n, (one, other) in enumerate(((mult_hbm, mult_ref), (aux_hbm, aux_ref)))
            ]
        )
    tables = [
        pltpu.make_async_copy(hart_hbm, hart_ref, table_sems.at[0]),
        pltpu.make_async_copy(basis_hbm.at[last], basis_ref, table_sems.at[1]),
        pltpu.make_async_copy(inverse_hbm.at[last], inverse_ref, table_sems.at[2]),
        pltpu.make_async_copy(edges_hbm.at[last], edges_ref, table_sems.at[3]),
    ]
    modes_here = lax.axis_index("px") * lax.axis_size("grp") + lax.axis_index("grp")
    factor_copy = pltpu.make_async_copy(factors_hbm.at[modes_here], factor_ref, table_sems.at[6])
    factor_out = pltpu.make_async_copy(factor_ref, factor_hbm, table_sems.at[7])
    start_copy = pltpu.make_async_copy(start_hbm, density_ref.at[0], table_sems.at[4])
    end_copy = pltpu.make_async_copy(end_hbm, density_ref.at[1], table_sems.at[5])
    for copy in fields[0] + [start_copy, end_copy] + fields[1] + tables + sum(fields[2:], []) + [factor_copy]:
        copy.start()

    row_index = lax.broadcasted_iota(jnp.int32, (rows, cols), 0)
    first_row = row_index == 0
    outs = [factor_out]
    for part in range(PARTS):
        mine = range(part * total_pairs // PARTS, (part + 1) * total_pairs // PARTS)
        field = []
        for q in mine:
            if q * FETCHES % total_pairs == 0:
                for copy in fields[q * FETCHES // total_pairs]:
                    copy.wait()
            if q == 0:
                start_copy.wait()
                end_copy.wait()
            blocks = []
            earlier = [0.0] * pair
            rims = jnp.zeros((rows, cols), jnp.float32)
            for t in range(here):
                for b in range(pair):
                    at = q * pair + b
                    time = aux_ref[0, t, at] - mult_ref[0, t, at]
                    if t == here - 1:
                        time = jnp.where(at_end, 0.0, time)
                    along = aux_ref[1, t, at] - mult_ref[1, t, at]
                    second = aux_ref[2, t, at] - mult_ref[2, t, at]
                    beside = jnp.where(first_row, 0.0, pltpu.roll(along, 1, 0))
                    total = (earlier[b] - time) + (beside - along)
                    total = total + (pltpu.roll(second, 1, 1) - second)
                    if t == 0:
                        total = total - jnp.where(at_start, density_ref[0, at], 0.0)
                    if t == here - 1:
                        total = total + jnp.where(at_end, density_ref[1, at], 0.0)
                    earlier[b] = time
                    blocks.append(total)
                    base = b * (rows // 2)
                    if t > 0:
                        rims = jnp.where(row_index == base + t - 1, total[:1], rims)
                    rims = jnp.where(row_index == base + here - 1 + t, along[rows - 1 :], rims)
            spare = jnp.zeros((lanes - (2 * pair + 1) * rows, cols), jnp.float32)
            nodes = jnp.concatenate(blocks + blocks[:pair] + earlier + [rims, spare], axis=0)
            field.append(long_data(nodes, 2, 1))
        if part == 0:
            for copy in tables:
                copy.wait()
        else:
            factor_copy.wait()
            factor_out.start()
        modes = [one_product(hart_ref[...], nodes, CROSS) for nodes in field]
        inner = [wide_product(mode[:, :lanes], basis_ref[...], 2) for mode in modes]
        for n, q in enumerate(mine):
            inner_ref[q] = inner[n]
            outs.append(pltpu.make_async_copy(inner_ref.at[q], inner_hbm.at[q], out_sems.at[1, q]))
            outs[-1].start()
        gone = [wide_product(value * inverse_ref[...], edges_ref[...], 2) for value in inner]
        for n, q in enumerate(mine):
            edges = modes[n][:, lanes:] + gone[n]
            blocks = exchange_pieces(
                [edges[j * each : (j + 1) * each] for j in range(pieces)], rows
            )
            for k in range(out_ref.shape[2]):
                out_ref[:, q, k] = blocks[k].reshape(out_ref.shape[0], out_ref.shape[3], lanes)
            outs.append(
                pltpu.make_async_copy(out_ref.at[:, q], out_hbm.at[:, q], out_sems.at[0, q])
            )
            outs[-1].start()
    for copy in outs:
        copy.wait()


def solve_kernel(
    groups, in_ref, hart_ref, back_ref, ones_ref, factor_ref, out_ref, field_ref, mean_ref, rim_ref
):
    row_blocks, time_blocks, kinds, few, lanes = in_ref.shape
    levels, high, cols = field_ref.shape
    here = levels // time_blocks
    rows = cols // row_blocks
    pieces = lanes // rows
    tall = (kinds - 1) * few
    count = high // tall
    half = levels // 2
    mine = lax.axis_index("px") * lax.axis_size("grp") + lax.axis_index("grp")
    stack = tall // few
    lane = lax.broadcasted_iota(jnp.int32, (tall, cols), 1) % rows
    row = lax.broadcasted_iota(jnp.int32, (tall, cols), 0)
    low = row < tall // 2
    even = (row // few) % 2 == 0

    def shift(value, steps):
        return pltpu.roll(value, steps % cols, 1)

    def swap(value):
        return pltpu.roll(value, tall // 2, 0)

    def place(g, j):
        block = g * pieces + j
        return block % (row_blocks // groups) * groups + block // (row_blocks // groups)

    def exchange(get):
        halves = [
            exchange_pieces([get(place(g, j)) for j in range(pieces)], rows)
            for g in range(row_blocks // pieces)
        ]
        return [jnp.concatenate([one[k] for one in halves], axis=1) for k in range(pieces)]

    for h in range(time_blocks // stack):
        times = slice(h * stack, (h + 1) * stack)
        for j, rim in enumerate(exchange(lambda x: in_ref[x, times, kinds - 1].reshape(tall, lanes))):
            rim_ref[h, j, 0] = rim
            rim_ref[h, j, 1] = shift(rim, -(rows // 2))

    def forward(i, carry):
        main = exchange(lambda x: in_ref[x, i, : kinds - 1].reshape(tall, lanes))
        here_rows = slice(i % stack * few, (i % stack + 1) * few)
        field = [[] for _ in range(here)]
        later = []
        for q in range(count):
            one, two = main[2 * q], main[2 * q + 1]
            level = jnp.where(low, one, swap(two)) + carry[q]
            later.append(jnp.where(low, swap(one), two))
            rim = jnp.concatenate(
                [rim_ref[i // stack, 2 * q + j, b, here_rows] for j in range(2) for b in range(2)],
                axis=0,
            )
            rim = jnp.where(lane < here - 1, rim, 0.0) + shift(rim, rows - here)
            for t in range(here):
                value = jnp.where(lane == 0, rim if t == 1 else shift(rim, 1 - t), 0.0)
                field[t].append(value + level if t == 0 else value)
        field = jnp.concatenate(sum(field, []), axis=0)
        modes = one_product(long_data(field, 2, 1), hart_ref[...], DIRECT)
        field_ref[pl.ds(i * here, here)] = modes.reshape(here, high, cols)
        return tuple(later)

    blank = jnp.zeros((tall, cols), jnp.float32)
    carry = (blank,) * count
    for i in range(time_blocks):
        carry = forward(i, carry)

    mean_ref[...] = jnp.zeros(mean_ref.shape, jnp.float32)

    @pl.when(mine == 0)
    def _():
        shape = (tall, 128)
        spot = lax.broadcasted_iota(jnp.int32, shape, 0)
        zero = (spot % few == 0) & (spot < tall // 2)
        zero = zero & (lax.broadcasted_iota(jnp.int32, shape, 1) == 0)
        scale = float(np.sqrt(cols)) / (levels * cols)
        sums = field_ref[0, :tall, :128]
        for t in range(1, levels):
            sums = sums + field_ref[t, :tall, :128]
        mean = jnp.sum(jnp.where(zero, sums * scale, 0.0), axis=1, keepdims=True)
        mean_ref[0] = jnp.broadcast_to(mean, (tall, cols))
        for t in range(levels):
            field_ref[t, :tall] = field_ref[t, :tall] - mean * ones_ref[t : t + 1]

    left = jnp.zeros(field_ref.shape[1:], jnp.float32)
    right = left
    for t in range(half):
        factor = factor_ref[t]
        left = (field_ref[t] + left) * factor
        right = (field_ref[levels - 1 - t] + right) * factor
        if t < half - 1:
            field_ref[t] = left
            field_ref[levels - 1 - t] = right
    first = (left + factor * right) * factor_ref[half]
    right = right + factor * first
    left = first
    field_ref[half - 1] = left
    field_ref[half] = right
    for t in range(half - 2, -1, -1):
        factor = factor_ref[t]
        left = field_ref[t] + factor * left
        right = field_ref[levels - 1 - t] + factor * right
        field_ref[t] = left
        field_ref[levels - 1 - t] = right

    def backward(i, carry):
        here_rows = slice(i % stack * few, (i % stack + 1) * few)
        field = field_ref[pl.ds(i * here, here)].reshape(here * high, cols)
        values = one_product(long_data(field, 3, 1), back_ref[...], DIRECT)
        main, first = [], []
        for q in range(count):
            part = [values[t * high + q * tall : t * high + (q + 1) * tall] for t in range(here)]
            rim = jnp.where(lane == rows - 1, shift(part[0], -1), part[1])
            for t in range(2, here):
                rim = jnp.where(lane == t - 1, shift(part[t], t - 1), rim)
            after = jnp.where(lane < 2 * here - 1, shift(rim, here - rows), mean_ref[q])
            rim = jnp.where(lane < here - 1, rim, after)
            rim = jnp.where(lane < 2 * here, rim, 0.0)
            rim = jnp.where(even, rim, shift(rim, rows // 2))
            rim = rim + pltpu.roll(rim, tall - few, 0)
            rim_ref[i // stack, 2 * q, 0, here_rows] = rim[:few]
            rim_ref[i // stack, 2 * q + 1, 0, here_rows] = rim[tall // 2 : tall // 2 + few]
            main.append(jnp.where(low, part[0], swap(carry[q])))
            main.append(jnp.where(low, swap(part[0]), carry[q]))
            first.append(part[0])
        for g in range(row_blocks // pieces):
            cut = slice(g * lanes, (g + 1) * lanes)
            for j, value in enumerate(exchange_pieces([a[:, cut] for a in main], rows)):
                out_ref[place(g, j), i, : kinds - 1] = value.reshape(kinds - 1, few, lanes)
        return tuple(first)

    carry = (blank,) * count
    for i in range(time_blocks - 1, -1, -1):
        carry = backward(i, carry)
    for h in range(time_blocks // stack):
        times = slice(h * stack, (h + 1) * stack)
        for g in range(row_blocks // pieces):
            cut = slice(g * lanes, (g + 1) * lanes)
            rims = exchange_pieces([rim_ref[h, j, 0, :, cut] for j in range(pieces)], rows)
            for j, value in enumerate(rims):
                out_ref[place(g, j), times, kinds - 1] = value.reshape(stack, few, lanes)


def step_kernel(
    levels,
    pair,
    mult_in,
    edge_ref,
    inner_ref,
    hart_ref,
    links_ref,
    inverse_ref,
    basis_ref,
    mult_hbm,
    aux_hbm,
    mult_ref,
    mult_out,
    aux_out,
    sems,
):
    _, here, batch, rows, cols = mult_ref.shape
    lanes = here * pair * rows
    pieces = lanes // rows
    kinds = edge_ref.shape[2]
    total_pairs = batch // pair
    first = lax.axis_index("py") * here
    last = (first + here == levels).astype(jnp.int32)
    inside = 1.0 - last.astype(jnp.float32)
    outs = []
    fetches = []
    for q in range(total_pairs):
        cut = pl.ds(q * pair, pair)
        fetches.append(
            pltpu.make_async_copy(mult_in.at[:, :, cut], mult_ref.at[:, :, cut], sems.at[2, q])
        )
        fetches[q].start()
    for part in range(STEP_PARTS):
        mine = range(part * total_pairs // STEP_PARTS, (part + 1) * total_pairs // STEP_PARTS)
        edges = []
        for q in mine:
            blocks = [edge_ref[:, q, k].reshape(cols // pieces, lanes) for k in range(kinds)]
            blocks += [jnp.zeros((cols // pieces, lanes), jnp.float32)] * (pieces - kinds)
            edges.append(jnp.concatenate(exchange_pieces(blocks, rows), axis=0))
        linked = [wide_product(edge, links_ref[last], 3) for edge in edges]
        gone = [(inner_ref[q] + link) * inverse_ref[last] for q, link in zip(mine, linked)]
        nodes = [wide_product(value, basis_ref[last], 3) for value in gone]
        whole = [
            jnp.concatenate(both, axis=1).T[: lanes + kinds * rows] for both in zip(nodes, edges)
        ]
        potential = [one_product(long_data(value, 3, 1), hart_ref[...], DIRECT) for value in whole]
        for q, values in zip(mine, potential):
            fetches[q].wait()
            step_part(q, pair, values, inside, mult_ref, mult_out, aux_out)
            cut = pl.ds(q * pair, pair)
            for n, (one, other) in enumerate(((mult_out, mult_hbm), (aux_out, aux_hbm))):
                copy = pltpu.make_async_copy(one.at[:, :, cut], other.at[:, :, cut], sems.at[n, q])
                copy.start()
                outs.append(copy)
    for copy in outs:
        copy.wait()


def step_part(q, pair, values, inside, mult_ref, mult_out, aux_out):
    _, here, _, rows, cols = mult_ref.shape
    lanes = here * pair * rows
    full = (pair, rows, cols)
    row_index = lax.broadcasted_iota(jnp.int32, full, 1)
    at = slice(q * pair, (q + 1) * pair)

    def level(start):
        return values[start : start + pair * rows].reshape(full)

    def rims(kind, t):
        starts = [lanes + slots(here, rows, b, kind, t) for b in range(pair)]
        rim = [jnp.broadcast_to(values[start : start + 1], (rows, cols)) for start in starts]
        return jnp.concatenate(rim, axis=0).reshape(full)

    phi = [level(lanes)]
    for t in range(1, here):
        phi.append(jnp.where(row_index == 0, rims("row", t), level(t * pair * rows)))
    phi.append(level(lanes + pair * rows))
    for t0 in range(0, here, 1):
        times = range(t0, t0 + 1)
        mine = jnp.concatenate([phi[t] for t in times], axis=0)
        rate = jnp.concatenate([phi[t + 1] for t in times], axis=0) - mine
        if times[-1] == here - 1:
            kept = [rate[: (1 - 1) * pair]] if 1 > 1 else []
            rate = jnp.concatenate(kept + [rate[(1 - 1) * pair :] * inside], axis=0)
        rim = jnp.concatenate([rims("next", t) for t in times], axis=0)
        index = lax.broadcasted_iota(jnp.int32, mine.shape, 1)
        below = jnp.where(index == rows - 1, rim, pltpu.roll(mine, rows - 1, 1))
        gradient = (rate, below - mine, pltpu.roll(mine, cols - 1, 2) - mine)
        target = [
            gradient[c] + jnp.concatenate([mult_ref[c, t, at] for t in times], axis=0)
            for c in range(3)
        ]
        time_part, one, two = target
        kinetic = 0.5 * (one * one + two * two)
        center = 1.0 + time_part
        scaling = jnp.maximum(center, 1.0) + jnp.exp(jnp.log(kinetic) * (1.0 / 3.0))
        for _ in range(NEWTON):
            linear = scaling * (scaling - center)
            residue = scaling * linear - kinetic
            derivative = scaling * scaling + (linear + linear)
            change = residue * pl.reciprocal(derivative, approx=True)
            scaling = jnp.maximum(scaling - change, 1.0)
        scaling = jnp.where(time_part + kinetic <= 0.0, 1.0, scaling)
        shrink = pl.reciprocal(scaling, approx=True)
        shrink = shrink * (2.0 - scaling * shrink)
        shrink = shrink * (2.0 - scaling * shrink)
        moved = scaling - 1.0
        fresh = (time_part - moved, one * shrink, two * shrink)
        for c, past in enumerate((moved, one - fresh[1], two - fresh[2])):
            for n, t in enumerate(times):
                part = slice(n * pair, (n + 1) * pair)
                aux_out[c, t, at] = fresh[c][part]
                mult_out[c, t, at] = past[part]


def params(size=48):
    return pltpu.CompilerParams(vmem_limit_bytes=size * 1024 * 1024)


def local(multiplier, auxiliary, density_start, density_end):
    _, here, batch, rows, cols = multiplier.shape
    time_blocks = lax.axis_size("py")
    row_blocks = lax.axis_size("grp") * lax.axis_size("px")
    levels = here * time_blocks
    row_count = rows * row_blocks
    pair = batch // time_blocks
    lanes = here * pair * rows
    pieces = lanes // rows
    kinds = 2 * pair + 1
    few = cols // (pieces * row_blocks)
    both = [interior_tables(here, rows, cols, last) for last in (False, True)]
    hart_there = long_table(hartley_table(cols), 2, 1)
    hart_back = long_table(hartley_table(cols), 3, 0)
    rows_there = long_table(hartley_table(row_count), 2, 0)
    rows_back = long_table(hartley_table(row_count), 3, 0)
    basis2 = np.stack([wide_table(one[0], 2) for one in both])
    basis3 = np.stack([wide_table(one[0].T, 3) for one in both])
    inverse = np.stack([one[1] for one in both]).astype(np.float32)
    to_edges = np.stack([wide_table(one[2], 2) for one in both])
    from_edges = np.stack([wide_table(one[3], 3) for one in both])
    ones = constant_source(here, rows, time_blocks, row_blocks, both).astype(np.float32)
    factors = elimination_table(levels, row_count, cols, row_blocks, pieces, pair)

    away = pl.BlockSpec(memory_space=pltpu.HBM)
    vmem = pl.BlockSpec(memory_space=pltpu.VMEM)
    chunked = jax.ShapeDtypeStruct((row_blocks, time_blocks, kinds, few, lanes), jnp.float32)
    inner_shape = (time_blocks, cols, lanes)
    edges, inner, factor = pl.pallas_call(
        functools.partial(source_kernel, levels, pair),
        in_specs=[away] * 9,
        out_specs=[away] * 3,
        out_shape=[
            chunked,
            jax.ShapeDtypeStruct(inner_shape, jnp.float32),
            jax.ShapeDtypeStruct(factors.shape[1:], jnp.float32),
        ],
        scratch_shapes=[
            pltpu.VMEM(multiplier.shape, jnp.float32),
            pltpu.VMEM(auxiliary.shape, jnp.float32),
            pltpu.VMEM((2,) + density_start.shape, jnp.float32),
            pltpu.VMEM(hart_there.shape, jnp.bfloat16),
            pltpu.VMEM(basis2.shape[1:], jnp.bfloat16),
            pltpu.VMEM(inverse.shape[1:], jnp.float32),
            pltpu.VMEM(to_edges.shape[1:], jnp.bfloat16),
            pltpu.VMEM(factors.shape[1:], jnp.float32),
            pltpu.VMEM(chunked.shape, jnp.float32),
            pltpu.VMEM(inner_shape, jnp.float32),
            pltpu.SemaphoreType.DMA((2, FETCHES)),
            pltpu.SemaphoreType.DMA((8,)),
            pltpu.SemaphoreType.DMA((2, time_blocks)),
        ],
        compiler_params=params(56),
        name="source",
    )(multiplier, auxiliary, density_start, density_end, hart_there, basis2, inverse, to_edges, factors)

    def spread(value):
        flat = value.reshape((row_blocks * time_blocks,) + value.shape[2:])
        return lax.all_to_all(flat, EVERY, 0, 0, tiled=True).reshape(value.shape)

    solved = pl.pallas_call(
        functools.partial(solve_kernel, lax.axis_size("grp")),
        in_specs=[vmem] * 5,
        out_specs=vmem,
        out_shape=chunked,
        scratch_shapes=[
            pltpu.VMEM((levels, pair * pieces * few, row_count), jnp.float32),
            pltpu.VMEM((pieces // 2, 2 * pair * few, row_count), jnp.float32),
            pltpu.VMEM((time_blocks // (2 * pair), pieces, 2, 2 * pair * few, row_count), jnp.float32),
        ],
        compiler_params=params(),
        name="solve",
    )(spread(edges), rows_there, rows_back, ones, factor)

    result = jax.ShapeDtypeStruct(multiplier.shape, jnp.float32)
    mult_next, aux_next = pl.pallas_call(
        functools.partial(step_kernel, levels, pair),
        in_specs=[away] + [vmem] * 6,
        out_specs=[away] * 2,
        scratch_shapes=[
            pltpu.VMEM(multiplier.shape, jnp.float32),
            pltpu.VMEM(multiplier.shape, jnp.float32),
            pltpu.VMEM(multiplier.shape, jnp.float32),
            pltpu.SemaphoreType.DMA((3, time_blocks)),
        ],
        out_shape=[result, result],
        compiler_params=params(),
        name="step",
    )(multiplier, spread(solved), inner, hart_back, from_edges, inverse, basis3)
    return mult_next, aux_next


def solution(mesh):
    field = P(None, "py", None, ROWS, None)
    density = P(None, ROWS, None)
    return jax.shard_map(
        local,
        mesh=mesh,
        in_specs=(field, field, density, density),
        out_specs=(field, field),
        check_vma=False,
    )
```
